32 devices in a mesh: grp: 2 (over x), rb: 16 (over z, y, core).
Axes of the slice: x: 2, y: 2, z: 4, core: 2. Of those that a mesh axis runs over, the one named last changes fastest.
Arguments:
- tiles: bfloat16 [2816, 256, 256], P(('grp', 'rb')), parts along dimension 0, may hold values from -0.25 to 0.25
- tile_rows: int32 [2816], P(('grp', 'rb')), parts along dimension 0, may hold values from 0 to 7, as said below
- tile_cols: int32 [2816], P(('grp', 'rb')), parts along dimension 0, may hold values from 0 to 191, as said below
- tile_counts: int32 [32], P(('grp', 'rb')), parts along dimension 0, may hold values from 29 to 88, as said below
- dual_step: float32 [65536], P(('grp', 'rb')), parts along dimension 0, may hold values from 0.1 to 1
- primal_step: float32 [98304], P(('grp', 'rb')), parts along dimension 0, may hold values from 0.1 to 1
- primal_mask: int32 [4, 16, 49152], P(None, 'grp', 'rb'), parts along dimension 1, may hold values 0 or 1
- dual_mask: int32 [4, 16, 32768], P(None, 'grp', 'rb'), parts along dimension 1, may hold values 0 or 1
- cot_x: float32 [16, 49152], P('grp', 'rb'), parts along dimension 0, may hold values from -6 to 6
- cot_y: float32 [16, 32768], P('grp', 'rb'), parts along dimension 0, may hold values from -6 to 6
Outputs:
- grad_cost: float32 [16, 49152], P('grp', 'rb'), parts along dimension 0
- grad_rhs: float32 [16, 32768], P('grp', 'rb'), parts along dimension 0
- grad_primal: float32 [16, 49152], P('grp', 'rb'), parts along dimension 0
- grad_dual: float32 [16, 32768], P('grp', 'rb'), parts along dimension 0
The draws below stay inside these ranges and needn't reach their ends.
There are 2 independent parts, one for each index of `grp`. The reference program is written for one: setup_inputs(seed, part) draws one part's arguments, and reference() takes and returns one part's arrays. A program takes and returns all parts, laid end to end along the dimension named above; each array names one. Nothing has to cross between parts.
Inputs may be any that keep to these rules, and one draw needn't show every extreme that they name: `tile_rows`: row block within its device's 8 row blocks. `tile_cols`: the owner of column block j is device j // 12; among the tiles of one device at most 6 have column blocks of one owner, and every device has 6 such tiles for some owner. A device's live tiles are the first tile_counts entries of its lists; some device has all 88 live in every draw.
All inputs are finite; a program needn't handle non-finite values. No bound on the sum of `primal_mask` or of `dual_mask` on one device may be relied on, other than what follows from the above.
Results may differ from the reference program's by a relative error of at most 0.008.
Values may be sent and summed in bfloat16 or wider, within the bound.
No kernel may reach another device: no remote copies, remote signals or barrier semaphores. Data moves between devices by JAX's collectives and lax.ppermute only.
A program may use at most 64 MiB of HBM per device.

```python
import math
import jax
import jax.numpy as jnp
from jax import lax

TILE = 256
BATCH = 8
RB_DEV = 8
CB_DEV = 12
TILES_DEV = 88
ITERS = 4
CAP = 6
ROWS = 32768
COLS = 49152
NTILES = 1408
N_RB = 16


def draw_tile_rows(key, part):
    key = jax.random.fold_in(key, 7)
    return jax.random.randint(key, (N_RB * TILES_DEV,), 0, RB_DEV).astype(jnp.int32)


def draw_tile_cols(key, part):
    key = jax.random.fold_in(key, 11)

    def one_device(device):
        device_key = jax.random.fold_in(key, device)
        order_key, within_key = jax.random.split(device_key)
        order = jax.random.permutation(order_key, N_RB * CAP).astype(jnp.int32)
        owners = order // CAP
        first = owners[0]
        score = jnp.where(owners == first, order % CAP - N_RB * CAP, jnp.arange(N_RB * CAP, dtype=jnp.int32))
        arranged = order[jnp.argsort(score, stable=True)]
        chosen = arranged[:TILES_DEV] // CAP
        within = jax.random.randint(within_key, (TILES_DEV,), 0, CB_DEV)
        return (chosen * CB_DEV + within).astype(jnp.int32)
    return jax.vmap(one_device)(jnp.arange(N_RB, dtype=jnp.int32)).reshape(-1)


def draw_tile_counts(key, part):
    key = jax.random.fold_in(key, 13)
    base_key, full_key = jax.random.split(key)
    lowest = max(CAP, TILES_DEV // 3)
    base = jax.random.randint(base_key, (N_RB,), lowest, TILES_DEV + 1)
    fullest = jax.random.randint(full_key, (), 0, N_RB)
    return jnp.where(jnp.arange(N_RB) == fullest, TILES_DEV, base).astype(jnp.int32)


def set_ends(values, own_key, low, high):
    dims = values.shape
    spot = [jax.random.randint(jax.random.fold_in(own_key, axis), (), 0, dims[axis]) for axis in range(len(dims))]
    values = values.at[tuple(spot)].set(low)
    longest = dims.index(max(dims))
    spot[longest] = (spot[longest] + 1) % dims[longest]
    return values.at[tuple(spot)].set(high)


def block_levels(stream_key, dims, cuts, low, top_value):
    level, own = 1.0, jax.random.fold_in(stream_key, 6)
    for position, shards_of in cuts:
        steps = jnp.exp(jax.random.uniform(jax.random.fold_in(own, position), (shards_of,), jnp.float32, low / len(cuts), top_value / len(cuts)))
        level = level * jnp.repeat(steps, dims[position] // shards_of).reshape([-1 if axis == position else 1 for axis in range(len(dims))])
    return level


def scatter_about(key, shape, spread, most, cuts=(), kind=jnp.bfloat16):
    result = spread * jax.random.normal(key, shape, jnp.float32)
    if cuts:
        result = result * block_levels(key, shape, cuts, -0.22, 0.18)
    return jnp.clip(result, -most, most).astype(kind)


def setup_inputs(seed: int = 0, part: int = 0) -> dict:
    key_of = jax.random.split(jax.random.key(seed), 11)
    own_keys = jax.random.split(jax.random.fold_in(key_of[10], part), 11)
    tiles = scatter_about(own_keys[0], (NTILES, TILE, TILE), (2 * TILE) ** -0.5, 0.25, ((0, 16),))
    tile_rows = draw_tile_rows(jax.random.fold_in(jax.random.fold_in(key_of[10], part), 71), part)
    tile_cols = draw_tile_cols(jax.random.fold_in(jax.random.fold_in(key_of[10], part), 71), part)
    tile_counts = draw_tile_counts(jax.random.fold_in(jax.random.fold_in(key_of[10], part), 71), part)
    dual_step = jnp.clip(jnp.exp(math.log(1.0) - 2.3025851 * jax.random.uniform(own_keys[4], (ROWS,), jnp.float32) ** block_levels(own_keys[4], (ROWS,), ((0, 16),), -0.2, 0.2)), 0.1, 1.0)
    primal_step = jnp.clip(jnp.exp(math.log(1.0) - 2.3025851 * jax.random.uniform(own_keys[5], (COLS,), jnp.float32) ** block_levels(own_keys[5], (COLS,), ((0, 16),), -0.2, 0.2)), 0.1, 1.0)
    primal_mask = set_ends((jax.random.randint(own_keys[6], (ITERS, BATCH, COLS), 0, 4) < 3).astype(jnp.int32), jax.random.fold_in(own_keys[6], 1), 0, 1)
    dual_mask = set_ends((jax.random.randint(own_keys[7], (ITERS, BATCH, ROWS), 0, 2) < 1).astype(jnp.int32), jax.random.fold_in(own_keys[7], 1), 0, 1)
    cot_x = scatter_about(own_keys[8], (BATCH, COLS), 1.0, 6.0, ((1, 16),), jnp.float32)
    cot_y = scatter_about(own_keys[9], (BATCH, ROWS), 1.0, 6.0, ((1, 16),), jnp.float32)
    return {"tiles": tiles, "tile_rows": tile_rows, "tile_cols": tile_cols, "tile_counts": tile_counts, "dual_step": dual_step, "primal_step": primal_step, "primal_mask": primal_mask, "dual_mask": dual_mask, "cot_x": cot_x, "cot_y": cot_y}


def reference(tiles, tile_rows, tile_cols, tile_counts, dual_step, primal_step, primal_mask, dual_mask, cot_x, cot_y):
    blocks = tiles.reshape(N_RB, TILES_DEV, TILE, TILE)
    offsets = RB_DEV * jnp.arange(N_RB, dtype=jnp.int32)
    rows_global = (tile_rows.reshape(N_RB, TILES_DEV) + offsets[:, None]).astype(jnp.int32)
    columns = tile_cols.reshape(N_RB, TILES_DEV).astype(jnp.int32)
    live = (jnp.arange(TILES_DEV, dtype=jnp.int32)[None, :] < tile_counts[:, None]).astype(jnp.float32)
    row_total = N_RB * RB_DEV
    col_total = N_RB * CB_DEV

    def forward(moved_blocks):
        def one_device(total, parts):
            tile_set, row_set, col_set, live_set = parts
            picked = moved_blocks[:, col_set].astype(jnp.float32)
            product = jnp.einsum("btj,tij->bti", picked, tile_set.astype(jnp.float32), precision=lax.Precision.HIGHEST)
            product = product * live_set[None, :, None]
            return total.at[:, row_set].add(product), None
        start = jnp.zeros((BATCH, row_total, TILE), jnp.float32)
        return lax.scan(one_device, start, (blocks, rows_global, columns, live))[0]

    def transpose(scaled_blocks):
        def one_device(total, parts):
            tile_set, row_set, col_set, live_set = parts
            picked = scaled_blocks[:, row_set].astype(jnp.float32)
            product = jnp.einsum("bti,tij->btj", picked, tile_set.astype(jnp.float32), precision=lax.Precision.HIGHEST)
            rounded = lax.optimization_barrier(product.astype(jnp.bfloat16))
            term = rounded.astype(jnp.float32) * live_set[None, :, None]
            return total.at[:, col_set].add(term), None
        start = jnp.zeros((BATCH, col_total, TILE), jnp.float32)
        return lax.scan(one_device, start, (blocks, rows_global, columns, live))[0]

    grad_x = cot_x
    grad_y = cot_y
    grad_cost = jnp.zeros((BATCH, COLS), jnp.float32)
    grad_rhs = jnp.zeros((BATCH, ROWS), jnp.float32)
    for step in reversed(range(ITERS)):
        dual_part = dual_mask[step].astype(jnp.float32) * grad_y
        scaled = dual_step[None, :] * dual_part
        scaled_bf = scaled.astype(jnp.bfloat16)
        back = transpose(scaled_bf.reshape(BATCH, row_total, TILE)).reshape(BATCH, COLS)
        primal_part = primal_mask[step].astype(jnp.float32) * (grad_x + 2.0 * back)
        moved = primal_step[None, :] * primal_part
        moved_bf = moved.astype(jnp.bfloat16)
        grad_x = primal_part - back
        ahead = forward(moved_bf.reshape(BATCH, col_total, TILE)).reshape(BATCH, ROWS)
        grad_y = dual_part - ahead
        grad_cost = grad_cost - moved
        grad_rhs = grad_rhs - scaled
    return grad_cost, grad_rhs, grad_x, grad_y
```

```python
import functools

import jax
import jax.numpy as jnp
from jax import lax
from jax.experimental import pallas as pl
from jax.experimental.pallas import tpu as pltpu
from jax.sharding import PartitionSpec as P

QUAD = 4
CHUNK = 8
VM = pl.BlockSpec(memory_space=pltpu.VMEM)
SM = pl.BlockSpec(memory_space=pltpu.SMEM)
ANY = pl.BlockSpec(memory_space=pl.ANY)
PARAMS = pltpu.CompilerParams(vmem_limit_bytes=20 * 1024 * 1024)


def shape(dims, dtype):
    return jax.ShapeDtypeStruct(dims, dtype)


def dual_update(step, side, dy, dual_mask, dual_step, hb, h_into):
    for r in range(hb.shape[0]):
        at = pl.ds(r * side, side)
        h = dual_step[:, at] * dy[:, at]
        hb[r] = h.astype(jnp.bfloat16)
        h_into(at, h)


def transpose_products(first, count, tiles, rows, slots, hb, staged):
    for j in range(count):
        t = first + j
        term = jnp.dot(hb[rows[t]], tiles[t], preferred_element_type=jnp.float32)
        staged[slots[t]] = term.astype(jnp.bfloat16)


def spread(staged, outs):
    for x, out in enumerate(outs):
        for s in range(out.shape[0]):
            out[s] = staged[x * out.shape[0] + s]


def start_kernel(step, peers, cap, col_blocks, place, rows, cols, count, tiles, dual_step, dual_mask, cot_y,
                 held, dy, rhs, slots, lands, wants, o0, o1, o2, o3, hb, staged, filled, sems):
    side = tiles.shape[1]
    tile_slots = tiles.shape[0]
    group = peers // QUAD
    per = group * cap
    chunks = tile_slots // CHUNK
    copies = [
        pltpu.make_async_copy(tiles.at[pl.ds(c * CHUNK, CHUNK)], held.at[pl.ds(c * CHUNK, CHUNK)], sems.at[c])
        for c in range(chunks)
    ]
    for copy in copies:
        copy.start()
    dy[...] = dual_mask[step].astype(jnp.float32) * cot_y[...]

    def h_into(at, h):
        rhs[:, at] = -h

    dual_update(step, side, dy, dual_mask, dual_step, hb, h_into)
    me = place[0]
    my_high, my_quad = me // QUAD, me % QUAD
    for x in range(QUAD):
        for s in range(per):
            wants[x, s] = group * col_blocks

    def clear(o, _):
        filled[o] = 0
        return 0

    lax.fori_loop(0, peers, clear, 0)

    def place_tile(t, _):
        col = cols[t]
        owner = col // col_blocks
        live = t < count[0]
        rank = filled[owner]
        high, quad = (owner // QUAD) ^ my_high, (owner % QUAD) ^ my_quad
        within = high * cap + rank
        slots[t] = jnp.where(live, quad * per + within, QUAD * per)
        lands[t] = jnp.where(live, rows[t], hb.shape[0])

        @pl.when(live)
        def _():
            filled[owner] = rank + 1
            wants[quad, within] = high * col_blocks + (col - owner * col_blocks)

        return 0

    lax.fori_loop(0, tile_slots, place_tile, 0)

    def one_chunk(c, _):
        pltpu.make_async_copy(tiles.at[pl.ds(c * CHUNK, CHUNK)], held.at[pl.ds(c * CHUNK, CHUNK)], sems.at[c]).wait()
        transpose_products(c * CHUNK, CHUNK, held, rows, slots, hb, staged)
        return 0

    lax.fori_loop(0, chunks, one_chunk, 0)
    spread(staged, (o0, o1, o2, o3))


def sum_kernel(wants, got1, got2, got3, a0, a1, a2, a3, *rest):
    total = rest[-1]
    outs = rest[:-1]
    total[...] = jnp.zeros_like(total)
    for x, (want, part) in enumerate(((None, a0), (got1, a1), (got2, a2), (got3, a3))):
        for s in range(part.shape[0]):
            c = wants[0, s] if x == 0 else want[x, s]
            total[c] = total[c] + part[s].astype(jnp.float32)
    blocks = outs[0].shape[0]
    for high, out in enumerate(outs):
        for c in range(blocks):
            out[c] = total[high * blocks + c].astype(out.dtype)


def primal_kernel(step, first, primal_mask, primal_step, x, cost, *refs):
    parts, (new_x, new_cost, q_out) = refs[:-3], refs[-3:]
    blocks, _, side = q_out.shape
    for c in range(blocks):
        at = pl.ds(c * side, side)
        u = parts[0][c]
        for part in parts[1:]:
            u = u + part[c].astype(jnp.float32)
        dx = primal_mask[step, :, at].astype(jnp.float32) * (x[:, at] + 2.0 * u)
        q = primal_step[:, at] * dx
        new_x[:, at] = dx - u
        new_cost[:, at] = -q if first else cost[:, at] - q
        q_out[c] = q.astype(jnp.bfloat16)


def forward_products(tiles, lands, cols, moved, total):
    total[...] = jnp.zeros_like(total)

    def one_chunk(c, _):
        for j in range(CHUNK):
            t = c * CHUNK + j
            product = lax.dot_general(
                moved[cols[t]], tiles[t], (((1,), (1,)), ((), ())), preferred_element_type=jnp.float32
            )
            r = lands[t]
            total[r] = total[r] + product
        return 0

    lax.fori_loop(0, tiles.shape[0] // CHUNK, one_chunk, 0)


def middle_kernel(step, rows, lands, cols, slots, tiles, dual_step, dual_mask, moved, dy, rhs,
                  new_dy, new_rhs, o0, o1, o2, o3, total, hb, staged):
    side = tiles.shape[1]
    forward_products(tiles, lands, cols, moved, total)
    for r in range(total.shape[0] - 1):
        at = pl.ds(r * side, side)
        new_dy[:, at] = dual_mask[step, :, at].astype(jnp.float32) * (dy[:, at] - total[r])

    def h_into(at, h):
        new_rhs[:, at] = rhs[:, at] - h

    dual_update(step, side, new_dy, dual_mask, dual_step, hb, h_into)

    def one_chunk(c, _):
        transpose_products(c * CHUNK, CHUNK, tiles, rows, slots, hb, staged)
        return 0

    lax.fori_loop(0, tiles.shape[0] // CHUNK, one_chunk, 0)
    spread(staged, (o0, o1, o2, o3))


def last_kernel(lands, cols, tiles, moved, dy, new_y, total):
    side = tiles.shape[1]
    forward_products(tiles, lands, cols, moved, total)
    for r in range(total.shape[0] - 1):
        at = pl.ds(r * side, side)
        new_y[:, at] = dy[:, at] - total[r]


def on_device(tiles, tile_rows, tile_cols, tile_counts, dual_step, primal_step, primal_mask, dual_mask, cot_x, cot_y):
    peers = lax.axis_size("rb")
    me = lax.axis_index("rb").astype(jnp.int32)
    tile_slots, side, _ = tiles.shape
    batch = cot_x.shape[0]
    row_blocks = dual_step.shape[0] // side
    col_blocks = primal_step.shape[0] // side
    cap = max(2, (tile_slots + peers - 1) // peers)
    group = peers // QUAD
    per = group * cap
    steps = primal_mask.shape[0]
    dual_step = dual_step.reshape(1, -1)
    primal_step = primal_step.reshape(1, -1)
    f32, bf16 = jnp.float32, jnp.bfloat16
    y_shape = shape(cot_y.shape, f32)
    x_shape = shape(cot_x.shape, f32)
    out_part = shape((per, batch, side), bf16)
    block_set = shape((col_blocks, batch, side), bf16)
    hb_scratch = pltpu.VMEM((row_blocks, batch, side), bf16)
    staged_scratch = pltpu.VMEM((QUAD * per + 1, batch, side), bf16)
    row_total = pltpu.VMEM((row_blocks + 1, batch, side), f32)

    def near(x):
        return [(p, p ^ x) for p in range(peers)]

    def far(x):
        return [(p, p ^ (x * QUAD)) for p in range(peers)]

    step = steps - 1
    held, dy, rhs, slots, lands, wants, *outs = pl.pallas_call(
        functools.partial(start_kernel, step, peers, cap, col_blocks),
        out_shape=(
            pltpu.VMEM(tiles.shape, bf16), y_shape, y_shape, shape((tile_slots,), jnp.int32), shape((tile_slots,), jnp.int32),
            shape((QUAD, per), jnp.int32), out_part, out_part, out_part, out_part,
        ),
        in_specs=[SM, SM, SM, SM, ANY, VM, VM, VM],
        out_specs=(VM, VM, VM, SM, SM, SM, VM, VM, VM, VM),
        scratch_shapes=[hb_scratch, staged_scratch, pltpu.SMEM((peers,), jnp.int32),
                        pltpu.SemaphoreType.DMA((tile_slots // CHUNK,))],
        compiler_params=PARAMS,
        name="start",
    )(me.reshape(1), tile_rows, tile_cols, tile_counts, tiles, dual_step, dual_mask, cot_y)
    got_wants = [lax.ppermute(wants, "rb", near(x)) for x in range(1, QUAD)]
    x_state, cost = cot_x, cot_x
    while True:
        parts = [outs[0]] + [lax.ppermute(outs[x], "rb", near(x)) for x in range(1, QUAD)]
        sums = pl.pallas_call(
            sum_kernel,
            out_shape=(shape(block_set.shape, f32),) + (block_set,) * (group - 1),
            in_specs=[SM] * 4 + [VM] * 4,
            out_specs=(VM,) * group,
            scratch_shapes=[pltpu.VMEM((group * col_blocks + 1, batch, side), f32)],
            compiler_params=PARAMS,
            name="quad_sum",
        )(wants, *got_wants, *parts)
        parts = [sums[0]] + [lax.ppermute(sums[x], "rb", far(x)) for x in range(1, group)]
        x_state, cost, moved = pl.pallas_call(
            functools.partial(primal_kernel, step, step == steps - 1),
            out_shape=(x_shape, x_shape, block_set),
            in_specs=[VM] * (4 + group),
            out_specs=(VM,) * 3,
            compiler_params=PARAMS,
            name="primal",
        )(primal_mask, primal_step, x_state, cost, *parts)
        moved = lax.all_gather(moved, "rb", axis=0, tiled=True)
        if step == 0:
            break
        step -= 1
        dy, rhs, *outs = pl.pallas_call(
            functools.partial(middle_kernel, step),
            out_shape=(y_shape, y_shape, out_part, out_part, out_part, out_part),
            in_specs=[SM] * 4 + [VM] * 6,
            out_specs=(VM,) * 6,
            scratch_shapes=[row_total, hb_scratch, staged_scratch],
            compiler_params=PARAMS,
            name="middle",
        )(tile_rows, lands, tile_cols, slots, held, dual_step, dual_mask, moved, dy, rhs)
    y_state = pl.pallas_call(
        last_kernel,
        out_shape=y_shape,
        in_specs=[SM] * 2 + [VM] * 3,
        out_specs=VM,
        scratch_shapes=[row_total],
        compiler_params=PARAMS,
        name="last",
    )(lands, tile_cols, held, moved, dy)
    return cost, rhs, x_state, y_state


def solution(mesh):
    rb = ("grp", "rb")
    return jax.shard_map(
        on_device,
        mesh=mesh,
        in_specs=(
            P(rb, None, None), P(rb), P(rb), P(rb), P(rb), P(rb),
            P(None, "grp", "rb"), P(None, "grp", "rb"), P("grp", "rb"), P("grp", "rb"),
        ),
        out_specs=(P("grp", "rb"),) * 4,
        check_vma=False,
    )
```

```python
import functools

import jax
import jax.numpy as jnp
from jax import lax
from jax.experimental import pallas as pl
from jax.experimental.pallas import tpu as pltpu
from jax.sharding import PartitionSpec as P

QUAD = 4
CHUNK = 8
VM = pl.BlockSpec(memory_space=pltpu.VMEM)
SM = pl.BlockSpec(memory_space=pltpu.SMEM)
ANY = pl.BlockSpec(memory_space=pl.ANY)
PARAMS = pltpu.CompilerParams(vmem_limit_bytes=16 * 1024 * 1024)
F32, BF16, I32 = jnp.float32, jnp.bfloat16, jnp.int32


def shape(dims, dtype):
    return jax.ShapeDtypeStruct(dims, dtype)


def scaled_blocks(side, dy, dual_step, hb, h_into):
    for r in range(hb.shape[0]):
        at = pl.ds(r * side, side)
        h = dual_step[:, at] * dy[:, at]
        hb[r] = h.astype(BF16)
        h_into(at, h)


def transpose_products(first, tiles, rows, slots, hb, out):
    for j in range(CHUNK):
        t = first + j
        term = jnp.dot(hb[rows[t]], tiles[t], preferred_element_type=F32)
        out[slots[t]] = term.astype(BF16)


def forward_products(turned, lands, places, moved, total):
    total[...] = jnp.zeros_like(total)

    def one_chunk(c, _):
        for j in range(CHUNK):
            t = c * CHUNK + j
            product = jnp.dot(moved[places[t]], turned[t], preferred_element_type=F32)
            r = lands[t]
            total[r] = total[r] + product
        return 0

    lax.fori_loop(0, turned.shape[0] // CHUNK, one_chunk, 0)


def start_kernel(step, peers, cap, col_blocks, rows_in, cols_in, count_in, tiles, dual_step, dual_mask, cot_y,
                 held, turned, dy, rhs, slots, places, lands, rows, out, cols, count, hb, filled, taken, sems, small):
    tile_slots, side, _ = tiles.shape
    group = peers // QUAD
    per = group * cap
    chunks = tile_slots // CHUNK
    minor = [
        pltpu.make_async_copy(src, dst, small.at[i])
        for i, (src, dst) in enumerate(((rows_in, rows), (cols_in, cols), (count_in, count)))
    ]
    for copy in minor:
        copy.start()

    def tile_copy(c):
        at = pl.ds(c * CHUNK, CHUNK)
        return pltpu.make_async_copy(tiles.at[at], held.at[at], sems.at[c])

    for c in range(chunks):
        tile_copy(c).start()
    dy[...] = dual_mask[step].astype(F32) * cot_y[...]

    def h_into(at, h):
        rhs[:, at] = -h

    scaled_blocks(side, dy, dual_step, hb, h_into)
    for copy in minor:
        copy.wait()

    def clear(o, _):
        filled[o] = 0
        return 0

    lax.fori_loop(0, peers, clear, 0)

    def clear_slot(s, _):
        taken[s] = 0
        return 0

    lax.fori_loop(0, QUAD * per, clear_slot, 0)
    lane = lax.broadcasted_iota(I32, (2 * QUAD, side), 1)
    line = lax.broadcasted_iota(I32, (2 * QUAD, side), 0)

    def place_tile(t, plan):
        col = cols[t]
        owner = col // col_blocks
        live = t < count[0]
        rank = filled[owner]
        high, quad = owner // QUAD, owner % QUAD
        within = high * cap + rank
        slot = quad * per + within
        slots[t] = jnp.where(live, slot, -1)
        lands[t] = jnp.where(live, rows[t], hb.shape[0])

        @pl.when(live)
        def _():
            filled[owner] = rank + 1
            taken[slot] = 1

        here = (lane == within) & live
        plan = jnp.where(here & (line == 2 * quad), high, plan)
        return jnp.where(here & (line == 2 * quad + 1), col - owner * col_blocks, plan)

    plan = lax.fori_loop(0, tile_slots, place_tile, jnp.full((2 * QUAD, side), -1, I32))
    for q in range(QUAD):
        out[q * (per + 1) + per] = plan.astype(BF16)
    spare = lax.fori_loop(0, QUAD * per, lambda s, best: jnp.where(taken[s] == 0, s, best), 0)

    def settle(t, _):
        slot = jnp.where(slots[t] < 0, spare, slots[t])
        slots[t] = slot
        places[t] = slot + slot // per
        return 0

    lax.fori_loop(0, tile_slots, settle, 0)

    def one_chunk(c, _):
        tile_copy(c).wait()
        transpose_products(c * CHUNK, held, rows, places, hb, out)
        for j in range(CHUNK):
            turned[c * CHUNK + j] = held[c * CHUNK + j].T
        return 0

    lax.fori_loop(0, chunks, one_chunk, 0)


def read_plan(col_blocks, group, got, wants, whole, sem):
    per = wants.shape[0] // QUAD
    mine = lax.axis_index("rb") % QUAD
    line = lax.broadcasted_iota(I32, got.shape[1:], 0)
    for q in range(QUAD):
        plan = got[q * (per + 1) + per].astype(F32)
        high = jnp.sum(jnp.where(line == 2 * mine, plan, 0.0), axis=0, keepdims=True)
        within = jnp.sum(jnp.where(line == 2 * mine + 1, plan, 0.0), axis=0, keepdims=True)
        index = jnp.where(high < 0.0, float(group * col_blocks), high * col_blocks + within)
        whole[pl.ds(q, 1)] = index.astype(I32)


def sum_kernel(first, col_blocks, *refs):
    if first:
        got, out, wants, total, whole, wide, sem = refs
    else:
        wants, got, out, total = refs
    group = out.shape[0] // col_blocks
    per = wants.shape[0] // QUAD
    stride = got.shape[0] // QUAD
    if first:
        read_plan(col_blocks, group, got, wants, whole, sem)
        copy = pltpu.make_async_copy(whole, wide, sem)
        copy.start()
    total[...] = jnp.zeros_like(total)
    if first:
        copy.wait()
    for q in range(QUAD):
        for s in range(per):
            if first:
                c = wide[q, s]
                wants[q * per + s] = c
            else:
                c = wants[q * per + s]
            total[c] = total[c] + got[q * stride + s].astype(F32)
    for c in range(out.shape[0]):
        out[c] = total[c].astype(BF16)


def primal_kernel(step, first, primal_mask, primal_step, x, cost, got, new_x, new_cost, out):
    side = out.shape[2]
    blocks = new_x.shape[1] // side
    group = out.shape[0] // blocks
    for c in range(blocks):
        at = pl.ds(c * side, side)
        u = got[c].astype(F32)
        for high in range(1, group):
            u = u + got[high * blocks + c].astype(F32)
        dx = primal_mask[step, :, at].astype(F32) * (x[:, at] + 2.0 * u)
        q = primal_step[:, at] * dx
        new_x[:, at] = dx - u
        new_cost[:, at] = -q if first else cost[:, at] - q
        rounded = q.astype(BF16)
        for high in range(group):
            out[high * blocks + c] = rounded


def pick_kernel(wants, blocks, out):
    last = blocks.shape[0] - 1
    for s in range(out.shape[0]):
        out[s] = blocks[jnp.minimum(wants[s], last)]


def middle_kernel(step, rows, lands, slots, held, turned, dual_step, dual_mask, moved, dy, rhs,
                  new_dy, new_rhs, out, total, hb):
    side = held.shape[1]
    forward_products(turned, lands, slots, moved, total)
    for r in range(total.shape[0] - 1):
        at = pl.ds(r * side, side)
        new_dy[:, at] = dual_mask[step, :, at].astype(F32) * (dy[:, at] - total[r])

    def h_into(at, h):
        new_rhs[:, at] = rhs[:, at] - h

    scaled_blocks(side, new_dy, dual_step, hb, h_into)

    def one_chunk(c, _):
        transpose_products(c * CHUNK, held, rows, slots, hb, out)
        return 0

    lax.fori_loop(0, held.shape[0] // CHUNK, one_chunk, 0)


def last_kernel(lands, slots, turned, moved, dy, new_y, total):
    side = turned.shape[1]
    forward_products(turned, lands, slots, moved, total)
    for r in range(total.shape[0] - 1):
        at = pl.ds(r * side, side)
        new_y[:, at] = dy[:, at] - total[r]


def on_device(tiles, tile_rows, tile_cols, tile_counts, dual_step, primal_step, primal_mask, dual_mask, cot_x, cot_y):
    peers = lax.axis_size("rb")
    tile_slots, side, _ = tiles.shape
    batch = cot_x.shape[0]
    row_blocks = dual_step.shape[0] // side
    col_blocks = primal_step.shape[0] // side
    cap = max(2, (tile_slots + peers - 1) // peers)
    group = peers // QUAD
    per = group * cap
    steps = primal_mask.shape[0]
    dual_step = dual_step.reshape(1, -1)
    primal_step = primal_step.reshape(1, -1)
    y_shape = shape(cot_y.shape, F32)
    x_shape = shape(cot_x.shape, F32)
    slot_set = shape((QUAD * per, batch, side), BF16)
    block_set = shape((group * col_blocks, batch, side), BF16)
    per_tile = shape((tile_slots,), I32)
    hb_scratch = pltpu.VMEM((row_blocks, batch, side), BF16)
    row_total = pltpu.VMEM((row_blocks + 1, batch, side), F32)
    col_total = pltpu.VMEM((group * col_blocks + 1, batch, side), F32)
    near = [[h * QUAD + q for q in range(QUAD)] for h in range(group)]
    far = [[h * QUAD + q for h in range(group)] for q in range(QUAD)]

    def swap(array, groups):
        return lax.all_to_all(array, "rb", 0, 0, axis_index_groups=groups, tiled=True)

    step = steps - 1
    held, turned, dy, rhs, slots, places, lands, rows, sent = pl.pallas_call(
        functools.partial(start_kernel, step, peers, cap, col_blocks),
        out_shape=(
            pltpu.VMEM(tiles.shape, BF16), pltpu.VMEM(tiles.shape, BF16), y_shape, y_shape,
            per_tile, per_tile, per_tile, per_tile, shape((QUAD * (per + 1), batch, side), BF16),
        ),
        in_specs=[ANY, ANY, ANY, ANY, VM, VM, VM],
        out_specs=(VM, VM, VM, VM, SM, SM, SM, SM, VM),
        scratch_shapes=[
            pltpu.SMEM((tile_slots,), I32), pltpu.SMEM((1,), I32), hb_scratch, pltpu.SMEM((peers,), I32),
            pltpu.SMEM((QUAD * per,), I32), pltpu.SemaphoreType.DMA((tile_slots // CHUNK,)),
            pltpu.SemaphoreType.DMA((3,)),
        ],
        compiler_params=PARAMS,
        name="start",
    )(tile_rows, tile_cols, tile_counts, tiles, dual_step, dual_mask, cot_y)
    x_state, cost, wants = cot_x, cot_x, None
    while True:
        got = swap(sent, near)
        if wants is None:
            sums, wants = pl.pallas_call(
                functools.partial(sum_kernel, True, col_blocks),
                out_shape=(block_set, shape((QUAD * per,), I32)),
                in_specs=[VM],
                out_specs=(VM, SM),
                scratch_shapes=[
                    col_total, pltpu.VMEM((8, side), I32), pltpu.SMEM((8, side), I32), pltpu.SemaphoreType.DMA,
                ],
                compiler_params=PARAMS,
                name="quad_sum_plan",
            )(got)
        else:
            sums = pl.pallas_call(
                functools.partial(sum_kernel, False, col_blocks),
                out_shape=block_set,
                in_specs=[SM, VM],
                out_specs=VM,
                scratch_shapes=[col_total],
                compiler_params=PARAMS,
                name="quad_sum",
            )(wants, got)
        x_state, cost, moved = pl.pallas_call(
            functools.partial(primal_kernel, step, step == steps - 1),
            out_shape=(x_shape, x_shape, block_set),
            in_specs=[VM] * 5,
            out_specs=(VM,) * 3,
            compiler_params=PARAMS,
            name="primal",
        )(primal_mask, primal_step, x_state, cost, swap(sums, far))
        picked = pl.pallas_call(
            pick_kernel,
            out_shape=slot_set,
            in_specs=[SM, VM],
            out_specs=VM,
            compiler_params=PARAMS,
            name="pick",
        )(wants, swap(moved, far))
        moved = swap(picked, near)
        if step == 0:
            break
        step -= 1
        dy, rhs, sent = pl.pallas_call(
            functools.partial(middle_kernel, step),
            out_shape=(y_shape, y_shape, slot_set),
            in_specs=[SM] * 3 + [VM] * 7,
            out_specs=(VM,) * 3,
            scratch_shapes=[row_total, hb_scratch],
            compiler_params=PARAMS,
            name="middle",
        )(rows, lands, slots, held, turned, dual_step, dual_mask, moved, dy, rhs)
    y_state = pl.pallas_call(
        last_kernel,
        out_shape=y_shape,
        in_specs=[SM] * 2 + [VM] * 3,
        out_specs=VM,
        scratch_shapes=[row_total],
        compiler_params=PARAMS,
        name="last",
    )(lands, slots, turned, moved, dy)
    return cost, rhs, x_state, y_state


def solution(mesh):
    rb = ("grp", "rb")
    return jax.shard_map(
        on_device,
        mesh=mesh,
        in_specs=(
            P(rb, None, None), P(rb), P(rb), P(rb), P(rb), P(rb),
            P(None, "grp", "rb"), P(None, "grp", "rb"), P("grp", "rb"), P("grp", "rb"),
        ),
        out_specs=(P("grp", "rb"),) * 4,
        check_vma=False,
    )
```

```python
import functools

import jax
import jax.numpy as jnp
from jax import lax
from jax.experimental import pallas as pl
from jax.experimental.pallas import tpu as pltpu
from jax.sharding import PartitionSpec as P

CHUNK = 8
LANES = 4
HALVES = 2
VM = pl.BlockSpec(memory_space=pltpu.VMEM)
SM = pl.BlockSpec(memory_space=pltpu.SMEM)
HBM = pl.BlockSpec(memory_space=pltpu.HBM)
PARAMS = pltpu.CompilerParams(vmem_limit_bytes=12 * 1024 * 1024)
F32, BF16, I32 = jnp.float32, jnp.bfloat16, jnp.int32


def shape(dims, dtype):
    return jax.ShapeDtypeStruct(dims, dtype)


def cost(moved):
    return pl.CostEstimate(flops=moved * 8, bytes_accessed=moved, transcendentals=0)


def scaled_blocks(side, dy, dual_step, hb, h_into):
    for r in range(hb.shape[0]):
        at = pl.ds(r * side, side)
        h = dual_step[:, at] * dy[:, at]
        hb[r] = h.astype(BF16)
        h_into(at, h)


def transpose_products(first, count, tiles, rows, slots, hb, out):
    for j in range(count):
        t = first + j
        term = jnp.dot(hb[rows[t]], tiles[t], preferred_element_type=F32)
        out[slots[t]] = term.astype(BF16)


def forward_products(turned, lands, places, moved, totals):
    for total in totals:
        total[...] = jnp.zeros_like(total)

    def one_chunk(c, _):
        terms = []
        for j in range(CHUNK):
            t = c * CHUNK + j
            terms.append(jnp.dot(moved[places[t]], turned[t], preferred_element_type=F32))
        for j in range(0, CHUNK, LANES):
            spots = [lands[c * CHUNK + j + i] for i in range(LANES)]
            held = [totals[i][spots[i]] + terms[j + i] for i in range(LANES)]
            for i in range(LANES):
                totals[i][spots[i]] = held[i]
        return 0

    lax.fori_loop(0, turned.shape[0] // CHUNK, one_chunk, 0)


def gathered(totals, r):
    value = totals[0][r]
    for total in totals[1:]:
        value = value + total[r]
    return value


def start_kernel(step, rows_of, peers, cap, col_blocks, count, rows_in, cols_in, tiles, step_in, mask_in, cot_in,
                 held, dy, rhs, slots, places, lands, rows, out, cols, dual_step, dual_mask, cot_y, hb, filled,
                 taken, sems, small):
    tile_slots, side, _ = tiles.shape
    chunks = tile_slots // CHUNK
    minor = [
        pltpu.make_async_copy(src, dst, small.at[i])
        for i, (src, dst) in enumerate((
            (rows_in, rows), (cols_in, cols), (step_in, dual_step), (mask_in.at[step], dual_mask),
            (cot_in, cot_y),
        ))
    ]
    for copy in minor:
        copy.start()

    def tile_copy(c):
        at = pl.ds(c * CHUNK, CHUNK)
        return pltpu.make_async_copy(tiles.at[at], held.at[at], sems.at[c])

    for c in range(chunks):
        tile_copy(c).start()
    for copy in minor:
        copy.wait()
    dy[...] = dual_mask[rows_of].astype(F32) * cot_y[rows_of]

    def h_into(at, h):
        rhs[:, at] = -h

    scaled_blocks(side, dy, dual_step, hb, h_into)

    def clear(o, _):
        filled[o] = 0
        return 0

    lax.fori_loop(0, peers, clear, 0)

    def clear_slot(s, _):
        taken[s] = 0
        return 0

    lax.fori_loop(0, peers * cap, clear_slot, 0)
    lane = lax.broadcasted_iota(I32, out.shape[1:], 1)

    def place_tile(t, plan):
        col = cols[t]
        owner = col // col_blocks
        live = t < count[0]
        rank = filled[owner]
        slot = owner * cap + rank
        slots[t] = jnp.where(live, slot, -1)
        lands[t] = jnp.where(live, rows[t], hb.shape[0])

        @pl.when(live)
        def _():
            filled[owner] = rank + 1
            taken[slot] = 1

        return jnp.where((lane == slot) & live, col - owner * col_blocks, plan)

    plan = lax.fori_loop(0, tile_slots, place_tile, jnp.full(out.shape[1:], -1, I32))
    plan = plan.astype(BF16)
    for p in range(peers):
        out[p * (cap + 1) + cap] = plan
    spare = lax.fori_loop(0, peers * cap, lambda s, best: jnp.where(taken[s] == 0, s, best), 0)

    def settle(t, _):
        slot = jnp.where(slots[t] < 0, spare, slots[t])
        slots[t] = slot
        places[t] = slot + slot // cap
        return 0

    lax.fori_loop(0, tile_slots, settle, 0)

    def one_chunk(c, _):
        tile_copy(c).wait()
        transpose_products(c * CHUNK, CHUNK, held, rows, places, hb, out)
        return 0

    lax.fori_loop(0, chunks, one_chunk, 0)


def second_kernel(step, rows_of, rows, slots, held, dual_step, dual_mask, cot_y, turned, dy, rhs, out, hb):
    side = held.shape[1]
    dy[...] = dual_mask[step, rows_of].astype(F32) * cot_y[rows_of]

    def h_into(at, h):
        rhs[:, at] = -h

    scaled_blocks(side, dy, dual_step, hb, h_into)

    def one_chunk(c, _):
        transpose_products(c * CHUNK, CHUNK, held, rows, slots, hb, out)
        for j in range(CHUNK):
            turned[c * CHUNK + j] = held[c * CHUNK + j].T
        return 0

    lax.fori_loop(0, held.shape[0] // CHUNK, one_chunk, 0)


def primal_kernel(step, rows_of, first, plan_in, cap, *refs):
    refs = list(refs)
    wants = None if plan_in else refs.pop(0)
    primal_mask, primal_step, x, spent, got, new_x, new_spent, out = refs[:8]
    rest = refs[8:]
    if plan_in:
        wants = rest.pop(0)
    moved, totals = rest[0], rest[1:1 + LANES]
    _, batch, side = out.shape
    blocks = new_x.shape[1] // side
    slots = out.shape[0]
    peers = slots // cap
    stride = got.shape[0] // peers
    if plan_in:
        whole, wide, sem = rest[1 + LANES:]
        me = lax.axis_index("rb")
        for p in range(peers):
            plan = got[p * stride + cap][0:1].astype(F32)
            whole[pl.ds(p, 1)] = jnp.where(plan < 0.0, float(blocks), plan).astype(I32)
        copy = pltpu.make_async_copy(whole, wide, sem)
        copy.start()
    for total in totals:
        total[...] = jnp.zeros_like(total)
    if plan_in:
        copy.wait()

        def note(p, _):
            for s in range(cap):
                wants[p * cap + s] = wide[p, me * cap + s]
            return 0

        lax.fori_loop(0, peers, note, 0)
    for s in range(0, slots, LANES):
        spots = [wants[s + i] for i in range(LANES)]
        parts = [got[(s + i) // cap * stride + (s + i) % cap].astype(F32) for i in range(LANES)]
        held = [totals[i][spots[i]] + parts[i] for i in range(LANES)]
        for i in range(LANES):
            totals[i][spots[i]] = held[i]
    for c in range(blocks):
        at = pl.ds(c * side, side)
        u = gathered(totals, c)
        state = x[rows_of, at] if first else x[:, at]
        dx = primal_mask[step, rows_of, at].astype(F32) * (state + 2.0 * u)
        q = primal_step[:, at] * dx
        new_x[:, at] = dx - u
        new_spent[:, at] = -q if first else spent[:, at] - q
        moved[c] = q.astype(BF16)
    moved[blocks] = jnp.zeros(moved.shape[1:], BF16)
    for s in range(0, slots, 2 * LANES):
        values = [moved[wants[s + i]] for i in range(2 * LANES)]
        for i in range(2 * LANES):
            out[s + i] = values[i]


def middle_kernel(step, rows_of, rows, lands, slots, held, turned, dual_step, dual_mask, moved, dy, rhs,
                  new_dy, new_rhs, out, hb, *totals):
    side = held.shape[1]
    forward_products(turned, lands, slots, moved, totals)
    for r in range(hb.shape[0]):
        at = pl.ds(r * side, side)
        new_dy[:, at] = dual_mask[step, rows_of, at].astype(F32) * (dy[:, at] - gathered(totals, r))

    def h_into(at, h):
        new_rhs[:, at] = rhs[:, at] - h

    scaled_blocks(side, new_dy, dual_step, hb, h_into)

    def one_chunk(c, _):
        transpose_products(c * CHUNK, CHUNK, held, rows, slots, hb, out)
        return 0

    lax.fori_loop(0, held.shape[0] // CHUNK, one_chunk, 0)


def last_kernel(lands, slots, turned, moved, dy, new_y, *totals):
    side = turned.shape[1]
    forward_products(turned, lands, slots, moved, totals)
    for r in range(totals[0].shape[0] - 1):
        at = pl.ds(r * side, side)
        new_y[:, at] = dy[:, at] - gathered(totals, r)


def on_device(tiles, tile_rows, tile_cols, tile_counts, dual_step, primal_step, primal_mask, dual_mask, cot_x, cot_y):
    peers = lax.axis_size("rb")
    tile_slots, side, _ = tiles.shape
    whole_batch = cot_x.shape[0]
    batch = whole_batch // HALVES
    row_blocks = dual_step.shape[0] // side
    col_blocks = primal_step.shape[0] // side
    cap = max(2, (tile_slots + peers - 1) // peers)
    slots_all = peers * cap
    steps = primal_mask.shape[0]
    dual_step = dual_step.reshape(1, -1)
    primal_step = primal_step.reshape(1, -1)
    y_shape = shape((batch, cot_y.shape[1]), F32)
    x_shape = shape((batch, cot_x.shape[1]), F32)
    slot_set = shape((slots_all, batch, side), BF16)
    per_tile = shape((tile_slots,), I32)
    hb_scratch = pltpu.VMEM((row_blocks, batch, side), BF16)
    row_totals = [pltpu.VMEM((row_blocks + 1, batch, side), F32)] * LANES
    col_totals = [pltpu.VMEM((col_blocks + 1, batch, side), F32)] * LANES
    moved_scratch = pltpu.VMEM((col_blocks + 1, batch, side), BF16)
    tile_bytes = tiles.size * 2

    def swap(array):
        return lax.all_to_all(array, "rb", 0, 0, tiled=True)

    def rows_of(half):
        return slice(half * batch, (half + 1) * batch)

    step = steps - 1
    held, dy, rhs, slots, places, lands, rows, sent = pl.pallas_call(
        functools.partial(start_kernel, step, rows_of(0), peers, cap, col_blocks),
        out_shape=(
            pltpu.VMEM(tiles.shape, BF16), y_shape, y_shape, per_tile, per_tile, per_tile, per_tile,
            shape((peers * (cap + 1), batch, side), BF16),
        ),
        in_specs=[SM] + [HBM] * 6,
        out_specs=(VM, VM, VM, SM, SM, SM, SM, VM),
        scratch_shapes=[
            pltpu.SMEM((tile_slots,), I32), pltpu.VMEM(dual_step.shape, F32),
            pltpu.VMEM(cot_y.shape, I32), pltpu.VMEM(cot_y.shape, F32), hb_scratch, pltpu.SMEM((peers,), I32),
            pltpu.SMEM((slots_all,), I32), pltpu.SemaphoreType.DMA((tile_slots // CHUNK,)),
            pltpu.SemaphoreType.DMA((5,)),
        ],
        compiler_params=PARAMS,
        cost_estimate=cost(2 * tile_bytes),
        name="start",
    )(tile_counts, *(
        pltpu.with_memory_space_constraint(array, pltpu.HBM)
        for array in (tile_rows, tile_cols, tiles, dual_step, dual_mask, cot_y)
    ))
    state_dy, state_rhs, got = [dy], [rhs], [swap(sent)]
    turned = None
    for half in range(1, HALVES):
        turned, dy, rhs, sent = pl.pallas_call(
            functools.partial(second_kernel, step, rows_of(half)),
            out_shape=(pltpu.VMEM(tiles.shape, BF16), y_shape, y_shape, slot_set),
            in_specs=[SM, SM] + [VM] * 4,
            out_specs=(VM,) * 4,
            scratch_shapes=[hb_scratch],
            compiler_params=PARAMS,
            cost_estimate=cost(2 * tile_bytes),
            name="second",
        )(rows, slots, held, dual_step, dual_mask, cot_y)
        state_dy.append(dy)
        state_rhs.append(rhs)
        got.append(swap(sent))
    state_x, spent, wants = [cot_x] * HALVES, [cot_x] * HALVES, None
    while True:
        moved = []
        for half in range(HALVES):
            first = step == steps - 1
            plan_in = wants is None
            outs = (x_shape, x_shape, slot_set)
            specs = (VM,) * 3
            scratch = [moved_scratch] + col_totals
            if plan_in:
                outs += (shape((slots_all,), I32),)
                specs += (SM,)
                scratch += [
                    pltpu.VMEM((peers, side), I32), pltpu.SMEM((peers, side), I32), pltpu.SemaphoreType.DMA,
                ]
            results = pl.pallas_call(
                functools.partial(primal_kernel, step, rows_of(half), first, plan_in, cap),
                out_shape=outs,
                in_specs=([] if plan_in else [SM]) + [VM] * 5,
                out_specs=specs,
                scratch_shapes=scratch,
                compiler_params=PARAMS,
                cost_estimate=cost(1 << 22),
                name="primal_plan" if plan_in else "primal",
            )(*([] if plan_in else [wants]), primal_mask, primal_step, state_x[half], spent[half], got[half])
            state_x[half], spent[half], sent = results[:3]
            if plan_in:
                wants = results[3]
            moved.append(swap(sent))
        if step == 0:
            break
        step -= 1
        for half in range(HALVES):
            state_dy[half], state_rhs[half], sent = pl.pallas_call(
                functools.partial(middle_kernel, step, rows_of(half)),
                out_shape=(y_shape, y_shape, slot_set),
                in_specs=[SM] * 3 + [VM] * 7,
                out_specs=(VM,) * 3,
                scratch_shapes=[hb_scratch] + row_totals,
                compiler_params=PARAMS,
                cost_estimate=cost(2 * tile_bytes),
                name="middle",
            )(rows, lands, slots, held, turned, dual_step, dual_mask, moved[half], state_dy[half], state_rhs[half])
            got[half] = swap(sent)
    state_y = []
    for half in range(HALVES):
        state_y.append(
            pl.pallas_call(
                last_kernel,
                out_shape=y_shape,
                in_specs=[SM] * 2 + [VM] * 3,
                out_specs=VM,
                scratch_shapes=row_totals,
                compiler_params=PARAMS,
                cost_estimate=cost(tile_bytes),
                name="last",
            )(lands, slots, turned, moved[half], state_dy[half])
        )
    return tuple(jnp.concatenate(parts, axis=0) for parts in (spent, state_rhs, state_x, state_y))


def solution(mesh):
    rb = ("grp", "rb")
    return jax.shard_map(
        on_device,
        mesh=mesh,
        in_specs=(
            P(rb, None, None), P(rb), P(rb), P(rb), P(rb), P(rb),
            P(None, "grp", "rb"), P(None, "grp", "rb"), P("grp", "rb"), P("grp", "rb"),
        ),
        out_specs=(P("grp", "rb"),) * 4,
        check_vma=False,
    )
```

```python
import functools

import jax
import jax.numpy as jnp
from jax import lax
from jax.experimental import pallas as pl
from jax.experimental.pallas import tpu as pltpu
from jax.sharding import PartitionSpec as P

QUAD = 4
CHUNK = 8
LANES = 4
VM = pl.BlockSpec(memory_space=pltpu.VMEM)
SM = pl.BlockSpec(memory_space=pltpu.SMEM)
HBM = pl.BlockSpec(memory_space=pltpu.HBM)
PARAMS = pltpu.CompilerParams(vmem_limit_bytes=12 * 1024 * 1024)
F32, BF16, I32 = jnp.float32, jnp.bfloat16, jnp.int32


def shape(dims, dtype):
    return jax.ShapeDtypeStruct(dims, dtype)


def cost(moved):
    return pl.CostEstimate(flops=moved * 8, bytes_accessed=moved, transcendentals=0)


def scaled_blocks(side, dy, dual_step, hb, h_into):
    for r in range(hb.shape[0]):
        at = pl.ds(r * side, side)
        h = dual_step[:, at] * dy[:, at]
        hb[r] = h.astype(BF16)
        h_into(at, h)


def transpose_products(base, tile_of, row_of, tiles, hb, outs):
    per = outs[0].shape[0]
    for x, out in enumerate(outs):
        for s in range(per):
            slot = base + x * per + s
            out[s] = jnp.dot(hb[row_of[slot]], tiles[tile_of[slot]], preferred_element_type=F32).astype(BF16)


def forward_products(base, tile_of, land_of, turned, moved, totals):
    per = moved[0].shape[0]
    for total in totals:
        total[...] = jnp.zeros_like(total)
    for x, part in enumerate(moved):
        first = base + x * per
        terms = [jnp.dot(part[s], turned[tile_of[first + s]], preferred_element_type=F32) for s in range(per)]
        for s in range(0, per, LANES):
            several = range(min(LANES, per - s))
            spots = [land_of[first + s + i] for i in several]
            held = [totals[i][spots[i]] + terms[s + i] for i in several]
            for i in several:
                totals[i][spots[i]] = held[i]


def gathered(totals, r):
    value = totals[0][r]
    for total in totals[1:]:
        value = value + total[r]
    return value


def start_kernel(step, peers, cap, col_blocks, count, rows_in, cols_in, tiles, step_in, mask_in, cot_in,
                 held, dy, rhs, hb, tile_of, row_of, land_of, wants, o0, o1, o2, o3,
                 rows, cols, dual_step, dual_mask, cot_y, filled, sems, small):
    tile_slots, side, _ = tiles.shape
    group = peers // QUAD
    half = group // 2
    chunks = tile_slots // CHUNK
    minor = [
        pltpu.make_async_copy(src, dst, small.at[i])
        for i, (src, dst) in enumerate((
            (cols_in, cols), (rows_in, rows), (step_in, dual_step), (mask_in.at[step], dual_mask), (cot_in, cot_y),
        ))
    ]
    for copy in minor:
        copy.start()

    def tile_copy(c):
        at = pl.ds(c * CHUNK, CHUNK)
        return pltpu.make_async_copy(tiles.at[at], held.at[at], sems.at[c])

    for c in range(chunks):
        tile_copy(c).start()
    for o in range(peers):
        filled[o] = 0
    for s in range(tile_of.shape[0]):
        tile_of[s] = 0
        row_of[s] = 0
        land_of[s] = hb.shape[0]
    for x in range(QUAD):
        for s in range(group * cap):
            wants[x, s] = col_blocks
    for copy in minor:
        copy.wait()
    me = lax.axis_index("rb").astype(I32)
    scale = (1 << 19) // col_blocks + 1

    def place_tile(t, _):
        col = cols[t]
        owner = (col * scale) >> 19
        rank = filled[owner]
        filled[owner] = rank + 1
        apart = owner ^ me
        high, quad = apart // QUAD, apart % QUAD
        place = high * cap + rank
        near = jnp.where(high < half, 1, 0)
        slot = (near * QUAD + quad) * (half * cap) + place - (1 - near) * (half * cap)
        tile_of[slot] = t
        row_of[slot] = rows[t]
        land_of[slot] = rows[t]
        wants[quad, place] = col - owner * col_blocks
        return 0

    lax.fori_loop(0, count[0], place_tile, 0)
    dy[...] = dual_mask[...].astype(F32) * cot_y[...]

    def h_into(at, h):
        rhs[:, at] = -h

    scaled_blocks(side, dy, dual_step, hb, h_into)
    for c in range(chunks):
        tile_copy(c).wait()
    transpose_products(0, tile_of, row_of, held, hb, (o0, o1, o2, o3))


def turn_kernel(held, turned):
    def one_chunk(c, _):
        for j in range(CHUNK):
            turned[c * CHUNK + j] = held[c * CHUNK + j].T
        return 0

    lax.fori_loop(0, held.shape[0] // CHUNK, one_chunk, 0)


def near_product_kernel(tile_of, row_of, held, hb, o0, o1, o2, o3):
    transpose_products(tile_of.shape[0] // 2, tile_of, row_of, held, hb, (o0, o1, o2, o3))


def sum_kernel(first_high, cap, wants, got1, got2, got3, a0, a1, a2, a3, *rest):
    parts = (a0, a1, a2, a3)
    half = a0.shape[0] // cap
    outs, totals = rest[:half], rest[half:]
    for total in totals:
        total[...] = jnp.zeros_like(total)
    for r in range(cap):
        for pair in range(QUAD // 2):
            jobs = []
            for h in range(half):
                for side in range(2):
                    x = 2 * pair + side
                    want = (wants, got1, got2, got3)[x]
                    spot = want[x, (first_high + h) * cap + r]
                    jobs.append((totals[2 * h + side], spot, parts[x][h * cap + r].astype(F32)))
            values = [total[spot] + part for total, spot, part in jobs]
            for (total, spot, _), value in zip(jobs, values):
                total[spot] = value
    for h, out in enumerate(outs):
        for c in range(out.shape[0]):
            out[c] = (totals[2 * h][c] + totals[2 * h + 1][c]).astype(out.dtype)


def primal_kernel(step, first, primal_mask, primal_step, x, spent, *refs):
    parts, (new_x, new_spent, out) = refs[:-3], refs[-3:]
    blocks, _, side = out.shape
    for c in range(blocks):
        at = pl.ds(c * side, side)
        u = parts[0][c]
        for part in parts[1:]:
            u = u + part[c].astype(F32)
        dx = primal_mask[step, :, at].astype(F32) * (x[:, at] + 2.0 * u)
        q = primal_step[:, at] * dx
        new_x[:, at] = dx - u
        new_spent[:, at] = -q if first else spent[:, at] - q
        out[c] = q.astype(BF16)


def pick_kernel(first_high, cap, wants, got1, got2, got3, *refs):
    blocks, outs = refs[:-QUAD], refs[-QUAD:]
    last = blocks[0].shape[0] - 1
    for x, out in enumerate(outs):
        want = (wants, got1, got2, got3)[x]
        values = [
            blocks[h][jnp.minimum(want[x, (first_high + h) * cap + r], last)]
            for h in range(len(blocks))
            for r in range(cap)
        ]
        for s, value in enumerate(values):
            out[s] = value


def near_forward_kernel(tile_of, land_of, turned, m0, m1, m2, m3, out, *totals):
    forward_products(tile_of.shape[0] // 2, tile_of, land_of, turned, (m0, m1, m2, m3), totals)
    for r in range(out.shape[0]):
        out[r] = gathered(totals, r)


def middle_kernel(step, tile_of, row_of, land_of, held, turned, dual_step, dual_mask, part, dy, rhs, m0, m1, m2, m3,
                  new_dy, new_rhs, hb, o0, o1, o2, o3, *totals):
    side = held.shape[1]
    forward_products(0, tile_of, land_of, turned, (m0, m1, m2, m3), totals)
    for r in range(hb.shape[0]):
        at = pl.ds(r * side, side)
        v = part[r] + gathered(totals, r)
        new_dy[:, at] = dual_mask[step, :, at].astype(F32) * (dy[:, at] - v)

    def h_into(at, h):
        new_rhs[:, at] = rhs[:, at] - h

    scaled_blocks(side, new_dy, dual_step, hb, h_into)
    transpose_products(0, tile_of, row_of, held, hb, (o0, o1, o2, o3))


def last_kernel(tile_of, land_of, turned, part, dy, m0, m1, m2, m3, new_y, *totals):
    side = turned.shape[1]
    forward_products(0, tile_of, land_of, turned, (m0, m1, m2, m3), totals)
    for r in range(part.shape[0]):
        at = pl.ds(r * side, side)
        new_y[:, at] = dy[:, at] - (part[r] + gathered(totals, r))


def on_device(tiles, tile_rows, tile_cols, tile_counts, dual_step, primal_step, primal_mask, dual_mask, cot_x, cot_y):
    peers = lax.axis_size("rb")
    tile_slots, side, _ = tiles.shape
    batch = cot_x.shape[0]
    row_blocks = dual_step.shape[0] // side
    col_blocks = primal_step.shape[0] // side
    cap = max(2, (tile_slots + peers - 1) // peers)
    group = peers // QUAD
    half = group // 2
    slots = peers * cap
    steps = primal_mask.shape[0]
    dual_step = dual_step.reshape(1, -1)
    primal_step = primal_step.reshape(1, -1)
    y_shape = shape(cot_y.shape, F32)
    x_shape = shape(cot_x.shape, F32)
    part_set = (shape((half * cap, batch, side), BF16),) * QUAD
    block_set = shape((col_blocks, batch, side), BF16)
    hb_set = shape((row_blocks, batch, side), BF16)
    per_slot = shape((slots,), I32)
    row_totals = [pltpu.VMEM((row_blocks + 1, batch, side), F32)] * LANES
    col_totals = [pltpu.VMEM((col_blocks + 1, batch, side), F32)] * (2 * half)
    tile_bytes = tiles.size * 2

    def call(kernel, name, moved, ins, outs, args, scratch=()):
        return pl.pallas_call(
            kernel,
            out_shape=outs,
            in_specs=ins,
            out_specs=jax.tree.map(lambda _: VM, outs),
            scratch_shapes=scratch,
            compiler_params=PARAMS,
            cost_estimate=cost(moved),
            name=name,
        )(*args)

    def swap(array, x):
        return lax.ppermute(array, "rb", [(p, p ^ x) for p in range(peers)])

    def near_swaps(parts):
        return [parts[0]] + [swap(parts[x], x) for x in range(1, QUAD)]

    step = steps - 1
    held, dy, rhs, hb, tile_of, row_of, land_of, wants, *far_parts = pl.pallas_call(
        functools.partial(start_kernel, step, peers, cap, col_blocks),
        out_shape=(
            pltpu.VMEM(tiles.shape, BF16), y_shape, y_shape, hb_set, per_slot, per_slot, per_slot,
            shape((QUAD, group * cap), I32),
        ) + part_set,
        in_specs=[SM] + [HBM] * 6,
        out_specs=(VM,) * 4 + (SM,) * 4 + (VM,) * QUAD,
        scratch_shapes=[
            pltpu.SMEM((tile_slots,), I32), pltpu.SMEM((tile_slots,), I32), pltpu.VMEM(dual_step.shape, F32),
            pltpu.VMEM(cot_y.shape, I32), pltpu.VMEM(cot_y.shape, F32), pltpu.SMEM((peers,), I32),
            pltpu.SemaphoreType.DMA((tile_slots // CHUNK,)), pltpu.SemaphoreType.DMA((5,)),
        ],
        compiler_params=PARAMS,
        cost_estimate=cost(2 * tile_bytes),
        name="start",
    )(tile_counts, *(
        pltpu.with_memory_space_constraint(array, pltpu.HBM)
        for array in (tile_rows, tile_cols, tiles, dual_step, dual_mask, cot_y)
    ))
    maps = [wants] + [swap(wants, x) for x in range(1, QUAD)]
    turned = call(turn_kernel, "turn", tile_bytes, [VM], pltpu.VMEM(tiles.shape, BF16), (held,))
    x_state, spent = cot_x, cot_x
    while True:
        far_got = near_swaps(far_parts)
        near_parts = call(near_product_kernel, "near_product", tile_bytes // 2, [SM] * 2 + [VM] * 2, part_set,
                          (tile_of, row_of, held, hb))
        near_got = near_swaps(near_parts)
        far_sums = call(functools.partial(sum_kernel, half, cap), "far_sum", 1 << 20, [SM] * QUAD + [VM] * QUAD,
                        (block_set,) * half, (*maps, *far_got), col_totals)
        got = [swap(far_sums[h], (half + h) * QUAD) for h in reversed(range(half))]
        near_sums = call(functools.partial(sum_kernel, 0, cap), "near_sum", 1 << 20, [SM] * QUAD + [VM] * QUAD,
                         (shape(block_set.shape, F32),) + (block_set,) * (half - 1), (*maps, *near_got), col_totals)
        got += [swap(near_sums[h], h * QUAD) for h in range(1, half)]
        x_state, spent, moved = call(
            functools.partial(primal_kernel, step, step == steps - 1), "primal", 1 << 20, [VM] * (4 + group),
            (x_shape, x_shape, block_set), (primal_mask, primal_step, x_state, spent, near_sums[0], *got))
        blocks = [moved] + [swap(moved, h * QUAD) for h in range(1, group)]
        near_moved = near_swaps(call(functools.partial(pick_kernel, 0, cap), "near_pick", 1 << 20,
                                     [SM] * QUAD + [VM] * half, part_set, (*maps, *blocks[:half])))
        far_moved = near_swaps(call(functools.partial(pick_kernel, half, cap), "far_pick", 1 << 20,
                                    [SM] * QUAD + [VM] * half, part_set, (*maps, *blocks[half:])))
        part = call(near_forward_kernel, "near_forward", tile_bytes // 2, [SM] * 2 + [VM] * (1 + QUAD),
                    shape(hb_set.shape, F32), (tile_of, land_of, turned, *near_moved), row_totals)
        if step == 0:
            break
        step -= 1
        dy, rhs, hb, *far_parts = call(
            functools.partial(middle_kernel, step), "middle", tile_bytes, [SM] * 3 + [VM] * (7 + QUAD),
            (y_shape, y_shape, hb_set) + part_set,
            (tile_of, row_of, land_of, held, turned, dual_step, dual_mask, part, dy, rhs, *far_moved), row_totals)
    y_state = call(last_kernel, "last", tile_bytes // 2, [SM] * 2 + [VM] * (3 + QUAD), y_shape,
                   (tile_of, land_of, turned, part, dy, *far_moved), row_totals)
    return spent, rhs, x_state, y_state


def solution(mesh):
    rb = ("grp", "rb")
    return jax.shard_map(
        on_device,
        mesh=mesh,
        in_specs=(
            P(rb, None, None), P(rb), P(rb), P(rb), P(rb), P(rb),
            P(None, "grp", "rb"), P(None, "grp", "rb"), P("grp", "rb"), P("grp", "rb"),
        ),
        out_specs=(P("grp", "rb"),) * 4,
        check_vma=False,
    )
```

```python
import functools

import jax
import jax.numpy as jnp
from jax import lax
from jax.experimental import pallas as pl
from jax.experimental.pallas import tpu as pltpu
from jax.sharding import PartitionSpec as P

QUAD = 4
CHUNK = 8
LANES = 4
VM = pl.BlockSpec(memory_space=pltpu.VMEM)
SM = pl.BlockSpec(memory_space=pltpu.SMEM)
HBM = pl.BlockSpec(memory_space=pltpu.HBM)
PARAMS = pltpu.CompilerParams(vmem_limit_bytes=12 * 1024 * 1024)
F32, BF16, I32 = jnp.float32, jnp.bfloat16, jnp.int32


def shape(dims, dtype):
    return jax.ShapeDtypeStruct(dims, dtype)


def cost(moved):
    return pl.CostEstimate(flops=moved * 8, bytes_accessed=moved, transcendentals=0)


def scaled_blocks(side, dy, dual_step, hb, h_into):
    for r in range(hb.shape[0]):
        at = pl.ds(r * side, side)
        h = dual_step[:, at] * dy[:, at]
        hb[r] = h.astype(BF16)
        h_into(at, h)


def transpose_products(base, tile_of, row_of, tiles, hb, outs):
    per = outs[0].shape[0]
    for x, out in enumerate(outs):
        for s in range(per):
            slot = base + x * per + s
            out[s] = jnp.dot(hb[row_of[slot]], tiles[tile_of[slot]], preferred_element_type=F32).astype(BF16)


def forward_products(base, tile_of, land_of, turned, moved, totals):
    per = moved[0].shape[0]
    for total in totals:
        total[...] = jnp.zeros_like(total)
    for x, part in enumerate(moved):
        first = base + x * per
        terms = [jnp.dot(part[s], turned[tile_of[first + s]], preferred_element_type=F32) for s in range(per)]
        for s in range(0, per, LANES):
            several = range(min(LANES, per - s))
            spots = [land_of[first + s + i] for i in several]
            held = [totals[i][spots[i]] + terms[s + i] for i in several]
            for i in several:
                totals[i][spots[i]] = held[i]


def gathered(totals, r):
    value = totals[0][r]
    for total in totals[1:]:
        value = value + total[r]
    return value


def start_kernel(step, peers, cap, col_blocks, count, rows_in, cols_in, tiles, step_in, mask_in, cot_in,
                 held, dy, rhs, hb, tile_of, row_of, land_of, wants, o0, o1, o2, o3,
                 rows, cols, dual_step, dual_mask, cot_y, filled, sems, small):
    tile_slots, side, _ = tiles.shape
    group = peers // QUAD
    half = group // 2
    chunks = tile_slots // CHUNK
    minor = [
        pltpu.make_async_copy(src, dst, small.at[i])
        for i, (src, dst) in enumerate((
            (cols_in, cols), (rows_in, rows), (step_in, dual_step), (mask_in.at[step], dual_mask), (cot_in, cot_y),
        ))
    ]
    for copy in minor:
        copy.start()

    def tile_copy(c):
        at = pl.ds(c * CHUNK, CHUNK)
        return pltpu.make_async_copy(tiles.at[at], held.at[at], sems.at[c])

    for c in range(chunks):
        tile_copy(c).start()
    for o in range(peers):
        filled[o] = 0
    for s in range(tile_of.shape[0]):
        tile_of[s] = 0
        row_of[s] = 0
        land_of[s] = hb.shape[0]
    for x in range(QUAD):
        for s in range(group * cap):
            wants[x * group * cap + s] = col_blocks
    for copy in minor:
        copy.wait()
    me = lax.axis_index("rb").astype(I32)
    scale = (1 << 19) // col_blocks + 1

    def place_tile(t, _):
        col = cols[t]
        owner = (col * scale) >> 19
        rank = filled[owner]
        filled[owner] = rank + 1
        apart = owner ^ me
        high, quad = apart // QUAD, apart % QUAD
        place = high * cap + rank
        near = jnp.where(high < half, 1, 0)
        slot = (near * QUAD + quad) * (half * cap) + place - (1 - near) * (half * cap)
        tile_of[slot] = t
        row_of[slot] = rows[t]
        land_of[slot] = rows[t]
        wants[quad * (group * cap) + place] = col - owner * col_blocks
        return 0

    lax.fori_loop(0, count[0], place_tile, 0)
    dy[...] = dual_mask[...].astype(F32) * cot_y[...]

    def h_into(at, h):
        rhs[:, at] = -h

    scaled_blocks(side, dy, dual_step, hb, h_into)
    for c in range(chunks):
        tile_copy(c).wait()
    transpose_products(0, tile_of, row_of, held, hb, (o0, o1, o2, o3))


def turn_kernel(held, turned):
    def one_chunk(c, _):
        for j in range(CHUNK):
            turned[c * CHUNK + j] = held[c * CHUNK + j].T
        return 0

    lax.fori_loop(0, held.shape[0] // CHUNK, one_chunk, 0)


def near_product_kernel(tile_of, row_of, held, hb, o0, o1, o2, o3):
    transpose_products(tile_of.shape[0] // 2, tile_of, row_of, held, hb, (o0, o1, o2, o3))


def map_kernel(own, got1, got2, got3, wants):
    per = own.shape[0] // QUAD
    for x, got in enumerate((own, got1, got2, got3)):
        for s in range(per):
            wants[x * per + s] = got[x * per + s]


def sum_kernel(first_high, cap, wants, a0, a1, a2, a3, *rest):
    parts = (a0, a1, a2, a3)
    half = a0.shape[0] // cap
    per = wants.shape[0] // QUAD
    outs, totals = rest[:half], rest[half:]
    for total in totals:
        total[...] = jnp.zeros_like(total)
    for r in range(cap):
        for pair in range(QUAD // 2):
            jobs = []
            for h in range(half):
                for side in range(2):
                    x = 2 * pair + side
                    spot = wants[x * per + (first_high + h) * cap + r]
                    jobs.append((totals[2 * h + side], spot, parts[x][h * cap + r].astype(F32)))
            values = [total[spot] + part for total, spot, part in jobs]
            for (total, spot, _), value in zip(jobs, values):
                total[spot] = value
    for h, out in enumerate(outs):
        for c in range(out.shape[0]):
            out[c] = (totals[2 * h][c] + totals[2 * h + 1][c]).astype(out.dtype)


def primal_kernel(step, first, primal_mask, primal_step, x, spent, *refs):
    parts, (new_x, new_spent, out) = refs[:-3], refs[-3:]
    blocks, _, side = out.shape
    for c in range(blocks):
        at = pl.ds(c * side, side)
        u = parts[0][c]
        for part in parts[1:]:
            u = u + part[c].astype(F32)
        dx = primal_mask[step, :, at].astype(F32) * (x[:, at] + 2.0 * u)
        q = primal_step[:, at] * dx
        new_x[:, at] = dx - u
        new_spent[:, at] = -q if first else spent[:, at] - q
        out[c] = q.astype(BF16)


def pick_kernel(first_high, cap, wants, *refs):
    blocks, outs = refs[:-QUAD], refs[-QUAD:]
    per = wants.shape[0] // QUAD
    last = blocks[0].shape[0] - 1
    for x, out in enumerate(outs):
        values = [
            blocks[h][jnp.minimum(wants[x * per + (first_high + h) * cap + r], last)]
            for h in range(len(blocks))
            for r in range(cap)
        ]
        for s, value in enumerate(values):
            out[s] = value


def near_forward_kernel(tile_of, land_of, turned, m0, m1, m2, m3, out, *totals):
    forward_products(tile_of.shape[0] // 2, tile_of, land_of, turned, (m0, m1, m2, m3), totals)
    for r in range(out.shape[0]):
        out[r] = gathered(totals, r)


def middle_kernel(step, tile_of, row_of, land_of, held, turned, dual_step, dual_mask, part, dy, rhs, m0, m1, m2, m3,
                  new_dy, new_rhs, hb, o0, o1, o2, o3, *totals):
    side = held.shape[1]
    forward_products(0, tile_of, land_of, turned, (m0, m1, m2, m3), totals)
    for r in range(hb.shape[0]):
        at = pl.ds(r * side, side)
        v = part[r] + gathered(totals, r)
        new_dy[:, at] = dual_mask[step, :, at].astype(F32) * (dy[:, at] - v)

    def h_into(at, h):
        new_rhs[:, at] = rhs[:, at] - h

    scaled_blocks(side, new_dy, dual_step, hb, h_into)
    transpose_products(0, tile_of, row_of, held, hb, (o0, o1, o2, o3))


def last_kernel(tile_of, land_of, turned, part, dy, m0, m1, m2, m3, new_y, *totals):
    side = turned.shape[1]
    forward_products(0, tile_of, land_of, turned, (m0, m1, m2, m3), totals)
    for r in range(part.shape[0]):
        at = pl.ds(r * side, side)
        new_y[:, at] = dy[:, at] - (part[r] + gathered(totals, r))


def on_device(tiles, tile_rows, tile_cols, tile_counts, dual_step, primal_step, primal_mask, dual_mask, cot_x, cot_y):
    peers = lax.axis_size("rb")
    tile_slots, side, _ = tiles.shape
    batch = cot_x.shape[0]
    row_blocks = dual_step.shape[0] // side
    col_blocks = primal_step.shape[0] // side
    cap = max(2, (tile_slots + peers - 1) // peers)
    group = peers // QUAD
    half = group // 2
    slots = peers * cap
    steps = primal_mask.shape[0]
    dual_step = dual_step.reshape(1, -1)
    primal_step = primal_step.reshape(1, -1)
    y_shape = shape(cot_y.shape, F32)
    x_shape = shape(cot_x.shape, F32)
    part_set = (shape((half * cap, batch, side), BF16),) * QUAD
    block_set = shape((col_blocks, batch, side), BF16)
    hb_set = shape((row_blocks, batch, side), BF16)
    per_slot = pltpu.SMEM((slots,), I32)
    row_totals = [pltpu.VMEM((row_blocks + 1, batch, side), F32)] * LANES
    col_totals = [pltpu.VMEM((col_blocks + 1, batch, side), F32)] * (2 * half)
    tile_bytes = tiles.size * 2

    def call(kernel, name, moved, ins, outs, args, scratch=()):
        return pl.pallas_call(
            kernel,
            out_shape=outs,
            in_specs=ins,
            out_specs=jax.tree.map(lambda _: VM, outs),
            scratch_shapes=scratch,
            compiler_params=PARAMS,
            cost_estimate=cost(moved),
            name=name,
        )(*args)

    def swap(array, x):
        return lax.ppermute(array, "rb", [(p, p ^ x) for p in range(peers)])

    def near_swaps(parts):
        return [parts[0]] + [swap(parts[x], x) for x in range(1, QUAD)]

    step = steps - 1
    held, dy, rhs, hb, tile_of, row_of, land_of, wants, *far_parts = pl.pallas_call(
        functools.partial(start_kernel, step, peers, cap, col_blocks),
        out_shape=(
            pltpu.VMEM(tiles.shape, BF16), y_shape, y_shape, hb_set, per_slot, per_slot, per_slot,
            shape((QUAD * group * cap,), I32),
        ) + part_set,
        in_specs=[SM] + [HBM] * 6,
        out_specs=(VM,) * 4 + (SM,) * 4 + (VM,) * QUAD,
        scratch_shapes=[
            pltpu.SMEM((tile_slots,), I32), pltpu.SMEM((tile_slots,), I32), pltpu.VMEM(dual_step.shape, F32),
            pltpu.VMEM(cot_y.shape, I32), pltpu.VMEM(cot_y.shape, F32), pltpu.SMEM((peers,), I32),
            pltpu.SemaphoreType.DMA((tile_slots // CHUNK,)), pltpu.SemaphoreType.DMA((5,)),
        ],
        compiler_params=PARAMS,
        cost_estimate=cost(2 * tile_bytes),
        name="start",
    )(tile_counts, *(
        pltpu.with_memory_space_constraint(array, pltpu.HBM)
        for array in (tile_rows, tile_cols, tiles, dual_step, dual_mask, cot_y)
    ))
    wants = pl.pallas_call(
        map_kernel,
        out_shape=pltpu.SMEM((slots,), I32),
        in_specs=[SM] * QUAD,
        out_specs=SM,
        compiler_params=PARAMS,
        name="maps",
    )(wants, *(swap(wants, x) for x in range(1, QUAD)))
    turned = call(turn_kernel, "turn", tile_bytes, [VM], pltpu.VMEM(tiles.shape, BF16), (held,))
    x_state, spent = cot_x, cot_x
    while True:
        far_got = near_swaps(far_parts)
        near_parts = call(near_product_kernel, "near_product", tile_bytes // 2, [SM] * 2 + [VM] * 2, part_set,
                          (tile_of, row_of, held, hb))
        near_got = near_swaps(near_parts)
        far_sums = call(functools.partial(sum_kernel, half, cap), "far_sum", 1 << 20, [SM] + [VM] * QUAD,
                        (block_set,) * half, (wants, *far_got), col_totals)
        got = [swap(far_sums[h], (half + h) * QUAD) for h in reversed(range(half))]
        near_sums = call(functools.partial(sum_kernel, 0, cap), "near_sum", 1 << 20, [SM] + [VM] * QUAD,
                         (shape(block_set.shape, F32),) + (block_set,) * (half - 1), (wants, *near_got), col_totals)
        got += [swap(near_sums[h], h * QUAD) for h in range(1, half)]
        if step == steps - 1:
            turned, x_state = lax.optimization_barrier((turned, x_state))
        x_state, spent, moved = call(
            functools.partial(primal_kernel, step, step == steps - 1), "primal", 1 << 20, [VM] * (4 + group),
            (x_shape, x_shape, block_set), (primal_mask, primal_step, x_state, spent, near_sums[0], *got))
        blocks = [moved] + [swap(moved, h * QUAD) for h in range(1, group)]
        near_moved = near_swaps(call(functools.partial(pick_kernel, 0, cap), "near_pick", 1 << 20,
                                     [SM] + [VM] * half, part_set, (wants, *blocks[:half])))
        far_moved = near_swaps(call(functools.partial(pick_kernel, half, cap), "far_pick", 1 << 20,
                                    [SM] + [VM] * half, part_set, (wants, *blocks[half:])))
        part = call(near_forward_kernel, "near_forward", tile_bytes // 2, [SM] * 2 + [VM] * (1 + QUAD),
                    shape(hb_set.shape, F32), (tile_of, land_of, turned, *near_moved), row_totals)
        if step == 0:
            break
        step -= 1
        dy, rhs, hb, *far_parts = call(
            functools.partial(middle_kernel, step), "middle", tile_bytes, [SM] * 3 + [VM] * (7 + QUAD),
            (y_shape, y_shape, hb_set) + part_set,
            (tile_of, row_of, land_of, held, turned, dual_step, dual_mask, part, dy, rhs, *far_moved), row_totals)
    y_state = call(last_kernel, "last", tile_bytes // 2, [SM] * 2 + [VM] * (3 + QUAD), y_shape,
                   (tile_of, land_of, turned, part, dy, *far_moved), row_totals)
    return spent, rhs, x_state, y_state


def solution(mesh):
    rb = ("grp", "rb")
    return jax.shard_map(
        on_device,
        mesh=mesh,
        in_specs=(
            P(rb, None, None), P(rb), P(rb), P(rb), P(rb), P(rb),
            P(None, "grp", "rb"), P(None, "grp", "rb"), P("grp", "rb"), P("grp", "rb"),
        ),
        out_specs=(P("grp", "rb"),) * 4,
        check_vma=False,
    )
```

```python
import functools

import jax
import jax.numpy as jnp
from jax import lax
from jax.experimental import pallas as pl
from jax.experimental.pallas import tpu as pltpu
from jax.sharding import PartitionSpec as P

QUAD = 4
CHUNK = 8
LANES = 4
VM = pl.BlockSpec(memory_space=pltpu.VMEM)
SM = pl.BlockSpec(memory_space=pltpu.SMEM)
HBM = pl.BlockSpec(memory_space=pltpu.HBM)
PARAMS = pltpu.CompilerParams(vmem_limit_bytes=12 * 1024 * 1024)
F32, BF16, I32 = jnp.float32, jnp.bfloat16, jnp.int32


def shape(dims, dtype):
    return jax.ShapeDtypeStruct(dims, dtype)


def cost(moved):
    return pl.CostEstimate(flops=moved * 8, bytes_accessed=moved, transcendentals=0)


def scaled_blocks(side, dy, dual_step, hb, h_into):
    for r in range(hb.shape[0]):
        at = pl.ds(r * side, side)
        h = dual_step[:, at] * dy[:, at]
        hb[r] = h.astype(BF16)
        h_into(at, h)


def transpose_products(base, tile_of, row_of, tiles, hb, outs):
    per = tile_of.shape[0] // (2 * QUAD)
    for x, out in enumerate(outs):
        for s in range(per):
            slot = base + x * per + s
            out[s] = jnp.dot(hb[row_of[slot]], tiles[tile_of[slot]], preferred_element_type=F32).astype(BF16)


def forward_products(base, tile_of, land_of, turned, moved, totals):
    per = moved[0].shape[0]
    for total in totals:
        total[...] = jnp.zeros_like(total)
    for x, part in enumerate(moved):
        first = base + x * per
        terms = [jnp.dot(part[s], turned[tile_of[first + s]], preferred_element_type=F32) for s in range(per)]
        for s in range(0, per, LANES):
            several = range(min(LANES, per - s))
            spots = [land_of[first + s + i] for i in several]
            held = [totals[i][spots[i]] + terms[s + i] for i in several]
            for i in several:
                totals[i][spots[i]] = held[i]


def gathered(totals, r):
    value = totals[0][r]
    for total in totals[1:]:
        value = value + total[r]
    return value


def start_kernel(step, peers, cap, col_blocks, count, rows_in, cols_in, tiles, step_in, mask_in, cot_in,
                 held, dy, rhs, hb, tile_of, row_of, land_of, o0, o1, o2, o3,
                 rows, cols, dual_step, dual_mask, cot_y, filled, sems, small):
    tile_slots, side, _ = tiles.shape
    group = peers // QUAD
    half = group // 2
    chunks = tile_slots // CHUNK
    minor = [
        pltpu.make_async_copy(src, dst, small.at[i])
        for i, (src, dst) in enumerate((
            (cols_in, cols), (rows_in, rows), (step_in, dual_step), (mask_in.at[step], dual_mask), (cot_in, cot_y),
        ))
    ]
    for copy in minor:
        copy.start()

    def tile_copy(c):
        at = pl.ds(c * CHUNK, CHUNK)
        return pltpu.make_async_copy(tiles.at[at], held.at[at], sems.at[c])

    for c in range(chunks):
        tile_copy(c).start()
    for o in range(peers):
        filled[o] = 0
    for s in range(tile_of.shape[0]):
        tile_of[s] = 0
        row_of[s] = 0
        land_of[s] = hb.shape[0]
    for copy in minor:
        copy.wait()
    me = lax.axis_index("rb").astype(I32)
    scale = (1 << 19) // col_blocks + 1

    lane = lax.broadcasted_iota(I32, o0.shape[1:], 1)
    line = lax.broadcasted_iota(I32, o0.shape[1:], 0)

    def place_tile(t, plan):
        col = cols[t]
        owner = (col * scale) >> 19
        rank = filled[owner]
        filled[owner] = rank + 1
        apart = owner ^ me
        high, quad = apart // QUAD, apart % QUAD
        slot = ((1 - high % 2) * QUAD + quad) * (half * cap) + high // 2 * cap + rank
        tile_of[slot] = t
        row_of[slot] = rows[t]
        land_of[slot] = rows[t]
        return jnp.where((line == quad) & (lane == high * cap + rank), col - owner * col_blocks, plan)

    plan = lax.fori_loop(0, count[0], place_tile, jnp.full(o0.shape[1:], col_blocks, I32)).astype(BF16)
    for out in (o0, o1, o2, o3):
        out[half * cap] = plan
    dy[...] = dual_mask[...].astype(F32) * cot_y[...]

    def h_into(at, h):
        rhs[:, at] = -h

    scaled_blocks(side, dy, dual_step, hb, h_into)
    for c in range(chunks):
        tile_copy(c).wait()
    transpose_products(0, tile_of, row_of, held, hb, (o0, o1, o2, o3))


def turn_kernel(held, turned):
    def one_chunk(c, _):
        for j in range(CHUNK):
            turned[c * CHUNK + j] = held[c * CHUNK + j].T
        return 0

    lax.fori_loop(0, held.shape[0] // CHUNK, one_chunk, 0)


def near_product_kernel(tile_of, row_of, held, hb, o0, o1, o2, o3):
    transpose_products(tile_of.shape[0] // 2, tile_of, row_of, held, hb, (o0, o1, o2, o3))


def map_kernel(a0, a1, a2, a3, wants, whole, sem):
    for x, part in enumerate((a0, a1, a2, a3)):
        plan = part[part.shape[0] - 1].astype(F32)
        whole[pl.ds(x, 1)] = plan[x:x + 1].astype(I32)
    whole[pl.ds(QUAD, QUAD)] = jnp.zeros((QUAD, whole.shape[1]), I32)
    copy = pltpu.make_async_copy(whole, wants, sem)
    copy.start()
    copy.wait()


def sum_kernel(highs, cap, wants, a0, a1, a2, a3, *rest):
    parts = (a0, a1, a2, a3)
    count = len(highs)
    totals = rest[len(rest) - 2 * count:]
    outs = rest[len(rest) - 3 * count:len(rest) - 2 * count]
    passed = rest[:len(rest) - 3 * count]
    for total in totals:
        total[...] = jnp.zeros_like(total)
    for r in range(cap):
        for pair in range(QUAD // 2):
            jobs = []
            for h in range(count):
                for side in range(2):
                    x = 2 * pair + side
                    spot = wants[x, highs[h] * cap + r]
                    jobs.append((totals[2 * h + side], spot, parts[x][h * cap + r].astype(F32)))
            values = [total[spot] + part for total, spot, part in jobs]
            for (total, spot, _), value in zip(jobs, values):
                total[spot] = value
    for h, out in enumerate(outs):
        for c in range(out.shape[0]):
            value = totals[2 * h][c] + totals[2 * h + 1][c]
            if passed and h > 0:
                value = value + passed[h - 1][c].astype(F32)
            out[c] = value.astype(out.dtype)


def primal_kernel(step, first, primal_mask, primal_step, x, spent, *refs):
    parts, (new_x, new_spent, out) = refs[:-3], refs[-3:]
    blocks, _, side = out.shape
    for c in range(blocks):
        at = pl.ds(c * side, side)
        u = parts[0][c]
        for part in parts[1:]:
            u = u + part[c].astype(F32)
        dx = primal_mask[step, :, at].astype(F32) * (x[:, at] + 2.0 * u)
        q = primal_step[:, at] * dx
        new_x[:, at] = dx - u
        new_spent[:, at] = -q if first else spent[:, at] - q
        out[c] = q.astype(BF16)


def pick_kernel(highs, cap, wants, *refs):
    blocks, outs = refs[:-QUAD], refs[-QUAD:]
    last = blocks[0].shape[0] - 1
    for x, out in enumerate(outs):
        values = [
            block[jnp.minimum(wants[x, high * cap + r], last)] for high, block in zip(highs, blocks) for r in range(cap)
        ]
        for s, value in enumerate(values):
            out[s] = value


def near_forward_kernel(tile_of, land_of, turned, m0, m1, m2, m3, out, *totals):
    forward_products(tile_of.shape[0] // 2, tile_of, land_of, turned, (m0, m1, m2, m3), totals)
    for r in range(out.shape[0]):
        out[r] = gathered(totals, r)


def middle_kernel(step, tile_of, row_of, land_of, held, turned, dual_step, dual_mask, part, dy, rhs, m0, m1, m2, m3,
                  new_dy, new_rhs, hb, o0, o1, o2, o3, *totals):
    side = held.shape[1]
    forward_products(0, tile_of, land_of, turned, (m0, m1, m2, m3), totals)
    for r in range(hb.shape[0]):
        at = pl.ds(r * side, side)
        v = part[r] + gathered(totals, r)
        new_dy[:, at] = dual_mask[step, :, at].astype(F32) * (dy[:, at] - v)

    def h_into(at, h):
        new_rhs[:, at] = rhs[:, at] - h

    scaled_blocks(side, new_dy, dual_step, hb, h_into)
    transpose_products(0, tile_of, row_of, held, hb, (o0, o1, o2, o3))


def last_kernel(tile_of, land_of, turned, part, dy, m0, m1, m2, m3, new_y, *totals):
    side = turned.shape[1]
    forward_products(0, tile_of, land_of, turned, (m0, m1, m2, m3), totals)
    for r in range(part.shape[0]):
        at = pl.ds(r * side, side)
        new_y[:, at] = dy[:, at] - (part[r] + gathered(totals, r))


def on_device(tiles, tile_rows, tile_cols, tile_counts, dual_step, primal_step, primal_mask, dual_mask, cot_x, cot_y):
    peers = lax.axis_size("rb")
    tile_slots, side, _ = tiles.shape
    batch = cot_x.shape[0]
    row_blocks = dual_step.shape[0] // side
    col_blocks = primal_step.shape[0] // side
    cap = max(2, (tile_slots + peers - 1) // peers)
    group = peers // QUAD
    half = group // 2
    slots = peers * cap
    steps = primal_mask.shape[0]
    dual_step = dual_step.reshape(1, -1)
    primal_step = primal_step.reshape(1, -1)
    y_shape = shape(cot_y.shape, F32)
    x_shape = shape(cot_x.shape, F32)
    part_set = (shape((half * cap, batch, side), BF16),) * QUAD
    block_set = shape((col_blocks, batch, side), BF16)
    hb_set = shape((row_blocks, batch, side), BF16)
    per_slot = pltpu.SMEM((slots,), I32)
    row_totals = [pltpu.VMEM((row_blocks + 1, batch, side), F32)] * LANES
    col_totals = [pltpu.VMEM((col_blocks + 1, batch, side), F32)] * (2 * half)
    tile_bytes = tiles.size * 2

    def call(kernel, name, moved, ins, outs, args, scratch=()):
        return pl.pallas_call(
            kernel,
            out_shape=outs,
            in_specs=ins,
            out_specs=jax.tree.map(lambda _: VM, outs),
            scratch_shapes=scratch,
            compiler_params=PARAMS,
            cost_estimate=cost(moved),
            name=name,
        )(*args)

    def swap(array, x):
        return lax.ppermute(array, "rb", [(p, p ^ x) for p in range(peers)])

    def near_swaps(parts):
        return [parts[0]] + [swap(parts[x], x) for x in range(1, QUAD)]

    step = steps - 1
    held, dy, rhs, hb, tile_of, row_of, land_of, *far_parts = pl.pallas_call(
        functools.partial(start_kernel, step, peers, cap, col_blocks),
        out_shape=(
            pltpu.VMEM(tiles.shape, BF16), y_shape, y_shape, hb_set, per_slot, per_slot, per_slot,
        ) + (shape((half * cap + 1, batch, side), BF16),) * QUAD,
        in_specs=[SM] + [HBM] * 6,
        out_specs=(VM,) * 4 + (SM,) * 3 + (VM,) * QUAD,
        scratch_shapes=[
            pltpu.SMEM((tile_slots,), I32), pltpu.SMEM((tile_slots,), I32), pltpu.VMEM(dual_step.shape, F32),
            pltpu.VMEM(cot_y.shape, I32), pltpu.VMEM(cot_y.shape, F32), pltpu.SMEM((peers,), I32),
            pltpu.SemaphoreType.DMA((tile_slots // CHUNK,)), pltpu.SemaphoreType.DMA((5,)),
        ],
        compiler_params=PARAMS,
        cost_estimate=cost(2 * tile_bytes),
        name="start",
    )(tile_counts, *(
        pltpu.with_memory_space_constraint(array, pltpu.HBM)
        for array in (tile_rows, tile_cols, tiles, dual_step, dual_mask, cot_y)
    ))
    turned = call(turn_kernel, "turn", tile_bytes, [VM], pltpu.VMEM(tiles.shape, BF16), (held,))
    x_state, spent, wants = cot_x, cot_x, None
    odd, even = tuple(range(1, group, 2)), tuple(range(0, group, 2))
    while True:
        far_got = near_swaps(far_parts)
        near_parts = call(near_product_kernel, "near_product", tile_bytes // 2, [SM] * 2 + [VM] * 2, part_set,
                          (tile_of, row_of, held, hb))
        near_got = near_swaps(near_parts)
        if wants is None:
            wants = pl.pallas_call(
                map_kernel,
                out_shape=pltpu.SMEM((2 * QUAD, side), I32),
                in_specs=[VM] * QUAD,
                out_specs=SM,
                scratch_shapes=[pltpu.VMEM((2 * QUAD, side), I32), pltpu.SemaphoreType.DMA],
                compiler_params=PARAMS,
                name="maps",
            )(*far_got)
        far_sums = call(functools.partial(sum_kernel, odd, cap), "odd_sum", 1 << 20, [SM] + [VM] * QUAD,
                        (block_set,) * half, (wants, *far_got), col_totals)
        passed = [swap(far_sums[j], QUAD) for j in range(1, half)]
        beside = swap(far_sums[0], QUAD)
        near_sums = call(functools.partial(sum_kernel, even, cap), "even_sum", 1 << 20, [SM] + [VM] * (QUAD + half - 1),
                         (shape(block_set.shape, F32),) + (block_set,) * (half - 1), (wants, *near_got, *passed),
                         col_totals)
        got = [beside] + [swap(near_sums[j], 2 * j * QUAD) for j in range(1, half)]
        if step == steps - 1:
            turned, x_state = lax.optimization_barrier((turned, x_state))
        x_state, spent, moved = call(
            functools.partial(primal_kernel, step, step == steps - 1), "primal", 1 << 20, [VM] * (5 + half),
            (x_shape, x_shape, block_set), (primal_mask, primal_step, x_state, spent, near_sums[0], *got))
        blocks = [moved] + [swap(moved, 2 * j * QUAD) for j in range(1, half)]
        beside = [swap(block, QUAD) for block in blocks]
        near_moved = near_swaps(call(functools.partial(pick_kernel, even, cap), "even_pick", 1 << 20,
                                     [SM] + [VM] * half, part_set, (wants, *blocks)))
        far_moved = near_swaps(call(functools.partial(pick_kernel, odd, cap), "odd_pick", 1 << 20,
                                    [SM] + [VM] * half, part_set, (wants, *beside)))
        part = call(near_forward_kernel, "near_forward", tile_bytes // 2, [SM] * 2 + [VM] * (1 + QUAD),
                    shape(hb_set.shape, F32), (tile_of, land_of, turned, *near_moved), row_totals)
        if step == 0:
            break
        step -= 1
        dy, rhs, hb, *far_parts = call(
            functools.partial(middle_kernel, step), "middle", tile_bytes, [SM] * 3 + [VM] * (7 + QUAD),
            (y_shape, y_shape, hb_set) + part_set,
            (tile_of, row_of, land_of, held, turned, dual_step, dual_mask, part, dy, rhs, *far_moved), row_totals)
    y_state = call(last_kernel, "last", tile_bytes // 2, [SM] * 2 + [VM] * (3 + QUAD), y_shape,
                   (tile_of, land_of, turned, part, dy, *far_moved), row_totals)
    return spent, rhs, x_state, y_state


def solution(mesh):
    rb = ("grp", "rb")
    return jax.shard_map(
        on_device,
        mesh=mesh,
        in_specs=(
            P(rb, None, None), P(rb), P(rb), P(rb), P(rb), P(rb),
            P(None, "grp", "rb"), P(None, "grp", "rb"), P("grp", "rb"), P("grp", "rb"),
        ),
        out_specs=(P("grp", "rb"),) * 4,
        check_vma=False,
    )
```

```python
import functools

import jax
import jax.numpy as jnp
from jax import lax
from jax.experimental import pallas as pl
from jax.experimental.pallas import tpu as pltpu
from jax.sharding import PartitionSpec as P

QUAD = 4
CHUNK = 8
LANES = 4
VM = pl.BlockSpec(memory_space=pltpu.VMEM)
SM = pl.BlockSpec(memory_space=pltpu.SMEM)
HBM = pl.BlockSpec(memory_space=pltpu.HBM)
PARAMS = pltpu.CompilerParams(vmem_limit_bytes=12 * 1024 * 1024)
F32, BF16, I32 = jnp.float32, jnp.bfloat16, jnp.int32


def shape(dims, dtype):
    return jax.ShapeDtypeStruct(dims, dtype)


def cost(moved):
    return pl.CostEstimate(flops=moved * 8, bytes_accessed=moved, transcendentals=0)


def scaled_blocks(side, dy, dual_step, hb, h_into):
    for r in range(hb.shape[0]):
        at = pl.ds(r * side, side)
        h = dual_step[:, at] * dy[:, at]
        hb[r] = h.astype(BF16)
        h_into(at, h)


def transpose_products(base, tile_of, row_of, tiles, hb, outs):
    per = tile_of.shape[0] // (2 * QUAD)
    for x, out in enumerate(outs):
        for s in range(per):
            slot = base + x * per + s
            out[s] = jnp.dot(hb[row_of[slot]], tiles[tile_of[slot]], preferred_element_type=F32).astype(BF16)


def forward_products(base, tile_of, land_of, turned, moved, totals):
    per = moved[0].shape[0]
    for total in totals:
        total[...] = jnp.zeros_like(total)
    for x, part in enumerate(moved):
        first = base + x * (tile_of.shape[0] // (2 * QUAD))
        terms = [jnp.dot(part[s], turned[tile_of[first + s]], preferred_element_type=F32) for s in range(per)]
        for s in range(0, per, LANES):
            several = range(min(LANES, per - s))
            spots = [land_of[first + s + i] for i in several]
            held = [totals[i][spots[i]] + terms[s + i] for i in several]
            for i in several:
                totals[i][spots[i]] = held[i]


def gathered(totals, r):
    value = totals[0][r]
    for total in totals[1:]:
        value = value + total[r]
    return value


def start_kernel(step, peers, cap, col_blocks, count, rows_in, cols_in, tiles, step_in, mask_in, cot_in,
                 held, dy, rhs, hb, tile_of, row_of, land_of, o0, o1, o2, o3,
                 rows, cols, dual_step, dual_mask, cot_y, filled, wants, plan, sems, small):
    tile_slots, side, _ = tiles.shape
    group = peers // QUAD
    half = group // 2
    chunks = tile_slots // CHUNK
    minor = [
        pltpu.make_async_copy(src, dst, small.at[i])
        for i, (src, dst) in enumerate((
            (cols_in, cols), (rows_in, rows), (step_in, dual_step), (mask_in.at[step], dual_mask), (cot_in, cot_y),
        ))
    ]
    for copy in minor:
        copy.start()

    def tile_copy(c):
        at = pl.ds(c * CHUNK, CHUNK)
        return pltpu.make_async_copy(tiles.at[at], held.at[at], sems.at[c])

    for c in range(chunks):
        tile_copy(c).start()
    for o in range(peers):
        filled[o] = 0
    for s in range(tile_of.shape[0]):
        tile_of[s] = 0
        row_of[s] = 0
        land_of[s] = hb.shape[0]
    for x in range(QUAD):
        for s in range(group * cap):
            wants[x, s] = col_blocks
    for copy in minor:
        copy.wait()
    me = lax.axis_index("rb").astype(I32)
    scale = (1 << 19) // col_blocks + 1

    def place_tile(t, _):
        col = cols[t]
        owner = (col * scale) >> 19
        rank = filled[owner]
        filled[owner] = rank + 1
        apart = owner ^ me
        high, quad = apart // QUAD, apart % QUAD
        place = high * cap + rank
        near = jnp.where(high < half, 1, 0)
        slot = (near * QUAD + quad) * (half * cap) + place - (1 - near) * (half * cap)
        tile_of[slot] = t
        row_of[slot] = rows[t]
        land_of[slot] = rows[t]
        wants[quad, place] = col - owner * col_blocks
        return 0

    lax.fori_loop(0, count[0], place_tile, 0)
    chart = pltpu.make_async_copy(wants, plan, small.at[len(minor)])
    chart.start()
    dy[...] = dual_mask[...].astype(F32) * cot_y[...]

    def h_into(at, h):
        rhs[:, at] = -h

    scaled_blocks(side, dy, dual_step, hb, h_into)
    chart.wait()
    for out in (o0, o1, o2, o3):
        out[half * cap] = plan[...].astype(BF16)
    for c in range(chunks):
        tile_copy(c).wait()
    transpose_products(0, tile_of, row_of, held, hb, (o0, o1, o2, o3))


def turn_kernel(held, turned):
    def one_chunk(c, _):
        for j in range(CHUNK):
            turned[c * CHUNK + j] = held[c * CHUNK + j].T
        return 0

    lax.fori_loop(0, held.shape[0] // CHUNK, one_chunk, 0)


def near_product_kernel(tile_of, row_of, held, hb, o0, o1, o2, o3):
    transpose_products(tile_of.shape[0] // 2, tile_of, row_of, held, hb, (o0, o1, o2, o3))


def map_kernel(a0, a1, a2, a3, wants, whole, sem):
    for x, part in enumerate((a0, a1, a2, a3)):
        plan = part[part.shape[0] - 1].astype(F32)
        whole[pl.ds(x, 1)] = plan[x:x + 1].astype(I32)
    whole[pl.ds(QUAD, QUAD)] = jnp.zeros((QUAD, whole.shape[1]), I32)
    copy = pltpu.make_async_copy(whole, wants, sem)
    copy.start()
    copy.wait()


def sum_kernel(first_high, cap, wants, a0, a1, a2, a3, *rest):
    parts = (a0, a1, a2, a3)
    half = len(rest) // 3
    outs, totals = rest[:half], rest[half:]
    for total in totals:
        total[...] = jnp.zeros_like(total)
    for r in range(cap):
        for pair in range(QUAD // 2):
            jobs = []
            for h in range(half):
                for side in range(2):
                    x = 2 * pair + side
                    spot = wants[x, (first_high + h) * cap + r]
                    jobs.append((totals[2 * h + side], spot, parts[x][h * cap + r].astype(F32)))
            values = [total[spot] + part for total, spot, part in jobs]
            for (total, spot, _), value in zip(jobs, values):
                total[spot] = value
    for h, out in enumerate(outs):
        for c in range(out.shape[0]):
            out[c] = (totals[2 * h][c] + totals[2 * h + 1][c]).astype(out.dtype)


def primal_kernel(step, first, primal_mask, primal_step, x, spent, *refs):
    parts, (new_x, new_spent, out) = refs[:-3], refs[-3:]
    blocks, _, side = out.shape
    for c in range(blocks):
        at = pl.ds(c * side, side)
        u = parts[0][c]
        for part in parts[1:]:
            u = u + part[c].astype(F32)
        dx = primal_mask[step, :, at].astype(F32) * (x[:, at] + 2.0 * u)
        q = primal_step[:, at] * dx
        new_x[:, at] = dx - u
        new_spent[:, at] = -q if first else spent[:, at] - q
        out[c] = q.astype(BF16)


def pick_kernel(first_high, cap, wants, *refs):
    blocks, outs = refs[:-QUAD], refs[-QUAD:]
    last = blocks[0].shape[0] - 1
    for x, out in enumerate(outs):
        values = [
            blocks[h][jnp.minimum(wants[x, (first_high + h) * cap + r], last)]
            for h in range(len(blocks))
            for r in range(cap)
        ]
        for s, value in enumerate(values):
            out[s] = value


def near_forward_kernel(base, tile_of, land_of, turned, m0, m1, m2, m3, *rest):
    out, totals = rest[-LANES - 1], rest[-LANES:]
    forward_products(base, tile_of, land_of, turned, (m0, m1, m2, m3), totals)
    for r in range(out.shape[0]):
        value = gathered(totals, r)
        out[r] = value + rest[0][r] if len(rest) > LANES + 1 else value


def middle_kernel(step, base, tile_of, row_of, land_of, held, turned, dual_step, dual_mask, part, dy, rhs, m0, m1, m2, m3,
                  new_dy, new_rhs, hb, o0, o1, o2, o3, *totals):
    side = held.shape[1]
    forward_products(base, tile_of, land_of, turned, (m0, m1, m2, m3), totals)
    for r in range(hb.shape[0]):
        at = pl.ds(r * side, side)
        v = part[r] + gathered(totals, r)
        new_dy[:, at] = dual_mask[step, :, at].astype(F32) * (dy[:, at] - v)

    def h_into(at, h):
        new_rhs[:, at] = rhs[:, at] - h

    scaled_blocks(side, new_dy, dual_step, hb, h_into)
    transpose_products(0, tile_of, row_of, held, hb, (o0, o1, o2, o3))


def last_kernel(base, tile_of, land_of, turned, part, dy, m0, m1, m2, m3, new_y, *totals):
    side = turned.shape[1]
    forward_products(base, tile_of, land_of, turned, (m0, m1, m2, m3), totals)
    for r in range(part.shape[0]):
        at = pl.ds(r * side, side)
        new_y[:, at] = dy[:, at] - (part[r] + gathered(totals, r))


def on_device(tiles, tile_rows, tile_cols, tile_counts, dual_step, primal_step, primal_mask, dual_mask, cot_x, cot_y):
    peers = lax.axis_size("rb")
    tile_slots, side, _ = tiles.shape
    batch = cot_x.shape[0]
    row_blocks = dual_step.shape[0] // side
    col_blocks = primal_step.shape[0] // side
    cap = max(2, (tile_slots + peers - 1) // peers)
    group = peers // QUAD
    half = group // 2
    slots = peers * cap
    steps = primal_mask.shape[0]
    dual_step = dual_step.reshape(1, -1)
    primal_step = primal_step.reshape(1, -1)
    y_shape = shape(cot_y.shape, F32)
    x_shape = shape(cot_x.shape, F32)
    part_set = (shape((half * cap, batch, side), BF16),) * QUAD
    block_set = shape((col_blocks, batch, side), BF16)
    hb_set = shape((row_blocks, batch, side), BF16)
    per_slot = pltpu.SMEM((slots,), I32)
    row_totals = [pltpu.VMEM((row_blocks + 1, batch, side), F32)] * LANES
    col_totals = [pltpu.VMEM((col_blocks + 1, batch, side), F32)] * (2 * half)
    tile_bytes = tiles.size * 2

    def call(kernel, name, moved, ins, outs, args, scratch=()):
        return pl.pallas_call(
            kernel,
            out_shape=outs,
            in_specs=ins,
            out_specs=jax.tree.map(lambda _: VM, outs),
            scratch_shapes=scratch,
            compiler_params=PARAMS,
            cost_estimate=cost(moved),
            name=name,
        )(*args)

    def swap(array, x):
        return lax.ppermute(array, "rb", [(p, p ^ x) for p in range(peers)])

    def near_swaps(parts):
        return [parts[0]] + [swap(parts[x], x) for x in range(1, QUAD)]

    step = steps - 1
    held, dy, rhs, hb, tile_of, row_of, land_of, *far_parts = pl.pallas_call(
        functools.partial(start_kernel, step, peers, cap, col_blocks),
        out_shape=(
            pltpu.VMEM(tiles.shape, BF16), y_shape, y_shape, hb_set, per_slot, per_slot, per_slot,
        ) + (shape((half * cap + 1, batch, side), BF16),) * QUAD,
        in_specs=[SM] + [HBM] * 6,
        out_specs=(VM,) * 4 + (SM,) * 3 + (VM,) * QUAD,
        scratch_shapes=[
            pltpu.SMEM((tile_slots,), I32), pltpu.SMEM((tile_slots,), I32), pltpu.VMEM(dual_step.shape, F32),
            pltpu.VMEM(cot_y.shape, I32), pltpu.VMEM(cot_y.shape, F32), pltpu.SMEM((peers,), I32),
            pltpu.SMEM((2 * QUAD, side), I32), pltpu.VMEM((2 * QUAD, side), I32),
            pltpu.SemaphoreType.DMA((tile_slots // CHUNK,)), pltpu.SemaphoreType.DMA((6,)),
        ],
        compiler_params=PARAMS,
        cost_estimate=cost(2 * tile_bytes),
        name="start",
    )(tile_counts, *(
        pltpu.with_memory_space_constraint(array, pltpu.HBM)
        for array in (tile_rows, tile_cols, tiles, dual_step, dual_mask, cot_y)
    ))
    turned = call(turn_kernel, "turn", tile_bytes, [VM], pltpu.VMEM(tiles.shape, BF16), (held,))
    x_state, spent, wants = cot_x, cot_x, None
    middle_high = half + half // 2
    late = half // 2 * cap
    while True:
        far_got = near_swaps(far_parts)
        near_parts = call(near_product_kernel, "near_product", tile_bytes // 2, [SM] * 2 + [VM] * 2, part_set,
                          (tile_of, row_of, held, hb))
        near_got = near_swaps(near_parts)
        if wants is None:
            wants = pl.pallas_call(
                map_kernel,
                out_shape=pltpu.SMEM((2 * QUAD, side), I32),
                in_specs=[VM] * QUAD,
                out_specs=SM,
                scratch_shapes=[pltpu.VMEM((2 * QUAD, side), I32), pltpu.SemaphoreType.DMA],
                compiler_params=PARAMS,
                name="maps",
            )(*far_got)
        far_sums = call(functools.partial(sum_kernel, half, cap), "far_sum", 1 << 20, [SM] + [VM] * QUAD,
                        (block_set,) * half, (wants, *far_got), col_totals)
        got = [swap(far_sums[h], (half + h) * QUAD) for h in reversed(range(half))]
        near_sums = call(functools.partial(sum_kernel, 0, cap), "near_sum", 1 << 20, [SM] + [VM] * QUAD,
                         (shape(block_set.shape, F32),) + (block_set,) * (half - 1), (wants, *near_got), col_totals)
        got += [swap(near_sums[h], h * QUAD) for h in range(1, half)]
        if step == steps - 1:
            turned, x_state = lax.optimization_barrier((turned, x_state))
        x_state, spent, moved = call(
            functools.partial(primal_kernel, step, step == steps - 1), "primal", 1 << 20, [VM] * (4 + group),
            (x_shape, x_shape, block_set), (primal_mask, primal_step, x_state, spent, near_sums[0], *got))
        blocks = [moved] + [swap(moved, h * QUAD) for h in range(1, group)]
        near_moved = near_swaps(call(functools.partial(pick_kernel, 0, cap), "near_pick", 1 << 20,
                                     [SM] + [VM] * half, part_set, (wants, *blocks[:half])))
        early_moved, late_moved = (
            near_swaps(call(functools.partial(pick_kernel, low, cap), name, 1 << 20, [SM] + [VM] * (top - low),
                            (shape(((top - low) * cap, batch, side), BF16),) * QUAD, (wants, *blocks[low:top])))
            for name, low, top in (("early_pick", half, middle_high), ("late_pick", middle_high, group))
        )
        part = call(functools.partial(near_forward_kernel, slots // 2), "near_forward", tile_bytes // 2,
                    [SM] * 2 + [VM] * (1 + QUAD), shape(hb_set.shape, F32), (tile_of, land_of, turned, *near_moved),
                    row_totals)
        part = call(functools.partial(near_forward_kernel, 0), "early_forward", tile_bytes // 4,
                    [SM] * 2 + [VM] * (2 + QUAD), shape(hb_set.shape, F32),
                    (tile_of, land_of, turned, *early_moved, part), row_totals)
        if step == 0:
            break
        step -= 1
        dy, rhs, hb, *far_parts = call(
            functools.partial(middle_kernel, step, late), "middle", tile_bytes, [SM] * 3 + [VM] * (7 + QUAD),
            (y_shape, y_shape, hb_set) + part_set,
            (tile_of, row_of, land_of, held, turned, dual_step, dual_mask, part, dy, rhs, *late_moved), row_totals)
    y_state = call(functools.partial(last_kernel, late), "last", tile_bytes // 2, [SM] * 2 + [VM] * (3 + QUAD), y_shape,
                   (tile_of, land_of, turned, part, dy, *late_moved), row_totals)
    return spent, rhs, x_state, y_state


def solution(mesh):
    rb = ("grp", "rb")
    return jax.shard_map(
        on_device,
        mesh=mesh,
        in_specs=(
            P(rb, None, None), P(rb), P(rb), P(rb), P(rb), P(rb),
            P(None, "grp", "rb"), P(None, "grp", "rb"), P("grp", "rb"), P("grp", "rb"),
        ),
        out_specs=(P("grp", "rb"),) * 4,
        check_vma=False,
    )
```

```python
import functools

import jax
import jax.numpy as jnp
from jax import lax
from jax.experimental import pallas as pl
from jax.experimental.pallas import tpu as pltpu
from jax.sharding import PartitionSpec as P

QUAD = 4
CHUNK = 8
LANES = 4
VM = pl.BlockSpec(memory_space=pltpu.VMEM)
SM = pl.BlockSpec(memory_space=pltpu.SMEM)
HBM = pl.BlockSpec(memory_space=pltpu.HBM)
PARAMS = pltpu.CompilerParams(vmem_limit_bytes=12 * 1024 * 1024)
F32, BF16, I32 = jnp.float32, jnp.bfloat16, jnp.int32


def shape(dims, dtype):
    return jax.ShapeDtypeStruct(dims, dtype)


def cost(moved):
    return pl.CostEstimate(flops=moved * 8, bytes_accessed=moved, transcendentals=0)


def scaled_blocks(side, dy, dual_step, hb, h_into):
    for r in range(hb.shape[0]):
        at = pl.ds(r * side, side)
        h = dual_step[:, at] * dy[:, at]
        hb[r] = h.astype(BF16)
        h_into(at, h)


def transpose_products(base, tile_of, row_of, tiles, hb, outs, xs=range(QUAD)):
    per = tile_of.shape[0] // (2 * QUAD)
    for x, out in zip(xs, outs):
        for s in range(per):
            slot = base + x * per + s
            out[s] = jnp.dot(hb[row_of[slot]], tiles[tile_of[slot]], preferred_element_type=F32).astype(BF16)


def forward_products(base, tile_of, land_of, turned, moved, totals, xs=range(QUAD)):
    per = tile_of.shape[0] // (2 * QUAD)
    for total in totals:
        total[...] = jnp.zeros_like(total)
    for x, part in zip(xs, moved):
        first = base + x * per
        terms = [jnp.dot(part[s], turned[tile_of[first + s]], preferred_element_type=F32) for s in range(per)]
        for s in range(0, per, LANES):
            several = range(min(LANES, per - s))
            spots = [land_of[first + s + i] for i in several]
            held = [totals[i][spots[i]] + terms[s + i] for i in several]
            for i in several:
                totals[i][spots[i]] = held[i]


def gathered(totals, r):
    value = totals[0][r]
    for total in totals[1:]:
        value = value + total[r]
    return value


def start_kernel(step, peers, cap, col_blocks, count, rows_in, cols_in, tiles, step_in, mask_in, cot_in,
                 held, dy, rhs, hb, tile_of, row_of, land_of, o0, o1, o2, o3,
                 rows, cols, dual_step, dual_mask, cot_y, filled, wants, plan, sems, small):
    tile_slots, side, _ = tiles.shape
    group = peers // QUAD
    half = group // 2
    chunks = tile_slots // CHUNK
    minor = [
        pltpu.make_async_copy(src, dst, small.at[i])
        for i, (src, dst) in enumerate((
            (cols_in, cols), (rows_in, rows), (step_in, dual_step), (mask_in.at[step], dual_mask), (cot_in, cot_y),
        ))
    ]
    for copy in minor:
        copy.start()

    def tile_copy(c):
        at = pl.ds(c * CHUNK, CHUNK)
        return pltpu.make_async_copy(tiles.at[at], held.at[at], sems.at[c])

    for c in range(chunks):
        tile_copy(c).start()
    for o in range(peers):
        filled[o] = 0
    for s in range(tile_of.shape[0]):
        tile_of[s] = 0
        row_of[s] = 0
        land_of[s] = hb.shape[0]
    for x in range(QUAD):
        for s in range(group * cap):
            wants[x, s] = col_blocks
    for copy in minor:
        copy.wait()
    me = lax.axis_index("rb").astype(I32)
    scale = (1 << 19) // col_blocks + 1

    def place_tile(t, _):
        col = cols[t]
        owner = (col * scale) >> 19
        rank = filled[owner]
        filled[owner] = rank + 1
        apart = owner ^ me
        high, quad = apart // QUAD, apart % QUAD
        place = high * cap + rank
        near = jnp.where(high < half, 1, 0)
        slot = (near * QUAD + quad) * (half * cap) + place - (1 - near) * (half * cap)
        tile_of[slot] = t
        row_of[slot] = rows[t]
        land_of[slot] = rows[t]
        wants[quad, place] = col - owner * col_blocks
        return 0

    lax.fori_loop(0, count[0], place_tile, 0)
    chart = pltpu.make_async_copy(wants, plan, small.at[len(minor)])
    chart.start()
    dy[...] = dual_mask[...].astype(F32) * cot_y[...]

    def h_into(at, h):
        rhs[:, at] = -h

    scaled_blocks(side, dy, dual_step, hb, h_into)
    chart.wait()
    for out in (o0, o1, o2, o3):
        out[half * cap] = plan[...].astype(BF16)
    for c in range(chunks):
        tile_copy(c).wait()
    transpose_products(0, tile_of, row_of, held, hb, (o0, o1, o2, o3))


def turn_kernel(held, turned):
    def one_chunk(c, _):
        for j in range(CHUNK):
            turned[c * CHUNK + j] = held[c * CHUNK + j].T
        return 0

    lax.fori_loop(0, held.shape[0] // CHUNK, one_chunk, 0)


def near_product_kernel(tile_of, row_of, held, hb, o0, o1, o2, o3):
    transpose_products(tile_of.shape[0] // 2, tile_of, row_of, held, hb, (o0, o1, o2, o3))


def map_kernel(a0, a1, a2, a3, wants, whole, sem):
    for x, part in enumerate((a0, a1, a2, a3)):
        plan = part[part.shape[0] - 1].astype(F32)
        whole[pl.ds(x, 1)] = plan[x:x + 1].astype(I32)
    whole[pl.ds(QUAD, QUAD)] = jnp.zeros((QUAD, whole.shape[1]), I32)
    copy = pltpu.make_async_copy(whole, wants, sem)
    copy.start()
    copy.wait()


def sum_kernel(first_high, cap, wants, a0, a1, a2, a3, *rest):
    parts = (a0, a1, a2, a3)
    half = len(rest) // 3
    outs, totals = rest[:half], rest[half:]
    for total in totals:
        total[...] = jnp.zeros_like(total)
    for r in range(cap):
        for pair in range(QUAD // 2):
            jobs = []
            for h in range(half):
                for side in range(2):
                    x = 2 * pair + side
                    spot = wants[x, (first_high + h) * cap + r]
                    jobs.append((totals[2 * h + side], spot, parts[x][h * cap + r].astype(F32)))
            values = [total[spot] + part for total, spot, part in jobs]
            for (total, spot, _), value in zip(jobs, values):
                total[spot] = value
    for h, out in enumerate(outs):
        for c in range(out.shape[0]):
            out[c] = (totals[2 * h][c] + totals[2 * h + 1][c]).astype(out.dtype)


def primal_kernel(step, first, primal_mask, primal_step, x, spent, *refs):
    parts, (new_x, new_spent, out) = refs[:-3], refs[-3:]
    blocks, _, side = out.shape
    for c in range(blocks):
        at = pl.ds(c * side, side)
        u = parts[0][c]
        for part in parts[1:]:
            u = u + part[c].astype(F32)
        dx = primal_mask[step, :, at].astype(F32) * (x[:, at] + 2.0 * u)
        q = primal_step[:, at] * dx
        new_x[:, at] = dx - u
        new_spent[:, at] = -q if first else spent[:, at] - q
        out[c] = q.astype(BF16)


def pick_kernel(highs, cap, wants, *refs):
    blocks, outs = dict(zip(highs, refs[:-QUAD])), refs[-QUAD:]
    last = refs[0].shape[0] - 1
    for x, out in enumerate(outs):
        values = [blocks[h][jnp.minimum(wants[x, h * cap + r], last)] for h in sorted(highs) for r in range(cap)]
        for s, value in enumerate(values):
            out[s] = value


def near_forward_kernel(tile_of, land_of, turned, m0, m1, m2, m3, out, *totals):
    forward_products(tile_of.shape[0] // 2, tile_of, land_of, turned, (m0, m1, m2, m3), totals)
    for r in range(out.shape[0]):
        out[r] = gathered(totals, r)


def chip_forward_kernel(tile_of, land_of, turned, part, m0, m1, out, *totals):
    forward_products(0, tile_of, land_of, turned, (m0, m1), totals, (0, 1))
    for r in range(out.shape[0]):
        out[r] = part[r] + gathered(totals, r)


def rest_product_kernel(tile_of, row_of, held, hb, o0, o1, o3):
    transpose_products(0, tile_of, row_of, held, hb, (o3, o1, o0), (3, 1, 0))


def middle_kernel(step, tile_of, row_of, land_of, held, turned, dual_step, dual_mask, part, dy, rhs, m2, m3,
                  new_dy, new_rhs, hb, o2, *totals):
    side = held.shape[1]
    forward_products(0, tile_of, land_of, turned, (m2, m3), totals, (2, 3))
    for r in range(hb.shape[0]):
        at = pl.ds(r * side, side)
        v = part[r] + gathered(totals, r)
        new_dy[:, at] = dual_mask[step, :, at].astype(F32) * (dy[:, at] - v)

    def h_into(at, h):
        new_rhs[:, at] = rhs[:, at] - h

    scaled_blocks(side, new_dy, dual_step, hb, h_into)
    transpose_products(0, tile_of, row_of, held, hb, (o2,), (2,))


def last_kernel(tile_of, land_of, turned, part, dy, m2, m3, new_y, *totals):
    side = turned.shape[1]
    forward_products(0, tile_of, land_of, turned, (m2, m3), totals, (2, 3))
    for r in range(part.shape[0]):
        at = pl.ds(r * side, side)
        new_y[:, at] = dy[:, at] - (part[r] + gathered(totals, r))


def on_device(tiles, tile_rows, tile_cols, tile_counts, dual_step, primal_step, primal_mask, dual_mask, cot_x, cot_y):
    peers = lax.axis_size("rb")
    tile_slots, side, _ = tiles.shape
    batch = cot_x.shape[0]
    row_blocks = dual_step.shape[0] // side
    col_blocks = primal_step.shape[0] // side
    cap = max(2, (tile_slots + peers - 1) // peers)
    group = peers // QUAD
    half = group // 2
    slots = peers * cap
    steps = primal_mask.shape[0]
    dual_step = dual_step.reshape(1, -1)
    primal_step = primal_step.reshape(1, -1)
    y_shape = shape(cot_y.shape, F32)
    x_shape = shape(cot_x.shape, F32)
    part_set = (shape((half * cap, batch, side), BF16),) * QUAD
    block_set = shape((col_blocks, batch, side), BF16)
    hb_set = shape((row_blocks, batch, side), BF16)
    per_slot = pltpu.SMEM((slots,), I32)
    row_totals = [pltpu.VMEM((row_blocks + 1, batch, side), F32)] * LANES
    col_totals = [pltpu.VMEM((col_blocks + 1, batch, side), F32)] * (2 * half)
    tile_bytes = tiles.size * 2

    def call(kernel, name, moved, ins, outs, args, scratch=()):
        return pl.pallas_call(
            kernel,
            out_shape=outs,
            in_specs=ins,
            out_specs=jax.tree.map(lambda _: VM, outs),
            scratch_shapes=scratch,
            compiler_params=PARAMS,
            cost_estimate=cost(moved),
            name=name,
        )(*args)

    def swap(array, x):
        return lax.ppermute(array, "rb", [(p, p ^ x) for p in range(peers)])

    def near_swaps(parts):
        return [parts[0]] + [swap(parts[x], x) for x in range(1, QUAD)]

    step = steps - 1
    held, dy, rhs, hb, tile_of, row_of, land_of, *far_parts = pl.pallas_call(
        functools.partial(start_kernel, step, peers, cap, col_blocks),
        out_shape=(
            pltpu.VMEM(tiles.shape, BF16), y_shape, y_shape, hb_set, per_slot, per_slot, per_slot,
        ) + (shape((half * cap + 1, batch, side), BF16),) * QUAD,
        in_specs=[SM] + [HBM] * 6,
        out_specs=(VM,) * 4 + (SM,) * 3 + (VM,) * QUAD,
        scratch_shapes=[
            pltpu.SMEM((tile_slots,), I32), pltpu.SMEM((tile_slots,), I32), pltpu.VMEM(dual_step.shape, F32),
            pltpu.VMEM(cot_y.shape, I32), pltpu.VMEM(cot_y.shape, F32), pltpu.SMEM((peers,), I32),
            pltpu.SMEM((2 * QUAD, side), I32), pltpu.VMEM((2 * QUAD, side), I32),
            pltpu.SemaphoreType.DMA((tile_slots // CHUNK,)), pltpu.SemaphoreType.DMA((6,)),
        ],
        compiler_params=PARAMS,
        cost_estimate=cost(2 * tile_bytes),
        name="start",
    )(tile_counts, *(
        pltpu.with_memory_space_constraint(array, pltpu.HBM)
        for array in (tile_rows, tile_cols, tiles, dual_step, dual_mask, cot_y)
    ))
    turned = call(turn_kernel, "turn", tile_bytes, [VM], pltpu.VMEM(tiles.shape, BF16), (held,))
    x_state, spent, wants = cot_x, cot_x, None
    near_highs, far_highs = tuple(range(half)), tuple(reversed(range(half, group)))
    while True:
        far_got = near_swaps(far_parts)
        near_parts = call(near_product_kernel, "near_product", tile_bytes // 2, [SM] * 2 + [VM] * 2, part_set,
                          (tile_of, row_of, held, hb))
        near_got = near_swaps(near_parts)
        if wants is None:
            wants = pl.pallas_call(
                map_kernel,
                out_shape=pltpu.SMEM((2 * QUAD, side), I32),
                in_specs=[VM] * QUAD,
                out_specs=SM,
                scratch_shapes=[pltpu.VMEM((2 * QUAD, side), I32), pltpu.SemaphoreType.DMA],
                compiler_params=PARAMS,
                name="maps",
            )(*far_got)
        far_sums = call(functools.partial(sum_kernel, half, cap), "far_sum", 1 << 20, [SM] + [VM] * QUAD,
                        (block_set,) * half, (wants, *far_got), col_totals)
        got = [swap(far_sums[h], (half + h) * QUAD) for h in reversed(range(half))]
        near_sums = call(functools.partial(sum_kernel, 0, cap), "near_sum", 1 << 20, [SM] + [VM] * QUAD,
                         (shape(block_set.shape, F32),) + (block_set,) * (half - 1), (wants, *near_got), col_totals)
        got += [swap(near_sums[h], h * QUAD) for h in range(1, half)]
        if step == steps - 1:
            turned, x_state = lax.optimization_barrier((turned, x_state))
        x_state, spent, moved = call(
            functools.partial(primal_kernel, step, step == steps - 1), "primal", 1 << 20, [VM] * (4 + group),
            (x_shape, x_shape, block_set), (primal_mask, primal_step, x_state, spent, near_sums[0], *got))
        blocks = [moved] + [swap(moved, h * QUAD) for h in range(1, group)]
        near_moved, far_moved = (
            near_swaps(call(functools.partial(pick_kernel, highs, cap), name, 1 << 20, [SM] + [VM] * half, part_set,
                            (wants, *(blocks[h] for h in highs))))
            for name, highs in (("near_pick", near_highs), ("far_pick", far_highs))
        )
        part = call(near_forward_kernel, "near_forward", tile_bytes // 2, [SM] * 2 + [VM] * (1 + QUAD),
                    shape(hb_set.shape, F32), (tile_of, land_of, turned, *near_moved), row_totals)
        part = call(chip_forward_kernel, "chip_forward", tile_bytes // 4, [SM] * 2 + [VM] * 4,
                    shape(hb_set.shape, F32), (tile_of, land_of, turned, part, *far_moved[:2]), row_totals)
        if step == 0:
            break
        step -= 1
        dy, rhs, hb, across = call(
            functools.partial(middle_kernel, step), "middle", tile_bytes // 2, [SM] * 3 + [VM] * 9,
            (y_shape, y_shape, hb_set, part_set[0]),
            (tile_of, row_of, land_of, held, turned, dual_step, dual_mask, part, dy, rhs, *far_moved[2:]), row_totals)
        own, beside, aslant = call(rest_product_kernel, "rest_product", tile_bytes // 4, [SM] * 2 + [VM] * 2,
                                   part_set[:3], (tile_of, row_of, held, hb))
        far_parts = [own, beside, across, aslant]
    y_state = call(last_kernel, "last", tile_bytes // 4, [SM] * 2 + [VM] * 5, y_shape,
                   (tile_of, land_of, turned, part, dy, *far_moved[2:]), row_totals)
    return spent, rhs, x_state, y_state


def solution(mesh):
    rb = ("grp", "rb")
    return jax.shard_map(
        on_device,
        mesh=mesh,
        in_specs=(
            P(rb, None, None), P(rb), P(rb), P(rb), P(rb), P(rb),
            P(None, "grp", "rb"), P(None, "grp", "rb"), P("grp", "rb"), P("grp", "rb"),
        ),
        out_specs=(P("grp", "rb"),) * 4,
        check_vma=False,
    )
```

```python
import functools

import jax
import jax.numpy as jnp
from jax import lax
from jax.experimental import pallas as pl
from jax.experimental.pallas import tpu as pltpu
from jax.sharding import PartitionSpec as P

QUAD = 4
CHUNK = 8
LANES = 4
VM = pl.BlockSpec(memory_space=pltpu.VMEM)
SM = pl.BlockSpec(memory_space=pltpu.SMEM)
HBM = pl.BlockSpec(memory_space=pltpu.HBM)
PARAMS = pltpu.CompilerParams(vmem_limit_bytes=12 * 1024 * 1024)
F32, BF16, I32 = jnp.float32, jnp.bfloat16, jnp.int32


def shape(dims, dtype):
    return jax.ShapeDtypeStruct(dims, dtype)


def cost(moved):
    return pl.CostEstimate(flops=moved * 8, bytes_accessed=moved, transcendentals=0)


def scaled_blocks(side, dy, dual_step, hb, h_into):
    for r in range(hb.shape[0]):
        at = pl.ds(r * side, side)
        h = dual_step[:, at] * dy[:, at]
        hb[r] = h.astype(BF16)
        h_into(at, h)


def transpose_products(base, tile_of, row_of, tiles, hb, outs, xs=range(QUAD)):
    per = tile_of.shape[0] // (2 * QUAD)
    for x, out in zip(xs, outs):
        for s in range(per):
            slot = base + x * per + s
            out[s] = jnp.dot(hb[row_of[slot]], tiles[tile_of[slot]], preferred_element_type=F32).astype(BF16)


def forward_products(base, tile_of, land_of, turned, moved, totals, xs=range(QUAD)):
    per = tile_of.shape[0] // (2 * QUAD)
    for total in totals:
        total[...] = jnp.zeros_like(total)
    for x, part in zip(xs, moved):
        first = base + x * per
        terms = [jnp.dot(part[s], turned[tile_of[first + s]], preferred_element_type=F32) for s in range(per)]
        for s in range(0, per, LANES):
            several = range(min(LANES, per - s))
            spots = [land_of[first + s + i] for i in several]
            held = [totals[i][spots[i]] + terms[s + i] for i in several]
            for i in several:
                totals[i][spots[i]] = held[i]


def gathered(totals, r):
    value = totals[0][r]
    for total in totals[1:]:
        value = value + total[r]
    return value


def start_kernel(step, peers, cap, col_blocks, count, rows_in, cols_in, tiles, step_in, mask_in, cot_in,
                 held, dy, rhs, hb, tile_of, row_of, land_of, o0, o1, o2, o3,
                 rows, cols, dual_step, dual_mask, cot_y, filled, wants, plan, sems, small):
    tile_slots, side, _ = tiles.shape
    group = peers // QUAD
    half = group // 2
    chunks = tile_slots // CHUNK
    minor = [
        pltpu.make_async_copy(src, dst, small.at[i])
        for i, (src, dst) in enumerate((
            (cols_in, cols), (rows_in, rows), (step_in, dual_step), (mask_in.at[step], dual_mask), (cot_in, cot_y),
        ))
    ]
    for copy in minor:
        copy.start()

    def tile_copy(c):
        at = pl.ds(c * CHUNK, CHUNK)
        return pltpu.make_async_copy(tiles.at[at], held.at[at], sems.at[c])

    for c in range(chunks):
        tile_copy(c).start()
    for o in range(peers):
        filled[o] = 0
    for s in range(tile_of.shape[0]):
        tile_of[s] = 0
        row_of[s] = 0
        land_of[s] = hb.shape[0]
    for x in range(QUAD):
        for s in range(group * cap):
            wants[x, s] = col_blocks
    for copy in minor:
        copy.wait()
    me = lax.axis_index("rb").astype(I32)
    scale = (1 << 19) // col_blocks + 1

    def place_tile(t, _):
        col = cols[t]
        owner = (col * scale) >> 19
        rank = filled[owner]
        filled[owner] = rank + 1
        apart = owner ^ me
        high, quad = apart // QUAD, apart % QUAD
        place = high * cap + rank
        near = jnp.where(high < half, 1, 0)
        slot = (near * QUAD + quad) * (half * cap) + place - (1 - near) * (half * cap)
        tile_of[slot] = t
        row_of[slot] = rows[t]
        land_of[slot] = rows[t]
        wants[quad, place] = col - owner * col_blocks
        return 0

    lax.fori_loop(0, count[0], place_tile, 0)
    chart = pltpu.make_async_copy(wants, plan, small.at[len(minor)])
    chart.start()
    dy[...] = dual_mask[...].astype(F32) * cot_y[...]

    def h_into(at, h):
        rhs[:, at] = -h

    scaled_blocks(side, dy, dual_step, hb, h_into)
    chart.wait()
    for out in (o0, o1, o2, o3):
        out[half * cap, :, pl.ds(0, plan.shape[1])] = plan[...].astype(BF16)
    for c in range(chunks):
        tile_copy(c).wait()
    transpose_products(0, tile_of, row_of, held, hb, (o0, o1, o2, o3))


def turn_kernel(held, turned):
    def one_chunk(c, _):
        for j in range(CHUNK):
            turned[c * CHUNK + j] = held[c * CHUNK + j].T
        return 0

    lax.fori_loop(0, held.shape[0] // CHUNK, one_chunk, 0)


def near_product_kernel(tile_of, row_of, held, hb, o0, o1, o2, o3):
    transpose_products(tile_of.shape[0] // 2, tile_of, row_of, held, hb, (o0, o1, o2, o3))


def map_kernel(a0, a1, a2, a3, wants, whole, sem):
    for x, part in enumerate((a0, a1, a2, a3)):
        plan = part[part.shape[0] - 1].astype(F32)
        whole[pl.ds(x, 1)] = plan[x:x + 1, :whole.shape[1]].astype(I32)
    whole[pl.ds(QUAD, QUAD)] = jnp.zeros((QUAD, whole.shape[1]), I32)
    copy = pltpu.make_async_copy(whole, wants, sem)
    copy.start()
    copy.wait()


def sum_kernel(first_high, cap, wants, a0, a1, a2, a3, *rest):
    parts = (a0, a1, a2, a3)
    half = len(rest) // 3
    outs, totals = rest[:half], rest[half:]
    for total in totals:
        total[...] = jnp.zeros_like(total)
    for r in range(cap):
        for pair in range(QUAD // 2):
            jobs = []
            for h in range(half):
                for side in range(2):
                    x = 2 * pair + side
                    spot = wants[x, (first_high + h) * cap + r]
                    jobs.append((totals[2 * h + side], spot, parts[x][h * cap + r].astype(F32)))
            values = [total[spot] + part for total, spot, part in jobs]
            for (total, spot, _), value in zip(jobs, values):
                total[spot] = value
    for h, out in enumerate(outs):
        for c in range(out.shape[0]):
            out[c] = (totals[2 * h][c] + totals[2 * h + 1][c]).astype(out.dtype)


def primal_kernel(step, first, primal_mask, primal_step, x, spent, *refs):
    parts, (new_x, new_spent, out) = refs[:-3], refs[-3:]
    blocks, _, side = out.shape
    for c in range(blocks):
        at = pl.ds(c * side, side)
        u = parts[0][c]
        for part in parts[1:]:
            u = u + part[c].astype(F32)
        dx = primal_mask[step, :, at].astype(F32) * (x[:, at] + 2.0 * u)
        q = primal_step[:, at] * dx
        new_x[:, at] = dx - u
        new_spent[:, at] = -q if first else spent[:, at] - q
        out[c] = q.astype(BF16)


def pick_kernel(highs, cap, wants, *refs):
    blocks, outs = dict(zip(highs, refs[:-QUAD])), refs[-QUAD:]
    last = refs[0].shape[0] - 1
    for x, out in enumerate(outs):
        values = [blocks[h][jnp.minimum(wants[x, h * cap + r], last)] for h in sorted(highs) for r in range(cap)]
        for s, value in enumerate(values):
            out[s] = value


def near_forward_kernel(tile_of, land_of, turned, m0, m1, m2, m3, out, *totals):
    forward_products(tile_of.shape[0] // 2, tile_of, land_of, turned, (m0, m1, m2, m3), totals)
    for r in range(out.shape[0]):
        out[r] = gathered(totals, r)


def chip_forward_kernel(tile_of, land_of, turned, part, m0, m1, out, *totals):
    forward_products(0, tile_of, land_of, turned, (m0, m1), totals, (0, 1))
    for r in range(out.shape[0]):
        out[r] = part[r] + gathered(totals, r)


def rest_product_kernel(tile_of, row_of, held, hb, o0, o1, o3):
    transpose_products(0, tile_of, row_of, held, hb, (o3, o1, o0), (3, 1, 0))


def middle_kernel(step, tile_of, row_of, land_of, held, turned, dual_step, dual_mask, part, dy, rhs, m2, m3,
                  new_dy, new_rhs, hb, o2, *totals):
    side = held.shape[1]
    forward_products(0, tile_of, land_of, turned, (m2, m3), totals, (2, 3))
    for r in range(hb.shape[0]):
        at = pl.ds(r * side, side)
        v = part[r] + gathered(totals, r)
        new_dy[:, at] = dual_mask[step, :, at].astype(F32) * (dy[:, at] - v)

    def h_into(at, h):
        new_rhs[:, at] = rhs[:, at] - h

    scaled_blocks(side, new_dy, dual_step, hb, h_into)
    transpose_products(0, tile_of, row_of, held, hb, (o2,), (2,))


def last_kernel(tile_of, land_of, turned, part, dy, m2, m3, new_y, *totals):
    side = turned.shape[1]
    forward_products(0, tile_of, land_of, turned, (m2, m3), totals, (2, 3))
    for r in range(part.shape[0]):
        at = pl.ds(r * side, side)
        new_y[:, at] = dy[:, at] - (part[r] + gathered(totals, r))


def on_device(tiles, tile_rows, tile_cols, tile_counts, dual_step, primal_step, primal_mask, dual_mask, cot_x, cot_y):
    peers = lax.axis_size("rb")
    tile_slots, side, _ = tiles.shape
    batch = cot_x.shape[0]
    row_blocks = dual_step.shape[0] // side
    col_blocks = primal_step.shape[0] // side
    cap = max(2, (tile_slots + peers - 1) // peers)
    group = peers // QUAD
    half = group // 2
    slots = peers * cap
    places = -(-group * cap // 128) * 128
    steps = primal_mask.shape[0]
    dual_step = dual_step.reshape(1, -1)
    primal_step = primal_step.reshape(1, -1)
    y_shape = shape(cot_y.shape, F32)
    x_shape = shape(cot_x.shape, F32)
    part_set = (shape((half * cap, batch, side), BF16),) * QUAD
    block_set = shape((col_blocks, batch, side), BF16)
    hb_set = shape((row_blocks, batch, side), BF16)
    per_slot = pltpu.SMEM((slots,), I32)
    row_totals = [pltpu.VMEM((row_blocks + 1, batch, side), F32)] * LANES
    col_totals = [pltpu.VMEM((col_blocks + 1, batch, side), F32)] * (2 * half)
    tile_bytes = tiles.size * 2

    def call(kernel, name, moved, ins, outs, args, scratch=()):
        return pl.pallas_call(
            kernel,
            out_shape=outs,
            in_specs=ins,
            out_specs=jax.tree.map(lambda _: VM, outs),
            scratch_shapes=scratch,
            compiler_params=PARAMS,
            cost_estimate=cost(moved),
            name=name,
        )(*args)

    def swap(array, x):
        return lax.ppermute(array, "rb", [(p, p ^ x) for p in range(peers)])

    def near_swaps(parts):
        return [parts[0]] + [swap(parts[x], x) for x in range(1, QUAD)]

    step = steps - 1
    held, dy, rhs, hb, tile_of, row_of, land_of, *far_parts = pl.pallas_call(
        functools.partial(start_kernel, step, peers, cap, col_blocks),
        out_shape=(
            pltpu.VMEM(tiles.shape, BF16), y_shape, y_shape, hb_set, per_slot, per_slot, per_slot,
        ) + (shape((half * cap + 1, batch, side), BF16),) * QUAD,
        in_specs=[SM] + [HBM] * 6,
        out_specs=(VM,) * 4 + (SM,) * 3 + (VM,) * QUAD,
        scratch_shapes=[
            pltpu.SMEM((tile_slots,), I32), pltpu.SMEM((tile_slots,), I32), pltpu.VMEM(dual_step.shape, F32),
            pltpu.VMEM(cot_y.shape, I32), pltpu.VMEM(cot_y.shape, F32), pltpu.SMEM((peers,), I32),
            pltpu.SMEM((2 * QUAD, places), I32), pltpu.VMEM((2 * QUAD, places), I32),
            pltpu.SemaphoreType.DMA((tile_slots // CHUNK,)), pltpu.SemaphoreType.DMA((6,)),
        ],
        compiler_params=PARAMS,
        cost_estimate=cost(2 * tile_bytes),
        name="start",
    )(tile_counts, *(
        pltpu.with_memory_space_constraint(array, pltpu.HBM)
        for array in (tile_rows, tile_cols, tiles, dual_step, dual_mask, cot_y)
    ))
    turned = call(turn_kernel, "turn", tile_bytes, [VM], pltpu.VMEM(tiles.shape, BF16), (held,))
    x_state, spent, wants = cot_x, cot_x, None
    near_highs, far_highs = tuple(range(half)), tuple(reversed(range(half, group)))
    while True:
        far_got = near_swaps(far_parts)
        near_parts = call(near_product_kernel, "near_product", tile_bytes // 2, [SM] * 2 + [VM] * 2, part_set,
                          (tile_of, row_of, held, hb))
        near_got = near_swaps(near_parts)
        if wants is None:
            wants = pl.pallas_call(
                map_kernel,
                out_shape=pltpu.SMEM((2 * QUAD, places), I32),
                in_specs=[VM] * QUAD,
                out_specs=SM,
                scratch_shapes=[pltpu.VMEM((2 * QUAD, places), I32), pltpu.SemaphoreType.DMA],
                compiler_params=PARAMS,
                name="maps",
            )(*far_got)
        far_sums = call(functools.partial(sum_kernel, half, cap), "far_sum", 1 << 20, [SM] + [VM] * QUAD,
                        (block_set,) * half, (wants, *far_got), col_totals)
        got = [swap(far_sums[h], (half + h) * QUAD) for h in range(half)]
        near_sums = call(functools.partial(sum_kernel, 0, cap), "near_sum", 1 << 20, [SM] + [VM] * QUAD,
                         (shape(block_set.shape, F32),) + (block_set,) * (half - 1), (wants, *near_got), col_totals)
        got += [swap(near_sums[h], h * QUAD) for h in range(1, half)]
        if step == steps - 1:
            turned, x_state = lax.optimization_barrier((turned, x_state))
        x_state, spent, moved = call(
            functools.partial(primal_kernel, step, step == steps - 1), "primal", 1 << 20, [VM] * (4 + group),
            (x_shape, x_shape, block_set), (primal_mask, primal_step, x_state, spent, near_sums[0], *got))
        blocks = [moved] + [swap(moved, h * QUAD) for h in range(1, group)]
        near_moved, far_moved = (
            near_swaps(call(functools.partial(pick_kernel, highs, cap), name, 1 << 20, [SM] + [VM] * half, part_set,
                            (wants, *(blocks[h] for h in highs))))
            for name, highs in (("near_pick", near_highs), ("far_pick", far_highs))
        )
        part = call(near_forward_kernel, "near_forward", tile_bytes // 2, [SM] * 2 + [VM] * (1 + QUAD),
                    shape(hb_set.shape, F32), (tile_of, land_of, turned, *near_moved), row_totals)
        part = call(chip_forward_kernel, "chip_forward", tile_bytes // 4, [SM] * 2 + [VM] * 4,
                    shape(hb_set.shape, F32), (tile_of, land_of, turned, part, *far_moved[:2]), row_totals)
        if step == 0:
            break
        step -= 1
        dy, rhs, hb, across = call(
            functools.partial(middle_kernel, step), "middle", tile_bytes // 2, [SM] * 3 + [VM] * 9,
            (y_shape, y_shape, hb_set, part_set[0]),
            (tile_of, row_of, land_of, held, turned, dual_step, dual_mask, part, dy, rhs, *far_moved[2:]), row_totals)
        own, beside, aslant = call(rest_product_kernel, "rest_product", tile_bytes // 4, [SM] * 2 + [VM] * 2,
                                   part_set[:3], (tile_of, row_of, held, hb))
        far_parts = [own, beside, across, aslant]
    y_state = call(last_kernel, "last", tile_bytes // 4, [SM] * 2 + [VM] * 5, y_shape,
                   (tile_of, land_of, turned, part, dy, *far_moved[2:]), row_totals)
    return spent, rhs, x_state, y_state


def solution(mesh):
    rb = ("grp", "rb")
    return jax.shard_map(
        on_device,
        mesh=mesh,
        in_specs=(
            P(rb, None, None), P(rb), P(rb), P(rb), P(rb), P(rb),
            P(None, "grp", "rb"), P(None, "grp", "rb"), P("grp", "rb"), P("grp", "rb"),
        ),
        out_specs=(P("grp", "rb"),) * 4,
        check_vma=False,
    )
```

```python
import functools

import jax
import jax.numpy as jnp
from jax import lax
from jax.experimental import pallas as pl
from jax.experimental.pallas import tpu as pltpu
from jax.sharding import PartitionSpec as P

QUAD = 4
CHUNK = 8
LANES = 4
VM = pl.BlockSpec(memory_space=pltpu.VMEM)
SM = pl.BlockSpec(memory_space=pltpu.SMEM)
HBM = pl.BlockSpec(memory_space=pltpu.HBM)
PARAMS = pltpu.CompilerParams(vmem_limit_bytes=12 * 1024 * 1024)
F32, BF16, I32 = jnp.float32, jnp.bfloat16, jnp.int32


def shape(dims, dtype):
    return jax.ShapeDtypeStruct(dims, dtype)


def cost(moved):
    return pl.CostEstimate(flops=moved * 8, bytes_accessed=moved, transcendentals=0)


def scaled_blocks(side, dy, dual_step, hb, h_into=None):
    for r in range(hb.shape[0]):
        at = pl.ds(r * side, side)
        h = dual_step[:, at] * dy[:, at]
        hb[r] = h.astype(BF16)
        if h_into is not None:
            h_into(at, h)


def transpose_products(base, tile_of, row_of, tiles, hb, outs, xs=range(QUAD)):
    per = tile_of.shape[0] // (2 * QUAD)
    for x, out in zip(xs, outs):
        for s in range(per):
            slot = base + x * per + s
            out[s] = jnp.dot(hb[row_of[slot]], tiles[tile_of[slot]], preferred_element_type=F32).astype(BF16)


def forward_products(base, tile_of, land_of, turned, moved, totals, xs=range(QUAD)):
    per = tile_of.shape[0] // (2 * QUAD)
    for total in totals:
        total[...] = jnp.zeros_like(total)
    for x, part in zip(xs, moved):
        first = base + x * per
        terms = [jnp.dot(part[s], turned[tile_of[first + s]], preferred_element_type=F32) for s in range(per)]
        for s in range(0, per, LANES):
            several = range(min(LANES, per - s))
            spots = [land_of[first + s + i] for i in several]
            held = [totals[i][spots[i]] + terms[s + i] for i in several]
            for i in several:
                totals[i][spots[i]] = held[i]


def gathered(totals, r):
    value = totals[0][r]
    for total in totals[1:]:
        value = value + total[r]
    return value


def start_kernel(step, peers, cap, col_blocks, count, rows_in, cols_in, tiles, step_in, mask_in, cot_in,
                 held, dy, rhs, hb, tile_of, row_of, land_of, o0, o1, o2, o3,
                 rows, cols, dual_step, dual_mask, cot_y, filled, wants, plan, sems, small):
    tile_slots, side, _ = tiles.shape
    group = peers // QUAD
    half = group // 2
    chunks = tile_slots // CHUNK
    minor = [
        pltpu.make_async_copy(src, dst, small.at[i])
        for i, (src, dst) in enumerate((
            (cols_in, cols), (rows_in, rows), (step_in, dual_step), (mask_in.at[step], dual_mask), (cot_in, cot_y),
        ))
    ]
    for copy in minor:
        copy.start()

    def tile_copy(c):
        at = pl.ds(c * CHUNK, CHUNK)
        return pltpu.make_async_copy(tiles.at[at], held.at[at], sems.at[c])

    for c in range(chunks):
        tile_copy(c).start()
    for o in range(peers):
        filled[o] = 0
    for s in range(tile_of.shape[0]):
        tile_of[s] = 0
        row_of[s] = 0
        land_of[s] = hb.shape[0]
    for x in range(QUAD):
        for s in range(group * cap):
            wants[x, s] = col_blocks
    for copy in minor:
        copy.wait()
    me = lax.axis_index("rb").astype(I32)
    scale = (1 << 19) // col_blocks + 1

    def place_tile(t, _):
        col = cols[t]
        owner = (col * scale) >> 19
        rank = filled[owner]
        filled[owner] = rank + 1
        apart = owner ^ me
        high, quad = apart // QUAD, apart % QUAD
        place = high * cap + rank
        near = jnp.where(high < half, 1, 0)
        slot = (near * QUAD + quad) * (half * cap) + place - (1 - near) * (half * cap)
        tile_of[slot] = t
        row_of[slot] = rows[t]
        land_of[slot] = rows[t]
        wants[quad, place] = col - owner * col_blocks
        return 0

    lax.fori_loop(0, count[0], place_tile, 0)
    chart = pltpu.make_async_copy(wants, plan, small.at[len(minor)])
    chart.start()
    dy[...] = dual_mask[...].astype(F32) * cot_y[...]

    def h_into(at, h):
        rhs[:, at] = -h

    scaled_blocks(side, dy, dual_step, hb, h_into)
    chart.wait()
    for out in (o0, o1, o2, o3):
        out[half * cap, :, pl.ds(0, plan.shape[1])] = plan[...].astype(BF16)
    for c in range(chunks):
        tile_copy(c).wait()
    transpose_products(0, tile_of, row_of, held, hb, (o0, o1, o2, o3))


def turn_kernel(held, turned):
    def one_chunk(c, _):
        for j in range(CHUNK):
            turned[c * CHUNK + j] = held[c * CHUNK + j].T
        return 0

    lax.fori_loop(0, held.shape[0] // CHUNK, one_chunk, 0)


def near_product_kernel(tile_of, row_of, held, hb, o0, o1, o2, o3):
    transpose_products(tile_of.shape[0] // 2, tile_of, row_of, held, hb, (o0, o1, o2, o3))


def map_kernel(a0, a1, a2, a3, wants, whole, sem):
    for x, part in enumerate((a0, a1, a2, a3)):
        plan = part[part.shape[0] - 1].astype(F32)
        whole[pl.ds(x, 1)] = plan[x:x + 1, :whole.shape[1]].astype(I32)
    whole[pl.ds(QUAD, QUAD)] = jnp.zeros((QUAD, whole.shape[1]), I32)
    copy = pltpu.make_async_copy(whole, wants, sem)
    copy.start()
    copy.wait()


def sum_kernel(first_high, cap, wants, a0, a1, a2, a3, *rest):
    parts = (a0, a1, a2, a3)
    half = len(rest) // 3
    outs, totals = rest[:half], rest[half:]
    for total in totals:
        total[...] = jnp.zeros_like(total)
    for r in range(cap):
        for pair in range(QUAD // 2):
            jobs = []
            for h in range(half):
                for side in range(2):
                    x = 2 * pair + side
                    spot = wants[x, (first_high + h) * cap + r]
                    jobs.append((totals[2 * h + side], spot, parts[x][h * cap + r].astype(F32)))
            values = [total[spot] + part for total, spot, part in jobs]
            for (total, spot, _), value in zip(jobs, values):
                total[spot] = value
    for h, out in enumerate(outs):
        for c in range(out.shape[0]):
            out[c] = (totals[2 * h][c] + totals[2 * h + 1][c]).astype(out.dtype)


def primal_kernel(step, primal_mask, primal_step, x, *refs):
    parts, (u_out, dx_out, out) = refs[:-3], refs[-3:]
    blocks, _, side = out.shape
    for c in range(blocks):
        at = pl.ds(c * side, side)
        u = parts[0][c]
        for part in parts[1:]:
            u = u + part[c].astype(F32)
        dx = primal_mask[step, :, at].astype(F32) * (x[:, at] + 2.0 * u)
        u_out[:, at] = u
        dx_out[:, at] = dx
        out[c] = (primal_step[:, at] * dx).astype(BF16)


def settle_kernel(first, primal_step, u, dx, spent, new_x, new_spent):
    new_x[...] = dx[...] - u[...]
    q = primal_step[...] * dx[...]
    new_spent[...] = -q if first else spent[...] - q


def settle_dual_kernel(dual_step, dy, rhs, new_rhs):
    new_rhs[...] = rhs[...] - dual_step[...] * dy[...]


def pick_kernel(highs, cap, wants, *refs):
    blocks, outs = dict(zip(highs, refs[:-QUAD])), refs[-QUAD:]
    last = refs[0].shape[0] - 1
    for x, out in enumerate(outs):
        values = [blocks[h][jnp.minimum(wants[x, h * cap + r], last)] for h in sorted(highs) for r in range(cap)]
        for s, value in enumerate(values):
            out[s] = value


def near_forward_kernel(tile_of, land_of, turned, m0, m1, m2, m3, out, *totals):
    forward_products(tile_of.shape[0] // 2, tile_of, land_of, turned, (m0, m1, m2, m3), totals)
    for r in range(out.shape[0]):
        out[r] = gathered(totals, r)


def chip_forward_kernel(tile_of, land_of, turned, part, m0, m1, out, *totals):
    forward_products(0, tile_of, land_of, turned, (m0, m1), totals, (0, 1))
    for r in range(out.shape[0]):
        out[r] = part[r] + gathered(totals, r)


def rest_product_kernel(tile_of, row_of, held, hb, o0, o1, o3):
    transpose_products(0, tile_of, row_of, held, hb, (o3, o1, o0), (3, 1, 0))


def middle_kernel(step, tile_of, row_of, land_of, held, turned, dual_step, dual_mask, part, dy, m2, m3,
                  new_dy, hb, o2, *totals):
    side = held.shape[1]
    forward_products(0, tile_of, land_of, turned, (m2, m3), totals, (2, 3))
    for r in range(hb.shape[0]):
        at = pl.ds(r * side, side)
        v = part[r] + gathered(totals, r)
        new_dy[:, at] = dual_mask[step, :, at].astype(F32) * (dy[:, at] - v)

    scaled_blocks(side, new_dy, dual_step, hb)
    transpose_products(0, tile_of, row_of, held, hb, (o2,), (2,))


def last_kernel(tile_of, land_of, turned, part, dy, m2, m3, new_y, *totals):
    side = turned.shape[1]
    forward_products(0, tile_of, land_of, turned, (m2, m3), totals, (2, 3))
    for r in range(part.shape[0]):
        at = pl.ds(r * side, side)
        new_y[:, at] = dy[:, at] - (part[r] + gathered(totals, r))


def on_device(tiles, tile_rows, tile_cols, tile_counts, dual_step, primal_step, primal_mask, dual_mask, cot_x, cot_y):
    peers = lax.axis_size("rb")
    tile_slots, side, _ = tiles.shape
    batch = cot_x.shape[0]
    row_blocks = dual_step.shape[0] // side
    col_blocks = primal_step.shape[0] // side
    cap = max(2, (tile_slots + peers - 1) // peers)
    group = peers // QUAD
    half = group // 2
    slots = peers * cap
    places = -(-group * cap // 128) * 128
    steps = primal_mask.shape[0]
    dual_step = dual_step.reshape(1, -1)
    primal_step = primal_step.reshape(1, -1)
    y_shape = shape(cot_y.shape, F32)
    x_shape = shape(cot_x.shape, F32)
    part_set = (shape((half * cap, batch, side), BF16),) * QUAD
    block_set = shape((col_blocks, batch, side), BF16)
    hb_set = shape((row_blocks, batch, side), BF16)
    per_slot = pltpu.SMEM((slots,), I32)
    row_totals = [pltpu.VMEM((row_blocks + 1, batch, side), F32)] * LANES
    col_totals = [pltpu.VMEM((col_blocks + 1, batch, side), F32)] * (2 * half)
    tile_bytes = tiles.size * 2

    def call(kernel, name, moved, ins, outs, args, scratch=()):
        return pl.pallas_call(
            kernel,
            out_shape=outs,
            in_specs=ins,
            out_specs=jax.tree.map(lambda _: VM, outs),
            scratch_shapes=scratch,
            compiler_params=PARAMS,
            cost_estimate=cost(moved),
            name=name,
        )(*args)

    def swap(array, x):
        return lax.ppermute(array, "rb", [(p, p ^ x) for p in range(peers)])

    def near_swaps(parts):
        return [parts[0]] + [swap(parts[x], x) for x in range(1, QUAD)]

    step = steps - 1
    held, dy, rhs, hb, tile_of, row_of, land_of, *far_parts = pl.pallas_call(
        functools.partial(start_kernel, step, peers, cap, col_blocks),
        out_shape=(
            pltpu.VMEM(tiles.shape, BF16), y_shape, y_shape, hb_set, per_slot, per_slot, per_slot,
        ) + (shape((half * cap + 1, batch, side), BF16),) * QUAD,
        in_specs=[SM] + [HBM] * 6,
        out_specs=(VM,) * 4 + (SM,) * 3 + (VM,) * QUAD,
        scratch_shapes=[
            pltpu.SMEM((tile_slots,), I32), pltpu.SMEM((tile_slots,), I32), pltpu.VMEM(dual_step.shape, F32),
            pltpu.VMEM(cot_y.shape, I32), pltpu.VMEM(cot_y.shape, F32), pltpu.SMEM((peers,), I32),
            pltpu.SMEM((2 * QUAD, places), I32), pltpu.VMEM((2 * QUAD, places), I32),
            pltpu.SemaphoreType.DMA((tile_slots // CHUNK,)), pltpu.SemaphoreType.DMA((6,)),
        ],
        compiler_params=PARAMS,
        cost_estimate=cost(2 * tile_bytes),
        name="start",
    )(tile_counts, *(
        pltpu.with_memory_space_constraint(array, pltpu.HBM)
        for array in (tile_rows, tile_cols, tiles, dual_step, dual_mask, cot_y)
    ))
    turned = call(turn_kernel, "turn", tile_bytes, [VM], pltpu.VMEM(tiles.shape, BF16), (held,))
    x_state, spent, wants = cot_x, cot_x, None
    near_highs, far_highs = tuple(range(half)), tuple(reversed(range(half, group)))
    while True:
        far_got = near_swaps(far_parts)
        near_parts = call(near_product_kernel, "near_product", tile_bytes // 2, [SM] * 2 + [VM] * 2, part_set,
                          (tile_of, row_of, held, hb))
        near_got = near_swaps(near_parts)
        if wants is None:
            wants = pl.pallas_call(
                map_kernel,
                out_shape=pltpu.SMEM((2 * QUAD, places), I32),
                in_specs=[VM] * QUAD,
                out_specs=SM,
                scratch_shapes=[pltpu.VMEM((2 * QUAD, places), I32), pltpu.SemaphoreType.DMA],
                compiler_params=PARAMS,
                name="maps",
            )(*far_got)
        far_sums = call(functools.partial(sum_kernel, half, cap), "far_sum", 1 << 20, [SM] + [VM] * QUAD,
                        (block_set,) * half, (wants, *far_got), col_totals)
        got = [swap(far_sums[h], (half + h) * QUAD) for h in range(half)]
        near_sums = call(functools.partial(sum_kernel, 0, cap), "near_sum", 1 << 20, [SM] + [VM] * QUAD,
                         (shape(block_set.shape, F32),) + (block_set,) * (half - 1), (wants, *near_got), col_totals)
        got += [swap(near_sums[h], h * QUAD) for h in range(1, half)]
        if step == steps - 1:
            turned, x_state = lax.optimization_barrier((turned, x_state))
        u, dx, moved = call(
            functools.partial(primal_kernel, step), "primal", 1 << 20, [VM] * (3 + group),
            (x_shape, x_shape, block_set), (primal_mask, primal_step, x_state, near_sums[0], *got))
        x_state, spent = call(functools.partial(settle_kernel, step == steps - 1), "settle", 1 << 20, [VM] * 4,
                              (x_shape, x_shape), (primal_step, u, dx, spent))
        blocks = [moved] + [swap(moved, h * QUAD) for h in range(1, group)]
        near_moved, far_moved = (
            near_swaps(call(functools.partial(pick_kernel, highs, cap), name, 1 << 20, [SM] + [VM] * half, part_set,
                            (wants, *(blocks[h] for h in highs))))
            for name, highs in (("near_pick", near_highs), ("far_pick", far_highs))
        )
        part = call(near_forward_kernel, "near_forward", tile_bytes // 2, [SM] * 2 + [VM] * (1 + QUAD),
                    shape(hb_set.shape, F32), (tile_of, land_of, turned, *near_moved), row_totals)
        part = call(chip_forward_kernel, "chip_forward", tile_bytes // 4, [SM] * 2 + [VM] * 4,
                    shape(hb_set.shape, F32), (tile_of, land_of, turned, part, *far_moved[:2]), row_totals)
        if step == 0:
            break
        step -= 1
        dy, hb, across = call(
            functools.partial(middle_kernel, step), "middle", tile_bytes // 2, [SM] * 3 + [VM] * 8,
            (y_shape, hb_set, part_set[0]),
            (tile_of, row_of, land_of, held, turned, dual_step, dual_mask, part, dy, *far_moved[2:]), row_totals)
        rhs = call(settle_dual_kernel, "settle_dual", 1 << 20, [VM] * 3, y_shape, (dual_step, dy, rhs))
        own, beside, aslant = call(rest_product_kernel, "rest_product", tile_bytes // 4, [SM] * 2 + [VM] * 2,
                                   part_set[:3], (tile_of, row_of, held, hb))
        far_parts = [own, beside, across, aslant]
    y_state = call(last_kernel, "last", tile_bytes // 4, [SM] * 2 + [VM] * 5, y_shape,
                   (tile_of, land_of, turned, part, dy, *far_moved[2:]), row_totals)
    return spent, rhs, x_state, y_state


def solution(mesh):
    rb = ("grp", "rb")
    return jax.shard_map(
        on_device,
        mesh=mesh,
        in_specs=(
            P(rb, None, None), P(rb), P(rb), P(rb), P(rb), P(rb),
            P(None, "grp", "rb"), P(None, "grp", "rb"), P("grp", "rb"), P("grp", "rb"),
        ),
        out_specs=(P("grp", "rb"),) * 4,
        check_vma=False,
    )
```

```python
import functools

import jax
import jax.numpy as jnp
from jax import lax
from jax.experimental import pallas as pl
from jax.experimental.pallas import tpu as pltpu
from jax.sharding import PartitionSpec as P

QUAD = 4
CHUNK = 8
LANES = 4
VM = pl.BlockSpec(memory_space=pltpu.VMEM)
SM = pl.BlockSpec(memory_space=pltpu.SMEM)
HBM = pl.BlockSpec(memory_space=pltpu.HBM)
PARAMS = pltpu.CompilerParams(vmem_limit_bytes=12 * 1024 * 1024)
F32, BF16, I32 = jnp.float32, jnp.bfloat16, jnp.int32


def shape(dims, dtype):
    return jax.ShapeDtypeStruct(dims, dtype)


def cost(moved):
    return pl.CostEstimate(flops=moved * 8, bytes_accessed=moved, transcendentals=0)


def scaled_blocks(side, dy, dual_step, hb, h_into=None):
    for r in range(hb.shape[0]):
        at = pl.ds(r * side, side)
        h = dual_step[:, at] * dy[:, at]
        hb[r] = h.astype(BF16)
        if h_into is not None:
            h_into(at, h)


def slot_at(cap, group, x, high, rank):
    if high == 0:
        return QUAD * (group - 1) * cap + x * cap + rank
    return x * (group - 1) * cap + (high - 1) * cap + rank


def transpose_products(cap, highs, tile_of, row_of, tiles, hb, outs, xs=range(QUAD)):
    group = tile_of.shape[0] // (QUAD * cap)
    for x, out in zip(xs, outs):
        for s in range(len(highs) * cap):
            slot = slot_at(cap, group, x, highs[s // cap], s % cap)
            out[s] = jnp.dot(hb[row_of[slot]], tiles[tile_of[slot]], preferred_element_type=F32).astype(BF16)


def forward_products(cap, highs, tile_of, land_of, turned, moved, totals, xs=range(QUAD)):
    group = tile_of.shape[0] // (QUAD * cap)
    per = len(highs) * cap
    for total in totals:
        total[...] = jnp.zeros_like(total)
    for x, part in zip(xs, moved):
        at = [slot_at(cap, group, x, high, rank) for high in highs for rank in range(cap)]
        terms = [jnp.dot(part[s], turned[tile_of[at[s]]], preferred_element_type=F32) for s in range(per)]
        for s in range(0, per, LANES):
            several = range(min(LANES, per - s))
            spots = [land_of[at[s + i]] for i in several]
            held = [totals[i][spots[i]] + terms[s + i] for i in several]
            for i in several:
                totals[i][spots[i]] = held[i]


def gathered(totals, r):
    value = totals[0][r]
    for total in totals[1:]:
        value = value + total[r]
    return value


def start_kernel(step, peers, cap, col_blocks, count, rows_in, cols_in, tiles, step_in, mask_in, cot_in,
                 held, dy, rhs, hb, tile_of, row_of, land_of, o0, o1, o2, o3,
                 rows, cols, dual_step, dual_mask, cot_y, filled, wants, plan, sems, small):
    tile_slots, side, _ = tiles.shape
    group = peers // QUAD
    most = (group - 1) * cap
    chunks = tile_slots // CHUNK
    minor = [
        pltpu.make_async_copy(src, dst, small.at[i])
        for i, (src, dst) in enumerate((
            (cols_in, cols), (rows_in, rows), (step_in, dual_step), (mask_in.at[step], dual_mask), (cot_in, cot_y),
        ))
    ]
    for copy in minor:
        copy.start()

    def tile_copy(c):
        at = pl.ds(c * CHUNK, CHUNK)
        return pltpu.make_async_copy(tiles.at[at], held.at[at], sems.at[c])

    for c in range(chunks):
        tile_copy(c).start()
    for o in range(peers):
        filled[o] = 0
    for s in range(tile_of.shape[0]):
        tile_of[s] = 0
        row_of[s] = 0
        land_of[s] = hb.shape[0]
    for x in range(QUAD):
        for s in range(group * cap):
            wants[x, s] = col_blocks
    for copy in minor:
        copy.wait()
    me = lax.axis_index("rb").astype(I32)
    scale = (1 << 19) // col_blocks + 1

    def place_tile(t, _):
        col = cols[t]
        owner = (col * scale) >> 19
        rank = filled[owner]
        filled[owner] = rank + 1
        apart = owner ^ me
        high, quad = apart // QUAD, apart % QUAD
        place = high * cap + rank
        slot = jnp.where(high == 0, QUAD * most + quad * cap + rank, quad * most + place - cap)
        tile_of[slot] = t
        row_of[slot] = rows[t]
        land_of[slot] = rows[t]
        wants[quad, place] = col - owner * col_blocks
        return 0

    lax.fori_loop(0, count[0], place_tile, 0)
    chart = pltpu.make_async_copy(wants, plan, small.at[len(minor)])
    chart.start()
    dy[...] = dual_mask[...].astype(F32) * cot_y[...]

    def h_into(at, h):
        rhs[:, at] = -h

    scaled_blocks(side, dy, dual_step, hb, h_into)
    chart.wait()
    for out in (o0, o1, o2, o3):
        out[most, :, pl.ds(0, plan.shape[1])] = plan[...].astype(BF16)
    for c in range(chunks):
        tile_copy(c).wait()
    transpose_products(cap, range(1, group), tile_of, row_of, held, hb, (o0, o1, o2, o3))


def turn_kernel(held, turned):
    def one_chunk(c, _):
        for j in range(CHUNK):
            turned[c * CHUNK + j] = held[c * CHUNK + j].T
        return 0

    lax.fori_loop(0, held.shape[0] // CHUNK, one_chunk, 0)


def near_product_kernel(cap, tile_of, row_of, held, hb, o0, o1, o2, o3):
    transpose_products(cap, (0,), tile_of, row_of, held, hb, (o0, o1, o2, o3))


def map_kernel(a0, a1, a2, a3, wants, whole, sem):
    for x, part in enumerate((a0, a1, a2, a3)):
        plan = part[part.shape[0] - 1].astype(F32)
        whole[pl.ds(x, 1)] = plan[x:x + 1, :whole.shape[1]].astype(I32)
    whole[pl.ds(QUAD, QUAD)] = jnp.zeros((QUAD, whole.shape[1]), I32)
    copy = pltpu.make_async_copy(whole, wants, sem)
    copy.start()
    copy.wait()


def sum_kernel(first_high, cap, wants, a0, a1, a2, a3, *rest):
    parts = (a0, a1, a2, a3)
    half = len(rest) // 3
    outs, totals = rest[:half], rest[half:]
    for total in totals:
        total[...] = jnp.zeros_like(total)
    for r in range(cap):
        for pair in range(QUAD // 2):
            jobs = []
            for h in range(half):
                for side in range(2):
                    x = 2 * pair + side
                    spot = wants[x, (first_high + h) * cap + r]
                    jobs.append((totals[2 * h + side], spot, parts[x][h * cap + r].astype(F32)))
            values = [total[spot] + part for total, spot, part in jobs]
            for (total, spot, _), value in zip(jobs, values):
                total[spot] = value
    for h, out in enumerate(outs):
        for c in range(out.shape[0]):
            out[c] = (totals[2 * h][c] + totals[2 * h + 1][c]).astype(out.dtype)


def primal_kernel(step, primal_mask, primal_step, x, *refs):
    parts, (u_out, dx_out, out) = refs[:-3], refs[-3:]
    blocks, _, side = out.shape
    for c in range(blocks):
        at = pl.ds(c * side, side)
        u = parts[0][c]
        for part in parts[1:]:
            u = u + part[c].astype(F32)
        dx = primal_mask[step, :, at].astype(F32) * (x[:, at] + 2.0 * u)
        u_out[:, at] = u
        dx_out[:, at] = dx
        out[c] = (primal_step[:, at] * dx).astype(BF16)


def settle_kernel(first, primal_step, u, dx, spent, new_x, new_spent):
    new_x[...] = dx[...] - u[...]
    q = primal_step[...] * dx[...]
    new_spent[...] = -q if first else spent[...] - q


def settle_dual_kernel(dual_step, dy, rhs, new_rhs):
    new_rhs[...] = rhs[...] - dual_step[...] * dy[...]


def pick_kernel(highs, cap, wants, *refs):
    blocks, outs = dict(zip(highs, refs[:-QUAD])), refs[-QUAD:]
    last = refs[0].shape[0] - 1
    for x, out in enumerate(outs):
        values = [blocks[h][jnp.minimum(wants[x, h * cap + r], last)] for h in sorted(highs) for r in range(cap)]
        for s, value in enumerate(values):
            out[s] = value


def near_forward_kernel(cap, highs, tile_of, land_of, turned, m0, m1, m2, m3, out, *totals):
    forward_products(cap, highs, tile_of, land_of, turned, (m0, m1, m2, m3), totals)
    for r in range(out.shape[0]):
        out[r] = gathered(totals, r)


def chip_forward_kernel(cap, highs, tile_of, land_of, turned, part, m0, m1, out, *totals):
    forward_products(cap, highs, tile_of, land_of, turned, (m0, m1), totals, (0, 1))
    for r in range(out.shape[0]):
        out[r] = part[r] + gathered(totals, r)


def rest_product_kernel(cap, highs, tile_of, row_of, held, hb, o0, o1, o3):
    transpose_products(cap, highs, tile_of, row_of, held, hb, (o3, o1, o0), (3, 1, 0))


def middle_kernel(step, cap, highs, sent, tile_of, row_of, land_of, held, turned, dual_step, dual_mask, part, dy, m2, m3,
                  new_dy, hb, o2, *totals):
    side = held.shape[1]
    forward_products(cap, highs, tile_of, land_of, turned, (m2, m3), totals, (2, 3))
    for r in range(hb.shape[0]):
        at = pl.ds(r * side, side)
        v = part[r] + gathered(totals, r)
        new_dy[:, at] = dual_mask[step, :, at].astype(F32) * (dy[:, at] - v)

    scaled_blocks(side, new_dy, dual_step, hb)
    transpose_products(cap, sent, tile_of, row_of, held, hb, (o2,), (2,))


def last_kernel(cap, highs, tile_of, land_of, turned, part, dy, m2, m3, new_y, *totals):
    side = turned.shape[1]
    forward_products(cap, highs, tile_of, land_of, turned, (m2, m3), totals, (2, 3))
    for r in range(part.shape[0]):
        at = pl.ds(r * side, side)
        new_y[:, at] = dy[:, at] - (part[r] + gathered(totals, r))


def on_device(tiles, tile_rows, tile_cols, tile_counts, dual_step, primal_step, primal_mask, dual_mask, cot_x, cot_y):
    peers = lax.axis_size("rb")
    tile_slots, side, _ = tiles.shape
    batch = cot_x.shape[0]
    row_blocks = dual_step.shape[0] // side
    col_blocks = primal_step.shape[0] // side
    cap = max(2, (tile_slots + peers - 1) // peers)
    group = peers // QUAD
    half = group // 2
    slots = peers * cap
    places = -(-group * cap // 128) * 128
    steps = primal_mask.shape[0]
    dual_step = dual_step.reshape(1, -1)
    primal_step = primal_step.reshape(1, -1)
    y_shape = shape(cot_y.shape, F32)
    x_shape = shape(cot_x.shape, F32)
    part_set, most_set, own_set = ((shape((n * cap, batch, side), BF16),) * QUAD for n in (half, group - 1, 1))
    block_set = shape((col_blocks, batch, side), BF16)
    hb_set = shape((row_blocks, batch, side), BF16)
    per_slot = pltpu.SMEM((slots,), I32)
    row_totals = [pltpu.VMEM((row_blocks + 1, batch, side), F32)] * LANES
    col_totals = [pltpu.VMEM((col_blocks + 1, batch, side), F32)] * (2 * (group - 1))
    tile_bytes = tiles.size * 2

    def call(kernel, name, moved, ins, outs, args, scratch=()):
        return pl.pallas_call(
            kernel,
            out_shape=outs,
            in_specs=ins,
            out_specs=jax.tree.map(lambda _: VM, outs),
            scratch_shapes=scratch,
            compiler_params=PARAMS,
            cost_estimate=cost(moved),
            name=name,
        )(*args)

    def swap(array, x):
        return lax.ppermute(array, "rb", [(p, p ^ x) for p in range(peers)])

    def near_swaps(parts):
        return [parts[0]] + [swap(parts[x], x) for x in range(1, QUAD)]

    step = steps - 1
    held, dy, rhs, hb, tile_of, row_of, land_of, *far_parts = pl.pallas_call(
        functools.partial(start_kernel, step, peers, cap, col_blocks),
        out_shape=(
            pltpu.VMEM(tiles.shape, BF16), y_shape, y_shape, hb_set, per_slot, per_slot, per_slot,
        ) + (shape(((group - 1) * cap + 1, batch, side), BF16),) * QUAD,
        in_specs=[SM] + [HBM] * 6,
        out_specs=(VM,) * 4 + (SM,) * 3 + (VM,) * QUAD,
        scratch_shapes=[
            pltpu.SMEM((tile_slots,), I32), pltpu.SMEM((tile_slots,), I32), pltpu.VMEM(dual_step.shape, F32),
            pltpu.VMEM(cot_y.shape, I32), pltpu.VMEM(cot_y.shape, F32), pltpu.SMEM((peers,), I32),
            pltpu.SMEM((2 * QUAD, places), I32), pltpu.VMEM((2 * QUAD, places), I32),
            pltpu.SemaphoreType.DMA((tile_slots // CHUNK,)), pltpu.SemaphoreType.DMA((6,)),
        ],
        compiler_params=PARAMS,
        cost_estimate=cost(2 * tile_bytes),
        name="start",
    )(tile_counts, *(
        pltpu.with_memory_space_constraint(array, pltpu.HBM)
        for array in (tile_rows, tile_cols, tiles, dual_step, dual_mask, cot_y)
    ))
    turned = call(turn_kernel, "turn", tile_bytes, [VM], pltpu.VMEM(tiles.shape, BF16), (held,))
    x_state, spent, wants = cot_x, cot_x, None
    near_highs, late_highs = tuple(range(half)), tuple(range(half, group))
    far_highs = tuple(reversed(late_highs))
    while True:
        far_got = near_swaps(far_parts)
        near_parts = call(functools.partial(near_product_kernel, cap), "near_product", tile_bytes // 4, [SM] * 2 + [VM] * 2, own_set,
                          (tile_of, row_of, held, hb))
        near_got = near_swaps(near_parts)
        if wants is None:
            wants = pl.pallas_call(
                map_kernel,
                out_shape=pltpu.SMEM((2 * QUAD, places), I32),
                in_specs=[VM] * QUAD,
                out_specs=SM,
                scratch_shapes=[pltpu.VMEM((2 * QUAD, places), I32), pltpu.SemaphoreType.DMA],
                compiler_params=PARAMS,
                name="maps",
            )(*far_got)
        far_sums = call(functools.partial(sum_kernel, 1, cap), "far_sum", 1 << 20, [SM] + [VM] * QUAD,
                        (block_set,) * (group - 1), (wants, *far_got), col_totals)
        own_sum = call(functools.partial(sum_kernel, 0, cap), "own_sum", 1 << 20, [SM] + [VM] * QUAD,
                       (shape(block_set.shape, F32),), (wants, *near_got), col_totals[:2])
        got = [swap(far_sums[h - 1], h * QUAD) for h in (*range(half, group), *range(1, half))]
        if step == steps - 1:
            turned, x_state = lax.optimization_barrier((turned, x_state))
        u, dx, moved = call(
            functools.partial(primal_kernel, step), "primal", 1 << 20, [VM] * (3 + group),
            (x_shape, x_shape, block_set), (primal_mask, primal_step, x_state, *own_sum, *got))
        x_state, spent = call(functools.partial(settle_kernel, step == steps - 1), "settle", 1 << 20, [VM] * 4,
                              (x_shape, x_shape), (primal_step, u, dx, spent))
        blocks = [moved] + [swap(moved, h * QUAD) for h in range(1, group)]
        near_moved, far_moved = (
            near_swaps(call(functools.partial(pick_kernel, highs, cap), name, 1 << 20, [SM] + [VM] * half, part_set,
                            (wants, *(blocks[h] for h in highs))))
            for name, highs in (("near_pick", near_highs), ("far_pick", far_highs))
        )
        part = call(functools.partial(near_forward_kernel, cap, near_highs), "near_forward", tile_bytes // 2, [SM] * 2 + [VM] * (1 + QUAD),
                    shape(hb_set.shape, F32), (tile_of, land_of, turned, *near_moved), row_totals)
        part = call(functools.partial(chip_forward_kernel, cap, late_highs), "chip_forward", tile_bytes // 4, [SM] * 2 + [VM] * 4,
                    shape(hb_set.shape, F32), (tile_of, land_of, turned, part, *far_moved[:2]), row_totals)
        if step == 0:
            break
        step -= 1
        dy, hb, across = call(
            functools.partial(middle_kernel, step, cap, late_highs, range(1, group)), "middle", tile_bytes // 2, [SM] * 3 + [VM] * 8,
            (y_shape, hb_set, most_set[0]),
            (tile_of, row_of, land_of, held, turned, dual_step, dual_mask, part, dy, *far_moved[2:]), row_totals)
        rhs = call(settle_dual_kernel, "settle_dual", 1 << 20, [VM] * 3, y_shape, (dual_step, dy, rhs))
        own, beside, aslant = call(functools.partial(rest_product_kernel, cap, range(1, group)), "rest_product",
                                   tile_bytes // 2, [SM] * 2 + [VM] * 2, most_set[:3], (tile_of, row_of, held, hb))
        far_parts = [own, beside, across, aslant]
    y_state = call(functools.partial(last_kernel, cap, late_highs), "last", tile_bytes // 4, [SM] * 2 + [VM] * 5, y_shape,
                   (tile_of, land_of, turned, part, dy, *far_moved[2:]), row_totals)
    return spent, rhs, x_state, y_state


def solution(mesh):
    rb = ("grp", "rb")
    return jax.shard_map(
        on_device,
        mesh=mesh,
        in_specs=(
            P(rb, None, None), P(rb), P(rb), P(rb), P(rb), P(rb),
            P(None, "grp", "rb"), P(None, "grp", "rb"), P("grp", "rb"), P("grp", "rb"),
        ),
        out_specs=(P("grp", "rb"),) * 4,
        check_vma=False,
    )
```

```python
import functools

import jax
import jax.numpy as jnp
from jax import lax
from jax.experimental import pallas as pl
from jax.experimental.pallas import tpu as pltpu
from jax.sharding import PartitionSpec as P

QUAD = 4
CHUNK = 8
LANES = 4
VM = pl.BlockSpec(memory_space=pltpu.VMEM)
SM = pl.BlockSpec(memory_space=pltpu.SMEM)
HBM = pl.BlockSpec(memory_space=pltpu.HBM)
PARAMS = pltpu.CompilerParams(vmem_limit_bytes=12 * 1024 * 1024)
F32, BF16, I32 = jnp.float32, jnp.bfloat16, jnp.int32


def shape(dims, dtype):
    return jax.ShapeDtypeStruct(dims, dtype)


def cost(moved):
    return pl.CostEstimate(flops=moved * 8, bytes_accessed=moved, transcendentals=0)


def scaled_blocks(side, dy, dual_step, hb, h_into=None):
    for r in range(hb.shape[0]):
        at = pl.ds(r * side, side)
        h = dual_step[:, at] * dy[:, at]
        hb[r] = h.astype(BF16)
        if h_into is not None:
            h_into(at, h)


def transpose_products(base, tile_of, row_of, tiles, hb, outs, xs=range(QUAD)):
    per = tile_of.shape[0] // (2 * QUAD)
    for x, out in zip(xs, outs):
        for s in range(per):
            slot = base + x * per + s
            out[s] = jnp.dot(hb[row_of[slot]], tiles[tile_of[slot]], preferred_element_type=F32).astype(BF16)


def forward_products(base, tile_of, land_of, turned, moved, totals, xs=range(QUAD)):
    per = tile_of.shape[0] // (2 * QUAD)
    for total in totals:
        total[...] = jnp.zeros_like(total)
    for x, part in zip(xs, moved):
        first = base + x * per
        terms = [jnp.dot(part[s], turned[tile_of[first + s]], preferred_element_type=F32) for s in range(per)]
        for s in range(0, per, LANES):
            several = range(min(LANES, per - s))
            spots = [land_of[first + s + i] for i in several]
            held = [totals[i][spots[i]] + terms[s + i] for i in several]
            for i in several:
                totals[i][spots[i]] = held[i]


def gathered(totals, r):
    value = totals[0][r]
    for total in totals[1:]:
        value = value + total[r]
    return value


def start_kernel(step, peers, cap, col_blocks, count, rows_in, cols_in, tiles, step_in, mask_in, cot_in,
                 held, dy, rhs, hb, tile_of, row_of, land_of, o0, o1, o2, o3,
                 rows, cols, dual_step, dual_mask, cot_y, filled, wants, plan, sems, small):
    tile_slots, side, _ = tiles.shape
    group = peers // QUAD
    half = group // 2
    chunks = tile_slots // CHUNK
    minor = [
        pltpu.make_async_copy(src, dst, small.at[i])
        for i, (src, dst) in enumerate((
            (cols_in, cols), (rows_in, rows), (step_in, dual_step), (mask_in.at[step], dual_mask), (cot_in, cot_y),
        ))
    ]
    for copy in minor:
        copy.start()

    def tile_copy(c):
        at = pl.ds(c * CHUNK, CHUNK)
        return pltpu.make_async_copy(tiles.at[at], held.at[at], sems.at[c])

    for c in range(chunks):
        tile_copy(c).start()
    for o in range(peers):
        filled[o] = 0
    for s in range(tile_of.shape[0]):
        tile_of[s] = 0
        row_of[s] = 0
        land_of[s] = hb.shape[0]
    for x in range(QUAD):
        for s in range(group * cap):
            wants[x, s] = col_blocks
    for copy in minor:
        copy.wait()
    me = lax.axis_index("rb").astype(I32)
    scale = (1 << 19) // col_blocks + 1

    def place_tile(t, _):
        col = cols[t]
        owner = (col * scale) >> 19
        rank = filled[owner]
        filled[owner] = rank + 1
        apart = owner ^ me
        high, quad = apart // QUAD, apart % QUAD
        place = high * cap + rank
        near = jnp.where(high < half, 1, 0)
        slot = (near * QUAD + quad) * (half * cap) + place - (1 - near) * (half * cap)
        tile_of[slot] = t
        row_of[slot] = rows[t]
        land_of[slot] = rows[t]
        wants[quad, place] = col - owner * col_blocks
        return 0

    lax.fori_loop(0, count[0], place_tile, 0)
    chart = pltpu.make_async_copy(wants, plan, small.at[len(minor)])
    chart.start()
    dy[...] = dual_mask[...].astype(F32) * cot_y[...]

    def h_into(at, h):
        rhs[:, at] = -h

    scaled_blocks(side, dy, dual_step, hb, h_into)
    chart.wait()
    for out in (o0, o1, o2, o3):
        out[half * cap, :, pl.ds(0, plan.shape[1])] = plan[...].astype(BF16)
    for c in range(chunks):
        tile_copy(c).wait()
    transpose_products(0, tile_of, row_of, held, hb, (o0, o1, o2, o3))


def turn_kernel(held, turned):
    def one_chunk(c, _):
        for j in range(CHUNK):
            turned[c * CHUNK + j] = held[c * CHUNK + j].T
        return 0

    lax.fori_loop(0, held.shape[0] // CHUNK, one_chunk, 0)


def across_product_kernel(tile_of, row_of, held, hb, o2):
    transpose_products(tile_of.shape[0] // 2, tile_of, row_of, held, hb, (o2,), (2,))


def map_kernel(a0, a1, a2, a3, wants, whole, sem):
    for x, part in enumerate((a0, a1, a2, a3)):
        plan = part[part.shape[0] - 1].astype(F32)
        whole[pl.ds(x, 1)] = plan[x:x + 1, :whole.shape[1]].astype(I32)
    whole[pl.ds(QUAD, QUAD)] = jnp.zeros((QUAD, whole.shape[1]), I32)
    copy = pltpu.make_async_copy(whole, wants, sem)
    copy.start()
    copy.wait()


def sum_kernel(first_high, cap, wants, a0, a1, a2, a3, *rest):
    parts = (a0, a1, a2, a3)
    half = len(rest) // 3
    outs, totals = rest[:half], rest[half:]
    for total in totals:
        total[...] = jnp.zeros_like(total)
    for r in range(cap):
        for pair in range(QUAD // 2):
            jobs = []
            for h in range(half):
                for side in range(2):
                    x = 2 * pair + side
                    spot = wants[x, (first_high + h) * cap + r]
                    jobs.append((totals[2 * h + side], spot, parts[x][h * cap + r].astype(F32)))
            values = [total[spot] + part for total, spot, part in jobs]
            for (total, spot, _), value in zip(jobs, values):
                total[spot] = value
    for h, out in enumerate(outs):
        for c in range(out.shape[0]):
            out[c] = (totals[2 * h][c] + totals[2 * h + 1][c]).astype(out.dtype)


def primal_kernel(step, primal_mask, primal_step, x, *refs):
    parts, (u_out, dx_out, out) = refs[:-3], refs[-3:]
    blocks, _, side = out.shape
    for c in range(blocks):
        at = pl.ds(c * side, side)
        u = parts[0][c]
        for part in parts[1:]:
            u = u + part[c].astype(F32)
        dx = primal_mask[step, :, at].astype(F32) * (x[:, at] + 2.0 * u)
        u_out[:, at] = u
        dx_out[:, at] = dx
        out[c] = (primal_step[:, at] * dx).astype(BF16)


def settle_kernel(first, primal_step, u, dx, spent, new_x, new_spent):
    new_x[...] = dx[...] - u[...]
    q = primal_step[...] * dx[...]
    new_spent[...] = -q if first else spent[...] - q


def settle_dual_kernel(dual_step, dy, rhs, new_rhs):
    new_rhs[...] = rhs[...] - dual_step[...] * dy[...]


def pick_kernel(highs, cap, wants, *refs):
    blocks, outs = dict(zip(highs, refs[:-QUAD])), refs[-QUAD:]
    last = refs[0].shape[0] - 1
    for x, out in enumerate(outs):
        values = [blocks[h][jnp.minimum(wants[x, h * cap + r], last)] for h in sorted(highs) for r in range(cap)]
        for s, value in enumerate(values):
            out[s] = value


def near_forward_kernel(tile_of, land_of, turned, m0, m1, m2, m3, out, *totals):
    forward_products(tile_of.shape[0] // 2, tile_of, land_of, turned, (m0, m1, m2, m3), totals)
    for r in range(out.shape[0]):
        out[r] = gathered(totals, r)


def chip_forward_kernel(tile_of, land_of, turned, part, m0, m1, out, *totals):
    forward_products(0, tile_of, land_of, turned, (m0, m1), totals, (0, 1))
    for r in range(out.shape[0]):
        out[r] = part[r] + gathered(totals, r)


def rest_product_kernel(base, tile_of, row_of, held, hb, o0, o1, o3):
    transpose_products(base, tile_of, row_of, held, hb, (o3, o1, o0), (3, 1, 0))


def middle_kernel(step, tile_of, row_of, land_of, held, turned, dual_step, dual_mask, part, dy, m2, m3,
                  new_dy, hb, o2, *totals):
    side = held.shape[1]
    forward_products(0, tile_of, land_of, turned, (m2, m3), totals, (2, 3))
    for r in range(hb.shape[0]):
        at = pl.ds(r * side, side)
        v = part[r] + gathered(totals, r)
        new_dy[:, at] = dual_mask[step, :, at].astype(F32) * (dy[:, at] - v)

    scaled_blocks(side, new_dy, dual_step, hb)
    transpose_products(0, tile_of, row_of, held, hb, (o2,), (2,))


def last_kernel(tile_of, land_of, turned, part, dy, m2, m3, new_y, *totals):
    side = turned.shape[1]
    forward_products(0, tile_of, land_of, turned, (m2, m3), totals, (2, 3))
    for r in range(part.shape[0]):
        at = pl.ds(r * side, side)
        new_y[:, at] = dy[:, at] - (part[r] + gathered(totals, r))


def on_device(tiles, tile_rows, tile_cols, tile_counts, dual_step, primal_step, primal_mask, dual_mask, cot_x, cot_y):
    peers = lax.axis_size("rb")
    tile_slots, side, _ = tiles.shape
    batch = cot_x.shape[0]
    row_blocks = dual_step.shape[0] // side
    col_blocks = primal_step.shape[0] // side
    cap = max(2, (tile_slots + peers - 1) // peers)
    group = peers // QUAD
    half = group // 2
    slots = peers * cap
    places = -(-group * cap // 128) * 128
    steps = primal_mask.shape[0]
    dual_step = dual_step.reshape(1, -1)
    primal_step = primal_step.reshape(1, -1)
    y_shape = shape(cot_y.shape, F32)
    x_shape = shape(cot_x.shape, F32)
    part_set = (shape((half * cap, batch, side), BF16),) * QUAD
    block_set = shape((col_blocks, batch, side), BF16)
    hb_set = shape((row_blocks, batch, side), BF16)
    per_slot = pltpu.SMEM((slots,), I32)
    row_totals = [pltpu.VMEM((row_blocks + 1, batch, side), F32)] * LANES
    col_totals = [pltpu.VMEM((col_blocks + 1, batch, side), F32)] * (2 * half)
    tile_bytes = tiles.size * 2

    def call(kernel, name, moved, ins, outs, args, scratch=()):
        return pl.pallas_call(
            kernel,
            out_shape=outs,
            in_specs=ins,
            out_specs=jax.tree.map(lambda _: VM, outs),
            scratch_shapes=scratch,
            compiler_params=PARAMS,
            cost_estimate=cost(moved),
            name=name,
        )(*args)

    def swap(array, x):
        return lax.ppermute(array, "rb", [(p, p ^ x) for p in range(peers)])

    def near_swaps(parts):
        return [parts[0]] + [swap(parts[x], x) for x in range(1, QUAD)]

    step = steps - 1
    held, dy, rhs, hb, tile_of, row_of, land_of, *far_parts = pl.pallas_call(
        functools.partial(start_kernel, step, peers, cap, col_blocks),
        out_shape=(
            pltpu.VMEM(tiles.shape, BF16), y_shape, y_shape, hb_set, per_slot, per_slot, per_slot,
        ) + (shape((half * cap + 1, batch, side), BF16),) * QUAD,
        in_specs=[SM] + [HBM] * 6,
        out_specs=(VM,) * 4 + (SM,) * 3 + (VM,) * QUAD,
        scratch_shapes=[
            pltpu.SMEM((tile_slots,), I32), pltpu.SMEM((tile_slots,), I32), pltpu.VMEM(dual_step.shape, F32),
            pltpu.VMEM(cot_y.shape, I32), pltpu.VMEM(cot_y.shape, F32), pltpu.SMEM((peers,), I32),
            pltpu.SMEM((2 * QUAD, places), I32), pltpu.VMEM((2 * QUAD, places), I32),
            pltpu.SemaphoreType.DMA((tile_slots // CHUNK,)), pltpu.SemaphoreType.DMA((6,)),
        ],
        compiler_params=PARAMS,
        cost_estimate=cost(2 * tile_bytes),
        name="start",
    )(tile_counts, *(
        pltpu.with_memory_space_constraint(array, pltpu.HBM)
        for array in (tile_rows, tile_cols, tiles, dual_step, dual_mask, cot_y)
    ))
    turned = call(turn_kernel, "turn", tile_bytes, [VM], pltpu.VMEM(tiles.shape, BF16), (held,))
    x_state, spent, wants = cot_x, cot_x, None
    near_highs, far_highs = tuple(range(half)), tuple(reversed(range(half, group)))
    while True:
        far_got = near_swaps(far_parts)
        across = call(across_product_kernel, "near_across", tile_bytes // 8, [SM] * 2 + [VM] * 2, part_set[0],
                      (tile_of, row_of, held, hb))
        later_hb, across = lax.optimization_barrier((hb, across))
        own, beside, aslant = call(functools.partial(rest_product_kernel, slots // 2), "near_rest", tile_bytes // 4,
                                   [SM] * 2 + [VM] * 2, part_set[:3], (tile_of, row_of, held, later_hb))
        near_parts = [own, beside, across, aslant]
        near_got = near_swaps(near_parts)
        if wants is None:
            wants = pl.pallas_call(
                map_kernel,
                out_shape=pltpu.SMEM((2 * QUAD, places), I32),
                in_specs=[VM] * QUAD,
                out_specs=SM,
                scratch_shapes=[pltpu.VMEM((2 * QUAD, places), I32), pltpu.SemaphoreType.DMA],
                compiler_params=PARAMS,
                name="maps",
            )(*far_got)
        far_sums = call(functools.partial(sum_kernel, half, cap), "far_sum", 1 << 20, [SM] + [VM] * QUAD,
                        (block_set,) * half, (wants, *far_got), col_totals)
        got = [swap(far_sums[h], (half + h) * QUAD) for h in range(half)]
        near_sums = call(functools.partial(sum_kernel, 0, cap), "near_sum", 1 << 20, [SM] + [VM] * QUAD,
                         (shape(block_set.shape, F32),) + (block_set,) * (half - 1), (wants, *near_got), col_totals)
        got += [swap(near_sums[h], h * QUAD) for h in range(1, half)]
        if step == steps - 1:
            turned, x_state = lax.optimization_barrier((turned, x_state))
        u, dx, moved = call(
            functools.partial(primal_kernel, step), "primal", 1 << 20, [VM] * (3 + group),
            (x_shape, x_shape, block_set), (primal_mask, primal_step, x_state, near_sums[0], *got))
        x_state, spent = call(functools.partial(settle_kernel, step == steps - 1), "settle", 1 << 20, [VM] * 4,
                              (x_shape, x_shape), (primal_step, u, dx, spent))
        blocks = [moved] + [swap(moved, h * QUAD) for h in range(1, group)]
        near_moved, far_moved = (
            near_swaps(call(functools.partial(pick_kernel, highs, cap), name, 1 << 20, [SM] + [VM] * half, part_set,
                            (wants, *(blocks[h] for h in highs))))
            for name, highs in (("near_pick", near_highs), ("far_pick", far_highs))
        )
        part = call(near_forward_kernel, "near_forward", tile_bytes // 2, [SM] * 2 + [VM] * (1 + QUAD),
                    shape(hb_set.shape, F32), (tile_of, land_of, turned, *near_moved), row_totals)
        part = call(chip_forward_kernel, "chip_forward", tile_bytes // 4, [SM] * 2 + [VM] * 4,
                    shape(hb_set.shape, F32), (tile_of, land_of, turned, part, *far_moved[:2]), row_totals)
        if step == 0:
            break
        step -= 1
        dy, hb, across = call(
            functools.partial(middle_kernel, step), "middle", tile_bytes // 2, [SM] * 3 + [VM] * 8,
            (y_shape, hb_set, part_set[0]),
            (tile_of, row_of, land_of, held, turned, dual_step, dual_mask, part, dy, *far_moved[2:]), row_totals)
        rhs = call(settle_dual_kernel, "settle_dual", 1 << 20, [VM] * 3, y_shape, (dual_step, dy, rhs))
        own, beside, aslant = call(functools.partial(rest_product_kernel, 0), "rest_product", tile_bytes // 4, [SM] * 2 + [VM] * 2,
                                   part_set[:3], (tile_of, row_of, held, hb))
        hb, own = lax.optimization_barrier((hb, own))
        far_parts = [own, beside, across, aslant]
    y_state = call(last_kernel, "last", tile_bytes // 4, [SM] * 2 + [VM] * 5, y_shape,
                   (tile_of, land_of, turned, part, dy, *far_moved[2:]), row_totals)
    return spent, rhs, x_state, y_state


def solution(mesh):
    rb = ("grp", "rb")
    return jax.shard_map(
        on_device,
        mesh=mesh,
        in_specs=(
            P(rb, None, None), P(rb), P(rb), P(rb), P(rb), P(rb),
            P(None, "grp", "rb"), P(None, "grp", "rb"), P("grp", "rb"), P("grp", "rb"),
        ),
        out_specs=(P("grp", "rb"),) * 4,
        check_vma=False,
    )
```

```python
import functools

import jax
import jax.numpy as jnp
from jax import lax
from jax.experimental import pallas as pl
from jax.experimental.pallas import tpu as pltpu
from jax.sharding import PartitionSpec as P

QUAD = 4
CHUNK = 8
LANES = 4
VM = pl.BlockSpec(memory_space=pltpu.VMEM)
SM = pl.BlockSpec(memory_space=pltpu.SMEM)
HBM = pl.BlockSpec(memory_space=pltpu.HBM)
PARAMS = pltpu.CompilerParams(vmem_limit_bytes=12 * 1024 * 1024)
F32, BF16, I32 = jnp.float32, jnp.bfloat16, jnp.int32


def shape(dims, dtype):
    return jax.ShapeDtypeStruct(dims, dtype)


def cost(moved):
    return pl.CostEstimate(flops=moved * 8, bytes_accessed=moved, transcendentals=0)


def scaled_blocks(side, dy, dual_step, hb, h_into=None):
    for r in range(hb.shape[0]):
        at = pl.ds(r * side, side)
        h = dual_step[:, at] * dy[:, at]
        hb[r] = h.astype(BF16)
        if h_into is not None:
            h_into(at, h)


def transpose_products(base, tile_of, row_of, tiles, hb, outs, xs=range(QUAD)):
    per = tile_of.shape[0] // (2 * QUAD)
    for x, out in zip(xs, outs):
        for s in range(per):
            slot = base + x * per + s
            out[s] = jnp.dot(hb[row_of[slot]], tiles[tile_of[slot]], preferred_element_type=F32).astype(BF16)


def forward_products(base, tile_of, land_of, turned, moved, totals, xs=range(QUAD)):
    per = tile_of.shape[0] // (2 * QUAD)
    for total in totals:
        total[...] = jnp.zeros_like(total)
    for x, part in zip(xs, moved):
        first = base + x * per
        terms = [jnp.dot(part[s], turned[tile_of[first + s]], preferred_element_type=F32) for s in range(per)]
        for s in range(0, per, LANES):
            several = range(min(LANES, per - s))
            spots = [land_of[first + s + i] for i in several]
            held = [totals[i][spots[i]] + terms[s + i] for i in several]
            for i in several:
                totals[i][spots[i]] = held[i]


def gathered(totals, r):
    value = totals[0][r]
    for total in totals[1:]:
        value = value + total[r]
    return value


def start_kernel(step, peers, cap, col_blocks, count, rows_in, cols_in, tiles, step_in, mask_in, cot_in,
                 held, dy, rhs, hb, tile_of, row_of, land_of, o0, o1, o2, o3,
                 rows, cols, dual_step, dual_mask, cot_y, filled, wants, plan, sems, small):
    tile_slots, side, _ = tiles.shape
    group = peers // QUAD
    half = group // 2
    chunks = tile_slots // CHUNK
    minor = [
        pltpu.make_async_copy(src, dst, small.at[i])
        for i, (src, dst) in enumerate((
            (cols_in, cols), (rows_in, rows), (step_in, dual_step), (mask_in.at[step], dual_mask), (cot_in, cot_y),
        ))
    ]
    for copy in minor:
        copy.start()

    def tile_copy(c):
        at = pl.ds(c * CHUNK, CHUNK)
        return pltpu.make_async_copy(tiles.at[at], held.at[at], sems.at[c])

    for c in range(chunks):
        tile_copy(c).start()
    for o in range(peers):
        filled[o] = 0
    for s in range(tile_of.shape[0]):
        tile_of[s] = 0
        row_of[s] = 0
        land_of[s] = hb.shape[0]
    for x in range(QUAD):
        for s in range(group * cap):
            wants[x, s] = col_blocks
    for copy in minor:
        copy.wait()
    me = lax.axis_index("rb").astype(I32)
    scale = (1 << 19) // col_blocks + 1

    def place_tile(t, _):
        col = cols[t]
        owner = (col * scale) >> 19
        rank = filled[owner]
        filled[owner] = rank + 1
        apart = owner ^ me
        high, quad = apart // QUAD, apart % QUAD
        place = high * cap + rank
        near = jnp.where(high < half, 1, 0)
        slot = (near * QUAD + quad) * (half * cap) + place - (1 - near) * (half * cap)
        tile_of[slot] = t
        row_of[slot] = rows[t]
        land_of[slot] = rows[t]
        wants[quad, place] = col - owner * col_blocks
        return 0

    lax.fori_loop(0, count[0], place_tile, 0)
    chart = pltpu.make_async_copy(wants, plan, small.at[len(minor)])
    chart.start()
    dy[...] = dual_mask[...].astype(F32) * cot_y[...]

    def h_into(at, h):
        rhs[:, at] = -h

    scaled_blocks(side, dy, dual_step, hb, h_into)
    chart.wait()
    for out in (o0, o1, o2, o3):
        out[half * cap, :, pl.ds(0, plan.shape[1])] = plan[...].astype(BF16)
    for c in range(chunks):
        tile_copy(c).wait()
    transpose_products(0, tile_of, row_of, held, hb, (o0, o1, o2, o3))


def turn_kernel(held, turned):
    def one_chunk(c, _):
        for j in range(CHUNK):
            turned[c * CHUNK + j] = held[c * CHUNK + j].T
        return 0

    lax.fori_loop(0, held.shape[0] // CHUNK, one_chunk, 0)


def near_product_kernel(tile_of, row_of, held, hb, o0, o1, o2, o3):
    transpose_products(tile_of.shape[0] // 2, tile_of, row_of, held, hb, (o0, o1, o2, o3))


def map_kernel(a0, a1, a2, a3, wants, whole, sem):
    for x, part in enumerate((a0, a1, a2, a3)):
        plan = part[part.shape[0] - 1].astype(F32)
        whole[pl.ds(x, 1)] = plan[x:x + 1, :whole.shape[1]].astype(I32)
    whole[pl.ds(QUAD, QUAD)] = jnp.zeros((QUAD, whole.shape[1]), I32)
    copy = pltpu.make_async_copy(whole, wants, sem)
    copy.start()
    copy.wait()


def sum_kernel(first_high, cap, wants, a0, a1, a2, a3, *rest):
    parts = (a0, a1, a2, a3)
    half = len(rest) // 3
    outs, totals = rest[:half], rest[half:]
    for total in totals:
        total[...] = jnp.zeros_like(total)
    for r in range(cap):
        for pair in range(QUAD // 2):
            jobs = []
            for h in range(half):
                for side in range(2):
                    x = 2 * pair + side
                    spot = wants[x, (first_high + h) * cap + r]
                    jobs.append((totals[2 * h + side], spot, parts[x][h * cap + r].astype(F32)))
            values = [total[spot] + part for total, spot, part in jobs]
            for (total, spot, _), value in zip(jobs, values):
                total[spot] = value
    for h, out in enumerate(outs):
        for c in range(out.shape[0]):
            out[c] = (totals[2 * h][c] + totals[2 * h + 1][c]).astype(out.dtype)


def primal_kernel(step, primal_mask, primal_step, x, *refs):
    parts, (u_out, dx_out, out) = refs[:-3], refs[-3:]
    blocks, _, side = out.shape
    for c in range(blocks):
        at = pl.ds(c * side, side)
        u = parts[0][c]
        for part in parts[1:]:
            u = u + part[c].astype(F32)
        dx = primal_mask[step, :, at].astype(F32) * (x[:, at] + 2.0 * u)
        u_out[:, at] = u
        dx_out[:, at] = dx
        out[c] = (primal_step[:, at] * dx).astype(BF16)


def settle_kernel(first, primal_step, u, dx, spent, new_x, new_spent):
    new_x[...] = dx[...] - u[...]
    q = primal_step[...] * dx[...]
    new_spent[...] = -q if first else spent[...] - q


def settle_dual_kernel(dual_step, dy, rhs, new_rhs):
    new_rhs[...] = rhs[...] - dual_step[...] * dy[...]


def pick_kernel(highs, cap, wants, *refs):
    blocks, outs = dict(zip(highs, refs[:-QUAD])), refs[-QUAD:]
    last = refs[0].shape[0] - 1
    for x, out in enumerate(outs):
        values = [blocks[h][jnp.minimum(wants[x, h * cap + r], last)] for h in sorted(highs) for r in range(cap)]
        for s, value in enumerate(values):
            out[s] = value


def near_forward_kernel(tile_of, land_of, turned, m0, m1, m2, m3, out, *totals):
    forward_products(tile_of.shape[0] // 2, tile_of, land_of, turned, (m0, m1, m2, m3), totals)
    for r in range(out.shape[0]):
        out[r] = gathered(totals, r)


def far_forward_kernel(xs, tile_of, land_of, turned, part, *refs):
    moved, out, totals = refs[:len(xs)], refs[len(xs)], refs[len(xs) + 1:]
    forward_products(0, tile_of, land_of, turned, moved, totals, xs)
    for r in range(out.shape[0]):
        out[r] = part[r] + gathered(totals, r)


def rest_product_kernel(tile_of, row_of, held, hb, o0, o1, o3):
    transpose_products(0, tile_of, row_of, held, hb, (o3, o1, o0), (3, 1, 0))


def middle_kernel(step, tile_of, row_of, land_of, held, turned, dual_step, dual_mask, part, dy, m3,
                  new_dy, hb, o2, *totals):
    side = held.shape[1]
    forward_products(0, tile_of, land_of, turned, (m3,), totals, (3,))
    for r in range(hb.shape[0]):
        at = pl.ds(r * side, side)
        v = part[r] + gathered(totals, r)
        new_dy[:, at] = dual_mask[step, :, at].astype(F32) * (dy[:, at] - v)

    scaled_blocks(side, new_dy, dual_step, hb)
    transpose_products(0, tile_of, row_of, held, hb, (o2,), (2,))


def last_kernel(tile_of, land_of, turned, part, dy, m3, new_y, *totals):
    side = turned.shape[1]
    forward_products(0, tile_of, land_of, turned, (m3,), totals, (3,))
    for r in range(part.shape[0]):
        at = pl.ds(r * side, side)
        new_y[:, at] = dy[:, at] - (part[r] + gathered(totals, r))


def on_device(tiles, tile_rows, tile_cols, tile_counts, dual_step, primal_step, primal_mask, dual_mask, cot_x, cot_y):
    peers = lax.axis_size("rb")
    tile_slots, side, _ = tiles.shape
    batch = cot_x.shape[0]
    row_blocks = dual_step.shape[0] // side
    col_blocks = primal_step.shape[0] // side
    cap = max(2, (tile_slots + peers - 1) // peers)
    group = peers // QUAD
    half = group // 2
    slots = peers * cap
    places = -(-group * cap // 128) * 128
    steps = primal_mask.shape[0]
    dual_step = dual_step.reshape(1, -1)
    primal_step = primal_step.reshape(1, -1)
    y_shape = shape(cot_y.shape, F32)
    x_shape = shape(cot_x.shape, F32)
    part_set = (shape((half * cap, batch, side), BF16),) * QUAD
    block_set = shape((col_blocks, batch, side), BF16)
    hb_set = shape((row_blocks, batch, side), BF16)
    per_slot = pltpu.SMEM((slots,), I32)
    row_totals = [pltpu.VMEM((row_blocks + 1, batch, side), F32)] * LANES
    col_totals = [pltpu.VMEM((col_blocks + 1, batch, side), F32)] * (2 * half)
    tile_bytes = tiles.size * 2

    def call(kernel, name, moved, ins, outs, args, scratch=()):
        return pl.pallas_call(
            kernel,
            out_shape=outs,
            in_specs=ins,
            out_specs=jax.tree.map(lambda _: VM, outs),
            scratch_shapes=scratch,
            compiler_params=PARAMS,
            cost_estimate=cost(moved),
            name=name,
        )(*args)

    def swap(array, x):
        return lax.ppermute(array, "rb", [(p, p ^ x) for p in range(peers)])

    def near_swaps(parts):
        return [parts[0]] + [swap(parts[x], x) for x in range(1, QUAD)]

    step = steps - 1
    held, dy, rhs, hb, tile_of, row_of, land_of, *far_parts = pl.pallas_call(
        functools.partial(start_kernel, step, peers, cap, col_blocks),
        out_shape=(
            pltpu.VMEM(tiles.shape, BF16), y_shape, y_shape, hb_set, per_slot, per_slot, per_slot,
        ) + (shape((half * cap + 1, batch, side), BF16),) * QUAD,
        in_specs=[SM] + [HBM] * 6,
        out_specs=(VM,) * 4 + (SM,) * 3 + (VM,) * QUAD,
        scratch_shapes=[
            pltpu.SMEM((tile_slots,), I32), pltpu.SMEM((tile_slots,), I32), pltpu.VMEM(dual_step.shape, F32),
            pltpu.VMEM(cot_y.shape, I32), pltpu.VMEM(cot_y.shape, F32), pltpu.SMEM((peers,), I32),
            pltpu.SMEM((2 * QUAD, places), I32), pltpu.VMEM((2 * QUAD, places), I32),
            pltpu.SemaphoreType.DMA((tile_slots // CHUNK,)), pltpu.SemaphoreType.DMA((6,)),
        ],
        compiler_params=PARAMS,
        cost_estimate=cost(2 * tile_bytes),
        name="start",
    )(tile_counts, *(
        pltpu.with_memory_space_constraint(array, pltpu.HBM)
        for array in (tile_rows, tile_cols, tiles, dual_step, dual_mask, cot_y)
    ))
    turned = call(turn_kernel, "turn", tile_bytes, [VM], pltpu.VMEM(tiles.shape, BF16), (held,))
    x_state, spent, wants = cot_x, cot_x, None
    near_highs, far_highs = tuple(range(half)), tuple(reversed(range(half, group)))
    while True:
        far_got = near_swaps(far_parts)
        near_parts = call(near_product_kernel, "near_product", tile_bytes // 2, [SM] * 2 + [VM] * 2, part_set,
                          (tile_of, row_of, held, hb))
        near_got = near_swaps(near_parts)
        if wants is None:
            wants = pl.pallas_call(
                map_kernel,
                out_shape=pltpu.SMEM((2 * QUAD, places), I32),
                in_specs=[VM] * QUAD,
                out_specs=SM,
                scratch_shapes=[pltpu.VMEM((2 * QUAD, places), I32), pltpu.SemaphoreType.DMA],
                compiler_params=PARAMS,
                name="maps",
            )(*far_got)
        far_sums = call(functools.partial(sum_kernel, half, cap), "far_sum", 1 << 20, [SM] + [VM] * QUAD,
                        (block_set,) * half, (wants, *far_got), col_totals)
        got = [swap(far_sums[h], (half + h) * QUAD) for h in range(half)]
        near_sums = call(functools.partial(sum_kernel, 0, cap), "near_sum", 1 << 20, [SM] + [VM] * QUAD,
                         (shape(block_set.shape, F32),) + (block_set,) * (half - 1), (wants, *near_got), col_totals)
        got += [swap(near_sums[h], h * QUAD) for h in range(1, half)]
        if step == steps - 1:
            turned, x_state = lax.optimization_barrier((turned, x_state))
        u, dx, moved = call(
            functools.partial(primal_kernel, step), "primal", 1 << 20, [VM] * (3 + group),
            (x_shape, x_shape, block_set), (primal_mask, primal_step, x_state, near_sums[0], *got))
        x_state, spent = call(functools.partial(settle_kernel, step == steps - 1), "settle", 1 << 20, [VM] * 4,
                              (x_shape, x_shape), (primal_step, u, dx, spent))
        blocks = [moved] + [swap(moved, h * QUAD) for h in range(1, group)]
        near_moved, far_moved = (
            near_swaps(call(functools.partial(pick_kernel, highs, cap), name, 1 << 20, [SM] + [VM] * half, part_set,
                            (wants, *(blocks[h] for h in highs))))
            for name, highs in (("near_pick", near_highs), ("far_pick", far_highs))
        )
        part = call(near_forward_kernel, "near_forward", tile_bytes // 2, [SM] * 2 + [VM] * (1 + QUAD),
                    shape(hb_set.shape, F32), (tile_of, land_of, turned, *near_moved), row_totals)
        for name, xs in (("chip_forward", (0, 1)), ("across_forward", (2,))):
            part = call(functools.partial(far_forward_kernel, xs), name, tile_bytes // 8 * len(xs),
                        [SM] * 2 + [VM] * (2 + len(xs)), shape(hb_set.shape, F32),
                        (tile_of, land_of, turned, part, *(far_moved[x] for x in xs)), row_totals)
        if step == 0:
            break
        step -= 1
        dy, hb, across = call(
            functools.partial(middle_kernel, step), "middle", tile_bytes // 4, [SM] * 3 + [VM] * 7,
            (y_shape, hb_set, part_set[0]),
            (tile_of, row_of, land_of, held, turned, dual_step, dual_mask, part, dy, far_moved[3]), row_totals)
        rhs = call(settle_dual_kernel, "settle_dual", 1 << 20, [VM] * 3, y_shape, (dual_step, dy, rhs))
        own, beside, aslant = call(rest_product_kernel, "rest_product", tile_bytes // 4, [SM] * 2 + [VM] * 2,
                                   part_set[:3], (tile_of, row_of, held, hb))
        far_parts = [own, beside, across, aslant]
    y_state = call(last_kernel, "last", tile_bytes // 8, [SM] * 2 + [VM] * 4, y_shape,
                   (tile_of, land_of, turned, part, dy, far_moved[3]), row_totals)
    return spent, rhs, x_state, y_state


def solution(mesh):
    rb = ("grp", "rb")
    return jax.shard_map(
        on_device,
        mesh=mesh,
        in_specs=(
            P(rb, None, None), P(rb), P(rb), P(rb), P(rb), P(rb),
            P(None, "grp", "rb"), P(None, "grp", "rb"), P("grp", "rb"), P("grp", "rb"),
        ),
        out_specs=(P("grp", "rb"),) * 4,
        check_vma=False,
    )
```

```python
import functools

import jax
import jax.numpy as jnp
from jax import lax
from jax.experimental import pallas as pl
from jax.experimental.pallas import tpu as pltpu
from jax.sharding import PartitionSpec as P

QUAD = 4
CHUNK = 8
LANES = 4
VM = pl.BlockSpec(memory_space=pltpu.VMEM)
SM = pl.BlockSpec(memory_space=pltpu.SMEM)
HBM = pl.BlockSpec(memory_space=pltpu.HBM)
PARAMS = pltpu.CompilerParams(vmem_limit_bytes=12 * 1024 * 1024)
F32, BF16, I32 = jnp.float32, jnp.bfloat16, jnp.int32


def shape(dims, dtype):
    return jax.ShapeDtypeStruct(dims, dtype)


def cost(moved):
    return pl.CostEstimate(flops=moved * 8, bytes_accessed=moved, transcendentals=0)


def scaled_blocks(side, dy, dual_step, hb, h_into=None):
    for r in range(hb.shape[0]):
        at = pl.ds(r * side, side)
        h = dual_step[:, at] * dy[:, at]
        hb[r] = h.astype(BF16)
        if h_into is not None:
            h_into(at, h)


def transpose_products(base, tile_of, row_of, tiles, hb, outs, xs=range(QUAD)):
    per = tile_of.shape[0] // (2 * QUAD)
    for x, out in zip(xs, outs):
        for s in range(per):
            slot = base + x * per + s
            out[s] = jnp.dot(hb[row_of[slot]], tiles[tile_of[slot]], preferred_element_type=F32).astype(BF16)


def forward_products(base, tile_of, land_of, turned, moved, totals, xs=range(QUAD)):
    per = tile_of.shape[0] // (2 * QUAD)
    for total in totals:
        total[...] = jnp.zeros_like(total)
    for x, part in zip(xs, moved):
        first = base + x * per
        terms = [jnp.dot(part[s], turned[tile_of[first + s]], preferred_element_type=F32) for s in range(per)]
        for s in range(0, per, LANES):
            several = range(min(LANES, per - s))
            spots = [land_of[first + s + i] for i in several]
            held = [totals[i][spots[i]] + terms[s + i] for i in several]
            for i in several:
                totals[i][spots[i]] = held[i]


def gathered(totals, r):
    value = totals[0][r]
    for total in totals[1:]:
        value = value + total[r]
    return value


def start_kernel(step, peers, cap, col_blocks, count, rows_in, cols_in, tiles, step_in, mask_in, cot_in,
                 held, dy, rhs, hb, tile_of, row_of, land_of, o0, o1, o2, o3,
                 rows, cols, dual_step, dual_mask, cot_y, filled, wants, plan, sems, small):
    tile_slots, side, _ = tiles.shape
    group = peers // QUAD
    half = group // 2
    chunks = tile_slots // CHUNK
    minor = [
        pltpu.make_async_copy(src, dst, small.at[i])
        for i, (src, dst) in enumerate((
            (cols_in, cols), (rows_in, rows), (step_in, dual_step), (mask_in.at[step], dual_mask), (cot_in, cot_y),
        ))
    ]
    for copy in minor:
        copy.start()

    def tile_copy(c):
        at = pl.ds(c * CHUNK, CHUNK)
        return pltpu.make_async_copy(tiles.at[at], held.at[at], sems.at[c])

    for c in range(chunks):
        tile_copy(c).start()
    for o in range(peers):
        filled[o] = 0
    for s in range(tile_of.shape[0]):
        tile_of[s] = 0
        row_of[s] = 0
        land_of[s] = hb.shape[0]
    for x in range(QUAD):
        for s in range(group * cap):
            wants[x, s] = col_blocks
    for copy in minor:
        copy.wait()
    me = lax.axis_index("rb").astype(I32)
    scale = (1 << 19) // col_blocks + 1

    def place_tile(t, _):
        col = cols[t]
        owner = (col * scale) >> 19
        rank = filled[owner]
        filled[owner] = rank + 1
        apart = owner ^ me
        high, quad = apart // QUAD, apart % QUAD
        place = high * cap + rank
        near = jnp.where(high < half, 1, 0)
        slot = (near * QUAD + quad) * (half * cap) + place - (1 - near) * (half * cap)
        tile_of[slot] = t
        row_of[slot] = rows[t]
        land_of[slot] = rows[t]
        wants[quad, place] = col - owner * col_blocks
        return 0

    lax.fori_loop(0, count[0], place_tile, 0)
    chart = pltpu.make_async_copy(wants, plan, small.at[len(minor)])
    chart.start()
    dy[...] = dual_mask[...].astype(F32) * cot_y[...]

    def h_into(at, h):
        rhs[:, at] = -h

    scaled_blocks(side, dy, dual_step, hb, h_into)
    chart.wait()
    for out in (o0, o1, o2, o3):
        out[half * cap, :, pl.ds(0, plan.shape[1])] = plan[...].astype(BF16)
    for c in range(chunks):
        tile_copy(c).wait()
    transpose_products(0, tile_of, row_of, held, hb, (o0, o1, o2, o3))


def turn_kernel(held, turned):
    def one_chunk(c, _):
        for j in range(CHUNK):
            turned[c * CHUNK + j] = held[c * CHUNK + j].T
        return 0

    lax.fori_loop(0, held.shape[0] // CHUNK, one_chunk, 0)


def near_product_kernel(tile_of, row_of, held, hb, o0, o1, o2, o3):
    transpose_products(tile_of.shape[0] // 2, tile_of, row_of, held, hb, (o0, o1, o2, o3))


def map_kernel(a0, a1, a2, a3, wants, whole, sem):
    for x, part in enumerate((a0, a1, a2, a3)):
        plan = part[part.shape[0] - 1].astype(F32)
        whole[pl.ds(x, 1)] = plan[x:x + 1, :whole.shape[1]].astype(I32)
    whole[pl.ds(QUAD, QUAD)] = jnp.zeros((QUAD, whole.shape[1]), I32)
    copy = pltpu.make_async_copy(whole, wants, sem)
    copy.start()
    copy.wait()


def sum_kernel(first_high, cap, wants, a0, a1, a2, a3, *rest):
    parts = (a0, a1, a2, a3)
    half = len(rest) // 3
    outs, totals = rest[:half], rest[half:]
    for total in totals:
        total[...] = jnp.zeros_like(total)
    for r in range(cap):
        for pair in range(QUAD // 2):
            jobs = []
            for h in range(half):
                for side in range(2):
                    x = 2 * pair + side
                    spot = wants[x, (first_high + h) * cap + r]
                    jobs.append((totals[2 * h + side], spot, parts[x][h * cap + r].astype(F32)))
            values = [total[spot] + part for total, spot, part in jobs]
            for (total, spot, _), value in zip(jobs, values):
                total[spot] = value
    for h, out in enumerate(outs):
        for c in range(out.shape[0]):
            out[c] = (totals[2 * h][c] + totals[2 * h + 1][c]).astype(out.dtype)


def primal_kernel(step, primal_mask, primal_step, x, *refs):
    parts, (u_out, dx_out, out) = refs[:-3], refs[-3:]
    blocks, _, side = out.shape
    for c in range(blocks):
        at = pl.ds(c * side, side)
        u = parts[0][c]
        for part in parts[1:]:
            u = u + part[c].astype(F32)
        dx = primal_mask[step, :, at].astype(F32) * (x[:, at] + 2.0 * u)
        u_out[:, at] = u
        dx_out[:, at] = dx
        out[c] = (primal_step[:, at] * dx).astype(BF16)


def settle_kernel(first, primal_step, u, dx, spent, new_x, new_spent):
    new_x[...] = dx[...] - u[...]
    q = primal_step[...] * dx[...]
    new_spent[...] = -q if first else spent[...] - q


def settle_dual_kernel(dual_step, dy, rhs, new_rhs):
    new_rhs[...] = rhs[...] - dual_step[...] * dy[...]


def pick_kernel(highs, cap, wants, *refs):
    blocks, outs = dict(zip(highs, refs[:-QUAD])), refs[-QUAD:]
    last = refs[0].shape[0] - 1
    for x, out in enumerate(outs):
        values = [blocks[h][jnp.minimum(wants[x, h * cap + r], last)] for h in sorted(highs) for r in range(cap)]
        for s, value in enumerate(values):
            out[s] = value


def near_forward_kernel(tile_of, land_of, turned, m0, m1, m2, m3, out, *totals):
    forward_products(tile_of.shape[0] // 2, tile_of, land_of, turned, (m0, m1, m2, m3), totals)
    for r in range(out.shape[0]):
        out[r] = gathered(totals, r)


def far_forward_kernel(xs, tile_of, land_of, turned, part, *refs):
    moved, out, totals = refs[:len(xs)], refs[len(xs)], refs[len(xs) + 1:]
    forward_products(0, tile_of, land_of, turned, moved, totals, xs)
    for r in range(out.shape[0]):
        out[r] = part[r] + gathered(totals, r)


def rest_product_kernel(tile_of, row_of, held, hb, o0, o1, o3):
    transpose_products(0, tile_of, row_of, held, hb, (o3, o1, o0), (3, 1, 0))


def middle_kernel(step, tile_of, row_of, land_of, held, turned, dual_step, dual_mask, part, dy, m3,
                  new_dy, hb, o2, *totals):
    side = held.shape[1]
    forward_products(0, tile_of, land_of, turned, (m3,), totals, (3,))
    for r in range(hb.shape[0]):
        at = pl.ds(r * side, side)
        v = part[r] + gathered(totals, r)
        new_dy[:, at] = dual_mask[step, :, at].astype(F32) * (dy[:, at] - v)

    scaled_blocks(side, new_dy, dual_step, hb)
    transpose_products(0, tile_of, row_of, held, hb, (o2,), (2,))


def last_kernel(tile_of, land_of, turned, part, dy, m3, new_y, *totals):
    side = turned.shape[1]
    forward_products(0, tile_of, land_of, turned, (m3,), totals, (3,))
    for r in range(part.shape[0]):
        at = pl.ds(r * side, side)
        new_y[:, at] = dy[:, at] - (part[r] + gathered(totals, r))


def on_device(tiles, tile_rows, tile_cols, tile_counts, dual_step, primal_step, primal_mask, dual_mask, cot_x, cot_y):
    peers = lax.axis_size("rb")
    tile_slots, side, _ = tiles.shape
    batch = cot_x.shape[0]
    row_blocks = dual_step.shape[0] // side
    col_blocks = primal_step.shape[0] // side
    cap = max(2, (tile_slots + peers - 1) // peers)
    group = peers // QUAD
    half = group // 2
    slots = peers * cap
    places = -(-group * cap // 128) * 128
    steps = primal_mask.shape[0]
    dual_step = dual_step.reshape(1, -1)
    primal_step = primal_step.reshape(1, -1)
    y_shape = shape(cot_y.shape, F32)
    x_shape = shape(cot_x.shape, F32)
    part_set = (shape((half * cap, batch, side), BF16),) * QUAD
    block_set = shape((col_blocks, batch, side), BF16)
    hb_set = shape((row_blocks, batch, side), BF16)
    per_slot = pltpu.SMEM((slots,), I32)
    row_totals = [pltpu.VMEM((row_blocks + 1, batch, side), F32)] * LANES
    col_totals = [pltpu.VMEM((col_blocks + 1, batch, side), F32)] * (2 * half)
    tile_bytes = tiles.size * 2

    def call(kernel, name, moved, ins, outs, args, scratch=()):
        return pl.pallas_call(
            kernel,
            out_shape=outs,
            in_specs=ins,
            out_specs=jax.tree.map(lambda _: VM, outs),
            scratch_shapes=scratch,
            compiler_params=PARAMS,
            cost_estimate=cost(moved),
            name=name,
        )(*args)

    def swap(array, x):
        return lax.ppermute(array, "rb", [(p, p ^ x) for p in range(peers)])

    def near_swaps(parts):
        return [parts[0]] + [swap(parts[x], x) for x in range(1, QUAD)]

    step = steps - 1
    held, dy, rhs, hb, tile_of, row_of, land_of, *far_parts = pl.pallas_call(
        functools.partial(start_kernel, step, peers, cap, col_blocks),
        out_shape=(
            pltpu.VMEM(tiles.shape, BF16), y_shape, y_shape, hb_set, per_slot, per_slot, per_slot,
        ) + (shape((half * cap + 1, batch, side), BF16),) * QUAD,
        in_specs=[SM] + [HBM] * 6,
        out_specs=(VM,) * 4 + (SM,) * 3 + (VM,) * QUAD,
        scratch_shapes=[
            pltpu.SMEM((tile_slots,), I32), pltpu.SMEM((tile_slots,), I32), pltpu.VMEM(dual_step.shape, F32),
            pltpu.VMEM(cot_y.shape, I32), pltpu.VMEM(cot_y.shape, F32), pltpu.SMEM((peers,), I32),
            pltpu.SMEM((2 * QUAD, places), I32), pltpu.VMEM((2 * QUAD, places), I32),
            pltpu.SemaphoreType.DMA((tile_slots // CHUNK,)), pltpu.SemaphoreType.DMA((6,)),
        ],
        compiler_params=PARAMS,
        cost_estimate=cost(2 * tile_bytes),
        name="start",
    )(tile_counts, *(
        pltpu.with_memory_space_constraint(array, pltpu.HBM)
        for array in (tile_rows, tile_cols, tiles, dual_step, dual_mask, cot_y)
    ))
    turned = call(turn_kernel, "turn", tile_bytes, [VM], pltpu.VMEM(tiles.shape, BF16), (held,))
    x_state, spent, wants = cot_x, cot_x, None
    near_highs, far_highs = tuple(range(half)), tuple(reversed(range(half, group)))
    while True:
        far_got = near_swaps(far_parts)
        near_parts = call(near_product_kernel, "near_product", tile_bytes // 2, [SM] * 2 + [VM] * 2, part_set,
                          (tile_of, row_of, held, hb))
        near_got = near_swaps(near_parts)
        if wants is None:
            wants = pl.pallas_call(
                map_kernel,
                out_shape=pltpu.SMEM((2 * QUAD, places), I32),
                in_specs=[VM] * QUAD,
                out_specs=SM,
                scratch_shapes=[pltpu.VMEM((2 * QUAD, places), I32), pltpu.SemaphoreType.DMA],
                compiler_params=PARAMS,
                name="maps",
            )(*far_got)
        far_sums = call(functools.partial(sum_kernel, half, cap), "far_sum", 1 << 20, [SM] + [VM] * QUAD,
                        (block_set,) * half, (wants, *far_got), col_totals)
        got = [swap(far_sums[h], (half + h) * QUAD) for h in range(half)]
        near_sums = call(functools.partial(sum_kernel, 0, cap), "near_sum", 1 << 20, [SM] + [VM] * QUAD,
                         (shape(block_set.shape, F32),) + (block_set,) * (half - 1), (wants, *near_got), col_totals)
        got += [swap(near_sums[h], h * QUAD) for h in range(1, half)]
        if step == steps - 1:
            turned, x_state = lax.optimization_barrier((turned, x_state))
        if step == 0:
            rhs, x_state = lax.optimization_barrier((rhs, x_state))
        u, dx, moved = call(
            functools.partial(primal_kernel, step), "primal", 1 << 20, [VM] * (3 + group),
            (x_shape, x_shape, block_set), (primal_mask, primal_step, x_state, near_sums[0], *got))
        x_state, spent = call(functools.partial(settle_kernel, step == steps - 1), "settle", 1 << 20, [VM] * 4,
                              (x_shape, x_shape), (primal_step, u, dx, spent))
        blocks = [moved] + [swap(moved, h * QUAD) for h in range(1, group)]
        near_moved, far_moved = (
            near_swaps(call(functools.partial(pick_kernel, highs, cap), name, 1 << 20, [SM] + [VM] * half, part_set,
                            (wants, *(blocks[h] for h in highs))))
            for name, highs in (("near_pick", near_highs), ("far_pick", far_highs))
        )
        part = call(near_forward_kernel, "near_forward", tile_bytes // 2, [SM] * 2 + [VM] * (1 + QUAD),
                    shape(hb_set.shape, F32), (tile_of, land_of, turned, *near_moved), row_totals)
        for name, xs in (("chip_forward", (0, 1)), ("across_forward", (2,))):
            part = call(functools.partial(far_forward_kernel, xs), name, tile_bytes // 8 * len(xs),
                        [SM] * 2 + [VM] * (2 + len(xs)), shape(hb_set.shape, F32),
                        (tile_of, land_of, turned, part, *(far_moved[x] for x in xs)), row_totals)
        if step == 0:
            break
        step -= 1
        dy, hb, across = call(
            functools.partial(middle_kernel, step), "middle", tile_bytes // 4, [SM] * 3 + [VM] * 7,
            (y_shape, hb_set, part_set[0]),
            (tile_of, row_of, land_of, held, turned, dual_step, dual_mask, part, dy, far_moved[3]), row_totals)
        rhs = call(settle_dual_kernel, "settle_dual", 1 << 20, [VM] * 3, y_shape, (dual_step, dy, rhs))
        own, beside, aslant = call(rest_product_kernel, "rest_product", tile_bytes // 4, [SM] * 2 + [VM] * 2,
                                   part_set[:3], (tile_of, row_of, held, hb))
        far_parts = [own, beside, across, aslant]
    y_state = call(last_kernel, "last", tile_bytes // 8, [SM] * 2 + [VM] * 4, y_shape,
                   (tile_of, land_of, turned, part, dy, far_moved[3]), row_totals)
    return spent, rhs, x_state, y_state


def solution(mesh):
    rb = ("grp", "rb")
    return jax.shard_map(
        on_device,
        mesh=mesh,
        in_specs=(
            P(rb, None, None), P(rb), P(rb), P(rb), P(rb), P(rb),
            P(None, "grp", "rb"), P(None, "grp", "rb"), P("grp", "rb"), P("grp", "rb"),
        ),
        out_specs=(P("grp", "rb"),) * 4,
        check_vma=False,
    )
```
